32 devices in a mesh: seq: 4 (over x, core), tp: 8 (over z, y).
Axes of the slice: x: 2, y: 2, z: 4, core: 2. Of those that a mesh axis runs over, the one named last changes fastest.
Arguments:
- tokens: bfloat16 [3, 4096, 2048], P(None, 'seq', 'tp'), may hold values from -6 to 6
- cotangent: bfloat16 [3, 4096, 2048], P(None, 'seq', 'tp'), may hold values from -6 to 6
- lengths: int32 [3], replicated, may hold values from 1024 to 4096, as said below
- in_gain: float32 [2048], replicated, may hold values from 0.1 to 1.9
- w_input: bfloat16 [2048, 2048], P(None, 'tp'), may hold values from -0.125 to 0.125
- w_forget: bfloat16 [2048, 2048], P(None, 'tp'), may hold values from -0.125 to 0.125
- w_output_gate: bfloat16 [2048, 2048], P(None, 'tp'), may hold values from -0.125 to 0.125
- lower_bound: float32 [2048], P('tp'), may hold values from 0 to 1
- mix_gain: float32 [2048], P('tp'), may hold values from 0.1 to 1.9
- w_out: bfloat16 [2048, 2048], P('tp'), may hold values from -0.25 to 0.25
- mlp_gain: float32 [2048], P('tp'), may hold values from 0.1 to 1.9
- w_gate: bfloat16 [2048, 5632], P(None, 'tp'), may hold values from -0.125 to 0.125
- w_up: bfloat16 [2048, 5632], P(None, 'tp'), may hold values from -0.125 to 0.125
- w_down: bfloat16 [5632, 2048], P('tp'), may hold values from -0.15625 to 0.15625
Outputs:
- mixed: bfloat16 [3, 4096, 2048], P(None, 'seq', 'tp')
- grad_tokens: float32 [3, 4096, 2048], P(None, 'seq', 'tp')
- grad_in_gain: float32 [2048], P('tp')
- grad_w_input: float32 [2048, 2048], P(None, 'tp')
- grad_w_forget: float32 [2048, 2048], P(None, 'tp')
- grad_w_output_gate: float32 [2048, 2048], P(None, 'tp')
- grad_lower_bound: float32 [2048], P('tp')
- grad_mix_gain: float32 [2048], P('tp')
- grad_w_out: float32 [2048, 2048], P('tp')
- grad_mlp_gain: float32 [2048], P('tp')
- grad_w_gate: float32 [2048, 5632], P(None, 'tp')
- grad_w_up: float32 [2048, 5632], P(None, 'tp')
- grad_w_down: float32 [5632, 2048], P('tp')
The draws below stay inside these ranges and needn't reach their ends.
Inputs may be any that keep to these rules, and one draw needn't show every extreme that they name: `lengths`: one slot, chosen by the seed, has exactly 4096 valid positions.
All inputs are finite; a program needn't handle non-finite values.
Results may differ from the reference program's by a relative error of at most 0.024.
Values may be sent and summed in bfloat16 or wider, within the bound.
No kernel may reach another device: no remote copies, remote signals or barrier semaphores. Data moves between devices by JAX's collectives and lax.ppermute only.
A program may use at most 256 MiB of HBM per device.

```python
import math
import jax
import jax.numpy as jnp
from jax import lax

D = 2048
FF = 5632
SLOTS = 3
LEN = 4096


def draw_lengths(key, part):
    first_key, second_key = jax.random.split(key)
    values = jax.random.randint(first_key, (SLOTS,), LEN // 4, LEN + 1)
    chosen = jax.random.randint(second_key, (), 0, SLOTS)
    return jnp.where(jnp.arange(SLOTS) == chosen, LEN, values).astype(jnp.int32)


def draw_lower_bound(key, part):
    first_key, second_key, third_key = jax.random.split(key, 3)
    share = 0.5
    slow = jax.random.uniform(first_key, (D,), jnp.float32) < share
    slow_log = jax.random.uniform(second_key, (D,), jnp.float32, math.log(1.0 / (8.0 * LEN)), math.log(4.0 / LEN))
    fast_log = jax.random.uniform(third_key, (D,), jnp.float32, math.log(0.05), 0.0)
    width = jnp.exp(jnp.where(slow, slow_log, fast_log))
    return (1.0 - width).astype(jnp.float32)


def shard_levels(stream_key, shape, cuts, low, top_value):
    factor_of, own = 1.0, jax.random.fold_in(stream_key, 6)
    for axis_at, blocks in cuts:
        steps = jnp.exp(jax.random.uniform(jax.random.fold_in(own, axis_at), (blocks,), jnp.float32, low / len(cuts), top_value / len(cuts)))
        factor_of = factor_of * jnp.repeat(steps, shape[axis_at] // blocks).reshape([-1 if axis == axis_at else 1 for axis in range(len(shape))])
    return factor_of


def gaussian(own_key, extent, scale, bound, cuts=(), kind=jnp.bfloat16):
    loudness = shard_levels(own_key, extent, cuts, -0.22, 0.18) if cuts else 1.0
    drawn = jax.random.normal(own_key, extent, jnp.float32) * scale * loudness
    return jnp.minimum(jnp.maximum(drawn, -bound), bound).astype(kind)


def setup_inputs(seed: int = 0) -> dict:
    streams_of = jax.random.split(jax.random.key(seed), 15)
    return {
        "tokens": gaussian(streams_of[0], (SLOTS, LEN, D), 1.0, 6.0, ((1, 4), (2, 8))),
        "cotangent": gaussian(streams_of[1], (SLOTS, LEN, D), 1.0, 6.0, ((1, 4), (2, 8))),
        "lengths": draw_lengths(jax.random.fold_in(streams_of[14], 71), 0),
        "in_gain": jnp.clip(1.0 + 0.18 * jax.random.normal(streams_of[3], (D,), jnp.float32), 0.1, 1.9),
        "w_input": gaussian(streams_of[4], (D, D), D ** -0.5, 0.125, ((1, 8),)),
        "w_forget": gaussian(streams_of[5], (D, D), D ** -0.5, 0.125, ((1, 8),)),
        "w_output_gate": gaussian(streams_of[6], (D, D), D ** -0.5, 0.125, ((1, 8),)),
        "lower_bound": draw_lower_bound(jax.random.fold_in(streams_of[14], 71), 0),
        "mix_gain": jnp.clip(1.0 + 0.18 * jax.random.normal(streams_of[8], (D,), jnp.float32), 0.1, 1.9),
        "w_out": gaussian(streams_of[9], (D, D), (D // 4) ** -0.5, 0.25, ((0, 8),)),
        "mlp_gain": jnp.clip(1.0 + 0.18 * jax.random.normal(streams_of[10], (D,), jnp.float32), 0.1, 1.9),
        "w_gate": gaussian(streams_of[11], (D, FF), D ** -0.5, 0.125, ((1, 8),)),
        "w_up": gaussian(streams_of[12], (D, FF), D ** -0.5, 0.125, ((1, 8),)),
        "w_down": gaussian(streams_of[13], (FF, D), (FF // 4) ** -0.5, 0.15625, ((0, 8),)),
    }


@jax.custom_vjp
def low(v):
    return lax.optimization_barrier(v.astype(jnp.bfloat16)).astype(jnp.float32)

@jax.custom_vjp
def low_back(v):
    return v

def low_keep(v):
    return (low(v), None)

def low_pass(kept, grad):
    return (grad,)

def back_keep(v):
    return (v, None)

def back_low(kept, grad):
    return (low(grad),)
low.defvjp(low_keep, low_pass)
low_back.defvjp(back_keep, back_low)
epsilon = 1e-06

def matmul(left, right):
    return jnp.dot(left, right, precision=lax.Precision.HIGHEST, preferred_element_type=jnp.float32)

def combine_pair(earlier, later):
    return (earlier[0] * later[0], later[0] * earlier[1] + later[1])

def one_slot(x_seq, size, params):
    in_gain, w_input, w_forget, w_output_gate, lower_bound, mix_gain, w_out, mlp_gain, w_gate, w_up, w_down = params
    places = jnp.arange(x_seq.shape[0], dtype=jnp.int32)
    live = (places < size).astype(jnp.float32)[:, None]
    r_in = lax.rsqrt(lax.optimization_barrier(jnp.mean(x_seq * x_seq, axis=-1, keepdims=True)) + epsilon)
    normed = low(x_seq * r_in * in_gain)
    pre_in = low_back(matmul(normed, w_input))
    pre_fg = low_back(matmul(normed, w_forget))
    pre_og = low_back(matmul(normed, w_output_gate))
    sig_f = jax.nn.sigmoid(pre_fg)
    forget = lower_bound + (1.0 - lower_bound) * sig_f
    drive = jax.nn.silu(pre_in) * (1.0 - forget)
    state = lax.associative_scan(combine_pair, (forget, drive), axis=0)[1]
    r_mix = lax.rsqrt(lax.optimization_barrier(jnp.mean(state * state, axis=-1, keepdims=True)) + epsilon)
    mixer_out = low(state * r_mix * mix_gain * jax.nn.silu(pre_og))
    resid = x_seq + low_back(matmul(mixer_out, w_out))
    r_mlp = lax.rsqrt(lax.optimization_barrier(jnp.mean(resid * resid, axis=-1, keepdims=True)) + epsilon)
    mlp_in = low(resid * r_mlp * mlp_gain)
    gate_pre = low_back(matmul(mlp_in, w_gate))
    up_pre = low_back(matmul(mlp_in, w_up))
    hidden = low(jax.nn.silu(gate_pre) * up_pre)
    ffn = low_back(matmul(hidden, w_down))
    return live * (resid + ffn)

def reference(tokens, cotangent, lengths, in_gain, w_input, w_forget, w_output_gate, lower_bound, mix_gain, w_out, mlp_gain, w_gate, w_up, w_down):
    tokens_f = tokens.astype(jnp.float32)
    cot_f = cotangent.astype(jnp.float32)
    params = (in_gain, w_input.astype(jnp.float32), w_forget.astype(jnp.float32), w_output_gate.astype(jnp.float32), lower_bound, mix_gain, w_out.astype(jnp.float32), mlp_gain, w_gate.astype(jnp.float32), w_up.astype(jnp.float32), w_down.astype(jnp.float32))
    slot_fn = jax.checkpoint(one_slot)

    def forward(x_all, param_set):

        def apply_one(item):
            return slot_fn(item[0], item[1], param_set)
        return lax.map(apply_one, (x_all, lengths))
    output, pull = jax.vjp(forward, tokens_f, params)
    grad_x, grad_p = pull(cot_f)
    return (output.astype(jnp.bfloat16), grad_x, grad_p[0], grad_p[1], grad_p[2], grad_p[3], grad_p[4], grad_p[5], grad_p[6], grad_p[7], grad_p[8], grad_p[9], grad_p[10])
```

```python
import functools

import jax
import jax.numpy as jnp
import numpy as np
from jax import lax
from jax.experimental import pallas as pl
from jax.experimental.pallas import tpu as pltpu
from jax.sharding import PartitionSpec as P

EPS = 1e-06
F32, BF16 = jnp.float32, jnp.bfloat16
VMEM_LIMIT = 56 * 1024 * 1024


def params(**more):
    return pltpu.CompilerParams(vmem_limit_bytes=VMEM_LIMIT, **more)


def sigmoid(v):
    return 1.0 / (1.0 + jnp.exp(-v))


def ring_of(mesh):
    count = mesh.shape["tp"]
    try:
        coords = [tuple(d.coords) for d in mesh.devices[0]]
        ys = len({c[1] for c in coords})
    except (AttributeError, TypeError):
        ys = 2 if count % 2 == 0 else 1
    zs = count // ys
    if zs * ys != count or zs % 2 or ys < 2:
        return list(range(count))
    cycle = [(z, 0) for z in range(zs)]
    for turn, z in enumerate(reversed(range(zs))):
        across = range(1, ys) if turn % 2 == 0 else reversed(range(1, ys))
        cycle += [(z, y) for y in across]
    return [z * ys + y for z, y in cycle]


class Net:
    def __init__(self, mesh):
        self.seq, self.tp = mesh.shape["seq"], mesh.shape["tp"]
        self.cycle = ring_of(mesh)
        self.bits = [1 << b for b in range(self.seq.bit_length() - 1)]

    def places(self):
        s, t = lax.axis_index("seq"), lax.axis_index("tp")
        where = np.zeros(self.tp, np.int32)
        for i, index in enumerate(self.cycle):
            where[index] = i
        pos = jnp.asarray(where)[t]
        steps = jnp.arange(self.tp, dtype=jnp.int32)
        table = jnp.asarray(np.array(self.cycle, np.int32))
        self.ahead = table[(pos + steps) % self.tp]
        self.behind = table[(pos - steps) % self.tp]
        return s, t

    def shift(self, x, k):
        n = self.tp
        return lax.ppermute(x, "tp", [(self.cycle[i], self.cycle[(i + k) % n]) for i in range(n)])

    def swap(self, x, bit):
        return lax.ppermute(x, "seq", [(i, i ^ bit) for i in range(self.seq)])

    def ring_gather(self, x):
        n = self.tp
        out = [x] + [None] * (n - 1)
        full = (n - 1) // 2
        fore = back = x
        for d in range(1, full + 1):
            fore = out[d] = self.shift(fore, 1)
            back = out[n - d] = self.shift(back, -1)
        if n % 2 == 0:
            half = x.shape[0] // 2
            out[n // 2] = jnp.concatenate([self.shift(fore[:half], 1), self.shift(back[half:], -1)], 0)
        return out

    def ring_scatter(self, chunk):
        n = self.tp
        full = (n - 1) // 2
        fore, back = [], []
        if n % 2 == 0:
            far = chunk(n // 2, [])
            half = far.shape[0] // 2
            up, down = self.shift(far[:half], 1), self.shift(far[half:], -1)
            fore = [jnp.concatenate([up, jnp.zeros_like(down)], 0)]
            back = [jnp.concatenate([jnp.zeros_like(up), down], 0)]
        for d in range(full, 0, -1):
            fore = [self.shift(chunk(n - d, fore), 1)]
            back = [self.shift(chunk(d, back), -1)]
        return chunk(0, fore + back)

    def quad_gather(self, x):
        out = [x] + [None] * (self.seq - 1)
        for bit in reversed(self.bits):
            for j in range(0, self.seq, 2 * bit):
                if out[j] is not None:
                    out[j ^ bit] = self.swap(out[j], bit)
        return out

    def quad_scatter(self, parts):
        parts = list(parts)
        for bit in self.bits[:-1]:
            for j in range(0, self.seq, 2 * bit):
                moved = self.swap(parts[j ^ bit], bit)
                if j == 0:
                    first = moved
                    parts[0] = (parts[0].astype(F32) + moved.astype(F32)).astype(BF16)
                else:
                    parts[j] = (parts[j].astype(F32) + moved.astype(F32)).astype(BF16)
        return [parts[0], self.swap(parts[self.bits[-1]], self.bits[-1])]

    def quad_total(self, x):
        for bit in self.bits:
            order = [j ^ bit for j in range(self.seq)]
            moved = self.swap(x, bit)
            x = x + jnp.stack([moved[j] for j in order], 0)
        return x


SMEM_SPEC = pl.BlockSpec(memory_space=pltpu.SMEM)
VMEM_SPEC = pl.BlockSpec(memory_space=pltpu.VMEM)


def split_rows(x, order, pos_n):
    slots, _, cols = x.shape
    count = order.shape[0]

    def body(order_ref, x_ref, *outs):
        for k in range(count):
            start = pl.multiple_of(order_ref[k] * pos_n, pos_n)
            outs[k][...] = x_ref[:, pl.ds(start, pos_n), :]

    return pl.pallas_call(
        body,
        out_shape=[jax.ShapeDtypeStruct((slots, pos_n, cols), x.dtype)] * count,
        in_specs=[SMEM_SPEC, VMEM_SPEC],
        out_specs=[VMEM_SPEC] * count,
        compiler_params=params(),
    )(order, x)


def join_rows(chunks, order, dtype):
    slots, pos_n, cols = chunks[0].shape
    count = len(chunks)

    def body(order_ref, *refs):
        out = refs[-1]
        for k in range(count):
            start = pl.multiple_of(order_ref[k] * pos_n, pos_n)
            out[:, pl.ds(start, pos_n), :] = refs[k][...].astype(dtype)

    return pl.pallas_call(
        body,
        out_shape=jax.ShapeDtypeStruct((slots, count * pos_n, cols), dtype),
        in_specs=[SMEM_SPEC] + [VMEM_SPEC] * count,
        out_specs=VMEM_SPEC,
        compiler_params=params(),
    )(order, *chunks)


def norm_tokens(chunks, order, gain):
    slots, pos_n, cols = chunks[0].shape
    count = len(chunks)
    rows, width = slots * pos_n, count * cols

    def body(order_ref, gain_ref, *refs):
        x_ref, n_ref = refs[-2:]
        total = jnp.zeros((rows, 1), F32)
        for k in range(count):
            c = refs[k][...].astype(F32).reshape(rows, cols)
            total += jnp.sum(c * c, axis=-1, keepdims=True)
        r = lax.rsqrt(total / width + EPS)
        for k in range(count):
            c = refs[k][...].reshape(rows, cols)
            at = pl.ds(pl.multiple_of(order_ref[k] * cols, cols), cols)
            x_ref[:, at] = c
            n_ref[:, at] = (c.astype(F32) * r * gain_ref[:, at]).astype(BF16)

    return pl.pallas_call(
        body,
        out_shape=[jax.ShapeDtypeStruct((rows, width), BF16)] * 2,
        in_specs=[SMEM_SPEC, VMEM_SPEC] + [VMEM_SPEC] * count,
        out_specs=[VMEM_SPEC] * 2,
        compiler_params=params(),
    )(order, gain.reshape(1, width), *chunks)


def mask_rows(chunks, order, live):
    slots, pos_n, cols = chunks[0].shape
    count = len(chunks)
    rows, width = slots * pos_n, count * cols

    def body(order_ref, live_ref, *refs):
        x_ref = refs[-1]
        for k in range(count):
            c = refs[k][...].astype(F32).reshape(rows, cols)
            at = pl.ds(pl.multiple_of(order_ref[k] * cols, cols), cols)
            x_ref[:, at] = (c * live_ref[...]).astype(BF16)

    return pl.pallas_call(
        body,
        out_shape=jax.ShapeDtypeStruct((rows, width), BF16),
        in_specs=[SMEM_SPEC, VMEM_SPEC] + [VMEM_SPEC] * count,
        out_specs=VMEM_SPEC,
        compiler_params=params(),
    )(order, live, *chunks)


def split_columns(x, order, slots, pos_n, cols):
    count = order.shape[0]

    def body(order_ref, x_ref, *outs):
        for k in range(count):
            at = pl.ds(pl.multiple_of(order_ref[k] * cols, cols), cols)
            outs[k][...] = x_ref[:, at].reshape(slots, pos_n, cols)

    return pl.pallas_call(
        body,
        out_shape=[jax.ShapeDtypeStruct((slots, pos_n, cols), x.dtype)] * count,
        in_specs=[SMEM_SPEC, VMEM_SPEC],
        out_specs=[VMEM_SPEC] * count,
        compiler_params=params(),
    )(order, x)


def tile_scan(decay, drive):
    place = lax.broadcasted_iota(jnp.int32, decay.shape, 0)
    for step in (1, 2, 4):
        inside = place >= step
        before_decay = jnp.where(inside, pltpu.roll(decay, step, 0), 1.0)
        before_drive = jnp.where(inside, pltpu.roll(drive, step, 0), 0.0)
        drive = drive + decay * before_drive
        decay = decay * before_decay
    return decay, drive


def tile_scan_up(decay, drive):
    place = lax.broadcasted_iota(jnp.int32, decay.shape, 0)
    for step in (1, 2, 4):
        inside = place < 8 - step
        before_decay = jnp.where(inside, pltpu.roll(decay, 8 - step, 0), 1.0)
        before_drive = jnp.where(inside, pltpu.roll(drive, 8 - step, 0), 0.0)
        drive = drive + decay * before_drive
        decay = decay * before_decay
    return decay, drive


def gates(pre_in, pre_fg, bound):
    sig_f = sigmoid(pre_fg)
    forget = bound + (1.0 - bound) * sig_f
    sig_in = sigmoid(pre_in)
    act_in = pre_in * sig_in
    slope_in = sig_in * (1.0 + pre_in * (1.0 - sig_in))
    keep = (1.0 - bound) * (1.0 - sig_f)
    return sig_f, forget, act_in, slope_in, keep


def scan_ends(pre, bound, pos_n):
    wide = pre.shape[1] // 3
    blocks = pre.shape[0] // pos_n

    def body(in_ref, fg_ref, bound_ref, decay_ref, end_ref):
        low = bound_ref[...]

        def one(i, carry):
            at = pl.ds(pl.multiple_of(i * 8, 8), 8)
            _, forget, act, _, keep = gates(in_ref[at, :], fg_ref[at, :], low)
            decay, local = tile_scan(forget, act * keep)
            a, h = carry
            return a * decay[7:8, :], decay[7:8, :] * h + local[7:8, :]

        a, h = lax.fori_loop(0, pos_n // 8, one, (jnp.ones((1, wide), F32), jnp.zeros((1, wide), F32)))
        decay_ref[0] = a
        end_ref[0] = h

    return pl.pallas_call(
        body,
        grid=(blocks,),
        out_shape=[jax.ShapeDtypeStruct((blocks, 1, wide), F32)] * 2,
        in_specs=[
            pl.BlockSpec((pos_n, wide), lambda b: (b, 0)),
            pl.BlockSpec((pos_n, wide), lambda b: (b, 1)),
            pl.BlockSpec((1, wide), lambda b: (0, 0)),
        ],
        out_specs=[pl.BlockSpec((1, 1, wide), lambda b: (b, 0, 0))] * 2,
        compiler_params=params(),
    )(pre, pre, bound)


def scan_heads(place, decay, end, reverse):
    behind, count, slots, wide = decay.shape

    def body(place_ref, decay_ref, end_ref, head_ref):
        s, own = place_ref[0], place_ref[1]

        def one(i, state):
            step = count * behind - 1 - i if reverse else i
            block, t = step // behind, step % behind
            j = lax.bitwise_xor(s, block)

            @pl.when(t == own)
            def _():
                head_ref[j] = state

            d = place_ref[2 + t]
            return decay_ref[d, j] * state + end_ref[d, j]

        lax.fori_loop(0, count * behind, one, jnp.zeros((slots, wide), F32))

    return pl.pallas_call(
        body,
        out_shape=jax.ShapeDtypeStruct((count, slots, wide), F32),
        in_specs=[SMEM_SPEC, VMEM_SPEC, VMEM_SPEC],
        out_specs=VMEM_SPEC,
        compiler_params=params(),
    )(place, decay, end)


def scan_states(pre, bound, gain, head, pos_n):
    wide = pre.shape[1] // 3
    blocks = pre.shape[0] // pos_n

    def body(in_ref, fg_ref, og_ref, bound_ref, gain_ref, head_ref, state_ref, mix_ref, sum_ref):
        low = bound_ref[...]

        def one(i, h):
            at = pl.ds(pl.multiple_of(i * 8, 8), 8)
            _, forget, act, _, keep = gates(in_ref[at, :], fg_ref[at, :], low)
            decay, local = tile_scan(forget, act * keep)
            state = local + decay * h
            state_ref[at, :] = state
            square = jnp.sum(state * state, axis=-1, keepdims=True)
            sum_ref[at, :] = jnp.broadcast_to(square, (8, 128))
            return state[7:8, :]

        lax.fori_loop(0, pos_n // 8, one, head_ref[0])
        og = og_ref[...]
        mix_ref[...] = (state_ref[...] * gain_ref[...] * (og * sigmoid(og))).astype(BF16)

    row = pl.BlockSpec((1, wide), lambda b: (0, 0))
    block = pl.BlockSpec((pos_n, wide), lambda b: (b, 0))
    return pl.pallas_call(
        body,
        grid=(blocks,),
        out_shape=[
            jax.ShapeDtypeStruct((blocks * pos_n, wide), F32),
            jax.ShapeDtypeStruct((blocks * pos_n, wide), BF16),
            jax.ShapeDtypeStruct((blocks * pos_n, 128), F32),
        ],
        in_specs=[
            block,
            pl.BlockSpec((pos_n, wide), lambda b: (b, 1)),
            pl.BlockSpec((pos_n, wide), lambda b: (b, 2)),
            row,
            row,
            pl.BlockSpec((1, 1, wide), lambda b: (b, 0, 0)),
        ],
        out_specs=[block, block, pl.BlockSpec((pos_n, 128), lambda b: (b, 0))],
        compiler_params=params(),
    )(pre, pre, pre, bound, gain, head)


def back_ends(pre, bound, local, pos_n):
    wide = local.shape[1]
    blocks = local.shape[0] // pos_n
    tiles = pos_n // 8

    def body(fg_ref, local_ref, bound_ref, end_ref):
        low = bound_ref[...]

        def one(i, g):
            at = pl.ds(pl.multiple_of((tiles - 1 - i) * 8, 8), 8)
            forget = low + (1.0 - low) * sigmoid(fg_ref[at, :])
            decay, part = tile_scan_up(forget, forget * local_ref[at, :])
            return decay[0:1, :] * g + part[0:1, :]

        end_ref[0] = lax.fori_loop(0, tiles, one, jnp.zeros((1, wide), F32))

    return pl.pallas_call(
        body,
        grid=(blocks,),
        out_shape=jax.ShapeDtypeStruct((blocks, 1, wide), F32),
        in_specs=[
            pl.BlockSpec((pos_n, wide), lambda b: (b, 1)),
            pl.BlockSpec((pos_n, wide), lambda b: (b, 0)),
            pl.BlockSpec((1, wide), lambda b: (0, 0)),
        ],
        out_specs=pl.BlockSpec((1, 1, wide), lambda b: (b, 0, 0)),
        compiler_params=params(),
    )(pre, local, bound)


def back_states(pre, bound, local, state, head, tail, pos_n):
    wide = local.shape[1]
    blocks = local.shape[0] // pos_n
    pairs = pos_n // 16

    def body(in_ref, fg_ref, bound_ref, local_ref, state_ref, head_ref, tail_ref, gin_ref, gfg_ref, low_ref):
        low = bound_ref[...]
        place = lax.broadcasted_iota(jnp.int32, (8, wide), 0)

        def half(tile, g, total):
            at = pl.ds(pl.multiple_of(tile * 8, 8), 8)
            sig_f, forget, act, slope, keep = gates(in_ref[at, :], fg_ref[at, :], low)
            loc = local_ref[at, :]
            decay, part = tile_scan_up(forget, forget * loc)
            whole = part + decay * g
            after = jnp.where(place == 7, g, pltpu.roll(whole, 7, 0))
            g_state = loc + after
            now = state_ref[at, :]
            last = jnp.maximum(tile * 8 - 1, 0)
            first = jnp.where(tile == 0, head_ref[0], state_ref[pl.ds(last, 1), :])
            before = jnp.where(place == 0, first, pltpu.roll(now, 1, 0))
            g_forget = g_state * (before - act)
            total = total + g_forget * (1.0 - sig_f)
            return g_state * keep * slope, g_forget * keep * sig_f, whole[0:1, :], total

        def one(i, carry):
            g, total = carry
            pair = pairs - 1 - i
            in_2, fg_2, g, total = half(2 * pair + 1, g, total)
            in_1, fg_1, g, total = half(2 * pair, g, total)
            at = pl.ds(pl.multiple_of(pair * 16, 16), 16)
            gin_ref[at, :] = jnp.concatenate([in_1, in_2], 0).astype(BF16)
            gfg_ref[at, :] = jnp.concatenate([fg_1, fg_2], 0).astype(BF16)
            return g, total

        _, total = lax.fori_loop(0, pairs, one, (tail_ref[0], jnp.zeros((8, wide), F32)))
        low_ref[0] = jnp.sum(total, axis=0, keepdims=True)

    row = pl.BlockSpec((1, wide), lambda b: (0, 0))
    block = pl.BlockSpec((pos_n, wide), lambda b: (b, 0))
    edge = pl.BlockSpec((1, 1, wide), lambda b: (b, 0, 0))
    return pl.pallas_call(
        body,
        grid=(blocks,),
        out_shape=[
            jax.ShapeDtypeStruct((blocks * pos_n, wide), BF16),
            jax.ShapeDtypeStruct((blocks * pos_n, wide), BF16),
            jax.ShapeDtypeStruct((blocks, 1, wide), F32),
        ],
        in_specs=[block, pl.BlockSpec((pos_n, wide), lambda b: (b, 1)), row, block, block, edge, edge],
        out_specs=[block, block, edge],
        compiler_params=params(),
    )(pre, pre, bound, local, state, head, tail)


def dot_nt(a, b):
    return lax.dot_general(a, b, (((1,), (1,)), ((), ())), preferred_element_type=F32)


def dot_nn(a, b):
    return lax.dot_general(a, b, (((1,), (0,)), ((), ())), preferred_element_type=F32)


def dot_tn(a, b):
    return lax.dot_general(a, b, (((0,), (0,)), ((), ())), preferred_element_type=F32)


def on_device(
    net,
    tokens,
    cotangent,
    lengths,
    in_gain,
    w_input,
    w_forget,
    w_output_gate,
    lower_bound,
    mix_gain,
    w_out,
    mlp_gain,
    w_gate,
    w_up,
    w_down,
):
    s, t = net.places()
    n_seq, n_tp = net.seq, net.tp
    slots, group, cols = tokens.shape
    width = cols * n_tp
    pos_n = group // n_tp
    rows = slots * pos_n
    dq = cols // n_seq
    fq = w_down.shape[0] // n_seq
    chan, hid = dq * n_tp, fq * n_tp
    order = [j for j in range(n_seq)]

    def quarter_t(w, q):
        return lax.dynamic_slice_in_dim(w, s * q, q, 1).T

    mix_w = jnp.concatenate(
        [quarter_t(w, dq) for w in (w_input, w_forget, w_output_gate)]
        + [lax.dynamic_slice_in_dim(w_out, s * dq, dq, 0)],
        0,
    )
    gate_w = jnp.concatenate([quarter_t(w_gate, fq), quarter_t(w_up, fq)], 0)
    down_w = lax.dynamic_slice_in_dim(w_down, s * fq, fq, 0)
    small = jnp.stack([lax.dynamic_slice_in_dim(v, s * dq, dq) for v in (lower_bound, mix_gain)], 0)

    def to_rows(x):
        pieces = split_rows(x, net.ahead, pos_n)
        return [pieces[0]] + [net.shift(pieces[k], k) for k in range(1, n_tp)]

    def from_rows(x, dtype):
        pieces = split_columns(x, net.ahead, slots, pos_n, cols)
        moved = [pieces[0]] + [net.shift(pieces[k], k) for k in range(1, n_tp)]
        return join_rows(moved, net.behind, dtype)

    def live_of(j):
        where = lax.bitwise_xor(s, j) * group + t * pos_n + jnp.arange(pos_n, dtype=jnp.int32)
        return (where[None, :] < lengths[:, None]).astype(F32).reshape(rows, 1)

    live = live_of(0)
    tok, normed_own = norm_tokens(to_rows(tokens), net.behind, in_gain)
    normed = jnp.concatenate(net.quad_gather(normed_own), 0)

    gathered_small = [small] + [net.shift(small, k) for k in range(1, n_tp)]
    bound = jnp.concatenate([g[0] for g in gathered_small], 0).reshape(1, chan)
    gain = jnp.concatenate([g[1] for g in gathered_small], 0).reshape(1, chan)
    gathered_gain = jnp.stack([mlp_gain] + [net.shift(mlp_gain, k) for k in range(1, n_tp)], 0)
    mlp_full = jnp.zeros((n_tp, cols), F32).at[net.behind].set(gathered_gain).reshape(1, width)

    mix_all = net.ring_gather(mix_w)
    w3 = jnp.concatenate([w[i * dq : (i + 1) * dq] for i in range(3) for w in mix_all], 0)
    wo = jnp.concatenate([w[3 * dq :] for w in mix_all], 0)
    gate_all = net.ring_gather(gate_w)
    wg = jnp.concatenate([w[:fq] for w in gate_all], 0)
    wu = jnp.concatenate([w[fq:] for w in gate_all], 0)
    wd = jnp.concatenate(net.ring_gather(down_w), 0)

    pre = dot_nt(normed, w3)
    decay, end = scan_ends(pre, bound, pos_n)

    place = jnp.concatenate([jnp.stack([s, t]), jnp.zeros((n_tp,), jnp.int32).at[net.behind].set(jnp.arange(n_tp, dtype=jnp.int32))])

    def spread(v):
        lead = v.shape[:-1]
        out = [v]
        for k in range(1, n_tp):
            moved = net.shift(v, k).reshape(lead + (n_tp, dq))
            out.append(jnp.roll(moved, k, axis=-2).reshape(v.shape))
        return jnp.stack(out, 0)

    both = spread(jnp.stack([decay, end], 0).reshape(2, n_seq, slots, chan))
    decays, ends = both[:, 0], both[:, 1]
    head = scan_heads(place, decays, ends, False).reshape(n_seq * slots, 1, chan)
    state, mix, squares = scan_states(pre, bound, gain, head, pos_n)
    total = net.quad_total(squares[:, 0].reshape(n_seq, rows))
    r_mix = lax.rsqrt(total / width + EPS).reshape(n_seq * rows, 1)
    part = dot_nn(mix, wo).astype(BF16).reshape(n_seq, rows, width)
    branch = sum(p.astype(F32) for p in net.quad_scatter([part[j] for j in order]))
    resid = tok.astype(F32) + r_mix[:rows] * branch
    r_mlp = lax.rsqrt(jnp.mean(resid * resid, axis=-1, keepdims=True) + EPS)
    scaled = resid * r_mlp
    mlp_in = jnp.concatenate(net.quad_gather((scaled * mlp_full).astype(BF16)), 0)

    gate_pre = dot_nt(mlp_in, wg)
    up_pre = dot_nt(mlp_in, wu)
    sig_g = sigmoid(gate_pre)
    act_g = gate_pre * sig_g
    slope_g = sig_g * (1.0 + gate_pre * (1.0 - sig_g))
    hidden = (act_g * up_pre).astype(BF16)
    part = dot_nn(hidden, wd).astype(BF16).reshape(n_seq, rows, width)
    ffn = sum(p.astype(F32) for p in net.quad_scatter([part[j] for j in order]))
    mixed = from_rows((live * (resid + ffn)).astype(BF16), BF16)

    cot = mask_rows(to_rows(cotangent), net.behind, live)
    grad_out = jnp.concatenate(net.quad_gather(cot), 0)
    grad_hidden = dot_nt(grad_out, wd)
    grad_gate = (grad_hidden * up_pre * slope_g).astype(BF16)
    grad_up = (grad_hidden * act_g).astype(BF16)
    part = (dot_nn(grad_gate, wg) + dot_nn(grad_up, wu)).astype(BF16).reshape(n_seq, rows, width)
    grad_mlp_in = sum(p.astype(F32) for p in net.quad_scatter([part[j] for j in order]))

    def reduce_rows(pairs):
        def chunk(d, add):
            out = jnp.concatenate(
                [dot_tn(left[:, d * q : (d + 1) * q], right) for left, right, q in pairs], 0
            )
            for a in add:
                out = out + a.astype(F32)
            return out.astype(BF16)

        return net.ring_scatter(chunk)

    def whole_rows(x):
        blocks = net.quad_gather(x)
        out = jnp.zeros((n_seq,) + x.shape, F32)
        for j in order:
            out = lax.dynamic_update_index_in_dim(out, blocks[j].astype(F32), lax.bitwise_xor(s, j), 0)
        return out

    grad_w_down = whole_rows(reduce_rows([(hidden, grad_out, fq)])).reshape(n_seq * fq, width)
    grad_gu = whole_rows(reduce_rows([(grad_gate, mlp_in, fq), (grad_up, mlp_in, fq)]))
    grad_w_gate = grad_gu[:, :fq].reshape(n_seq * fq, width).T
    grad_w_up = grad_gu[:, fq:].reshape(n_seq * fq, width).T

    grad_mlp_gain = jnp.sum(grad_mlp_in * scaled, axis=0)
    grad_scaled = grad_mlp_in * mlp_full
    inner = jnp.sum(resid * grad_scaled, axis=-1, keepdims=True)
    grad_resid = cot.astype(F32) + r_mlp * grad_scaled - resid * r_mlp**3 * inner / width
    grad_branch = jnp.concatenate(net.quad_gather(grad_resid.astype(BF16)), 0)

    grad_mix = dot_nt(grad_branch, wo)
    pre_og = pre[:, 2 * chan :]
    sig_o = sigmoid(pre_og)
    act_o = pre_og * sig_o
    slope_o = sig_o * (1.0 + pre_og * (1.0 - sig_o))
    state_norm = state * r_mix
    grad_mix_gain = jnp.sum(grad_mix * state_norm * act_o, axis=0)
    grad_og = (grad_mix * state_norm * gain * slope_o).astype(BF16)
    grad_norm = grad_mix * gain * act_o
    inner = net.quad_total(jnp.sum(state * grad_norm, axis=-1).reshape(n_seq, rows)).reshape(-1, 1)
    grad_local = r_mix * grad_norm - state * (r_mix**3 * inner / width)
    back_end = spread(back_ends(pre, bound, grad_local, pos_n).reshape(n_seq, slots, chan))
    tail = scan_heads(place, decays, back_end, True).reshape(n_seq * slots, 1, chan)
    grad_in, grad_fg, low_sums = back_states(pre, bound, grad_local, state, head, tail, pos_n)
    mixer_out = (mix.astype(F32) * r_mix).astype(BF16)
    grad_3 = jnp.concatenate([grad_in, grad_fg, grad_og], 1)
    part = dot_nn(grad_3, w3).astype(BF16).reshape(n_seq, rows, width)
    grad_normed = sum(p.astype(F32) for p in net.quad_scatter([part[j] for j in order]))

    grad_mw = whole_rows(
        reduce_rows(
            [(grad_3[:, i * chan : (i + 1) * chan], normed, dq) for i in range(3)]
            + [(mixer_out, grad_branch, dq)]
        )
    )
    grads_3 = [grad_mw[:, i * dq : (i + 1) * dq].reshape(n_seq * dq, width).T for i in range(3)]
    grad_w_out = grad_mw[:, 3 * dq :].reshape(n_seq * dq, width)

    x = tok.astype(F32)
    r_in = lax.rsqrt(jnp.mean(x * x, axis=-1, keepdims=True) + EPS)
    grad_in_gain = jnp.sum(grad_normed * x * r_in, axis=0)
    scaled_g = grad_normed * in_gain
    inner = jnp.sum(x * scaled_g, axis=-1, keepdims=True)
    grad_tok = grad_resid + r_in * scaled_g - x * r_in**3 * inner / width
    grad_tokens = from_rows(grad_tok.astype(BF16), F32)

    full = lax.psum(jnp.stack([grad_in_gain, grad_mlp_gain], 0), ("seq", "tp"))
    mine = lax.dynamic_slice_in_dim(full, t * cols, cols, 1)
    sums = jnp.stack([jnp.sum(low_sums, axis=(0, 1)), grad_mix_gain], 0).reshape(2, n_tp, dq)
    chans = sums[:, 0]
    for k in range(1, n_tp):
        chans = chans + net.shift(sums[:, (n_tp - k) % n_tp], k)
    chans = whole_rows(chans)
    return (
        mixed,
        grad_tokens,
        mine[0],
        grads_3[0],
        grads_3[1],
        grads_3[2],
        chans[:, 0].reshape(-1),
        chans[:, 1].reshape(-1),
        grad_w_out,
        mine[1],
        grad_w_gate,
        grad_w_up,
        grad_w_down,
    )


def solution(mesh):
    return jax.shard_map(
        functools.partial(on_device, Net(mesh)),
        mesh=mesh,
        in_specs=(
            P(None, "seq", "tp"),
            P(None, "seq", "tp"),
            P(),
            P(),
            P(None, "tp"),
            P(None, "tp"),
            P(None, "tp"),
            P("tp"),
            P("tp"),
            P("tp", None),
            P("tp"),
            P(None, "tp"),
            P(None, "tp"),
            P("tp", None),
        ),
        out_specs=(
            P(None, "seq", "tp"),
            P(None, "seq", "tp"),
            P("tp"),
            P(None, "tp"),
            P(None, "tp"),
            P(None, "tp"),
            P("tp"),
            P("tp"),
            P("tp", None),
            P("tp"),
            P(None, "tp"),
            P(None, "tp"),
            P("tp", None),
        ),
        check_vma=False,
    )
```

```python
import functools

import jax
import jax.numpy as jnp
import numpy as np
from jax import lax
from jax.experimental import pallas as pl
from jax.experimental.pallas import tpu as pltpu
from jax.sharding import PartitionSpec as P

EPS = 1e-06
F32, BF16 = jnp.float32, jnp.bfloat16
VMEM_LIMIT = 56 * 1024 * 1024


def params(**more):
    return pltpu.CompilerParams(vmem_limit_bytes=VMEM_LIMIT, **more)


def sigmoid(v):
    return 1.0 / (1.0 + jnp.exp(-v))


def fast_sigmoid(v):
    d = 1.0 + jnp.exp(jnp.minimum(-v, 80.0))
    r = pl.reciprocal(d, approx=True)
    return r * (2.0 - d * r)


def ring_of(mesh):
    count = mesh.shape["tp"]
    try:
        coords = [tuple(d.coords) for d in mesh.devices[0]]
        ys = len({c[1] for c in coords})
    except (AttributeError, TypeError):
        ys = 2 if count % 2 == 0 else 1
    zs = count // ys
    if zs * ys != count or zs % 2 or ys < 2:
        return list(range(count))
    cycle = [(z, 0) for z in range(zs)]
    for turn, z in enumerate(reversed(range(zs))):
        across = range(1, ys) if turn % 2 == 0 else reversed(range(1, ys))
        cycle += [(z, y) for y in across]
    return [z * ys + y for z, y in cycle]


class Net:
    def __init__(self, mesh):
        self.seq, self.tp = mesh.shape["seq"], mesh.shape["tp"]
        self.cycle = ring_of(mesh)
        self.bits = [1 << b for b in range(self.seq.bit_length() - 1)]
        self.tp_bits = [1 << b for b in range(self.tp.bit_length() - 1)]

    def places(self):
        s, t = lax.axis_index("seq"), lax.axis_index("tp")
        where = np.zeros(self.tp, np.int32)
        for i, index in enumerate(self.cycle):
            where[index] = i
        pos = jnp.asarray(where)[t]
        steps = [[self.cycle[(i - d) % self.tp] for d in range(self.tp)] for i in where]
        self.order = lax.dynamic_index_in_dim(jnp.asarray(np.array(steps, np.int32)), t, 0, False)
        self.behind = [self.order[d] for d in range(self.tp)]
        self.inverse = (pos - jnp.asarray(where)) % self.tp
        return s, t

    def shift(self, x, k):
        n = self.tp
        return lax.ppermute(x, "tp", [(self.cycle[i], self.cycle[(i + k) % n]) for i in range(n)])

    def cross(self, x, bit):
        return lax.ppermute(x, "tp", [(i, i ^ bit) for i in range(self.tp)])

    def swap(self, x, bit):
        return lax.ppermute(x, "seq", [(i, i ^ bit) for i in range(self.seq)])

    def halves(self, size):
        half = size // 2
        return half // 16 * 16 if size >= 32 else half

    def gather_first(self, x):
        out = [x] + [None] * (self.seq - 1)
        for bit in reversed(self.bits):
            out[bit] = self.swap(x, bit)
        return out

    def gather_rest(self, out):
        out = list(out)
        for j in range(self.seq):
            if out[j] is None:
                out[j] = self.swap(out[j & (j - 1)], j & -j)
        return out

    def quad_far_part(self, parts):
        parts = list(parts)
        for bit in self.bits[:-1]:
            for j in reversed(range(0, len(parts), 2 * bit)):
                moved = self.swap(parts[j ^ bit], bit)
                parts[j] = (parts[j].astype(F32) + moved.astype(F32)).astype(BF16)
        return parts[0]

    def quad_near(self, parts):
        half = self.seq // 2
        far = self.quad_far_part(parts[half:])
        return [self.quad_far_part(parts[:half]), far]

    def quad_far(self, near):
        return [near[0], self.swap(near[1], self.bits[-1])]

    def total_step(self, x, bit):
        moved = self.swap(x, bit)
        return x + jnp.stack([moved[j ^ bit] for j in range(self.seq)], 0)

    def total_near(self, x):
        for bit in self.bits[:-1]:
            x = self.total_step(x, bit)
        return x

    def total_far(self, x):
        return self.total_step(x, self.bits[-1])


def after(x, *others):
    return lax.optimization_barrier((x,) + others)[0]


def hold(*trees):
    return lax.optimization_barrier(trees)


class RingGather:
    def __init__(self, net, x):
        self.net, self.size = net, x.shape[0]
        n = net.tp
        self.blocks = [[(x, 0)]] + [None] * (n - 1)
        self.full = (n - 1) // 2
        self.made = 0
        self.came = (x, x)

    def done(self):
        return self.made == self.net.tp // 2

    def sends(self):
        if self.done():
            return ()
        fore, back = self.came
        if self.made < self.full:
            return fore, back
        half = self.net.halves(self.size)
        return fore[:half], back[half:]

    def launch(self, sends):
        if self.done():
            return
        net, n = self.net, self.net.tp
        self.made += 1
        d = self.made
        self.came = net.shift(sends[0], 1), net.shift(sends[1], -1)
        if d <= self.full:
            self.blocks[d], self.blocks[n - d] = [(self.came[0], 0)], [(self.came[1], 0)]
        else:
            self.blocks[d] = [(self.came[0], 0), (self.came[1], net.halves(self.size))]

    def finish(self):
        while not self.done():
            self.launch(self.sends())

    def rows(self, start, q):
        out = []
        for block in self.blocks:
            whole = jnp.concatenate([a for a, _ in block], 0) if len(block) > 1 else block[0][0]
            out.append(whole[start : start + q])
        return out


class RingScatter:
    def __init__(self, net, chunk):
        self.net, self.chunk = net, chunk
        self.d = net.tp // 2
        self.came = ()
        self.half = net.halves(chunk(self.d).shape[0]) if net.tp % 2 == 0 else 0

    def done(self):
        return self.d == 0

    def plus(self, own, part, start):
        if part is None:
            return own
        rest = own.shape[0] - start - part.shape[0]
        return (own.astype(F32) + jnp.pad(part.astype(F32), ((start, rest), (0, 0)))).astype(BF16)

    def sends(self):
        if self.done():
            return ()
        n, d = self.net.tp, self.d
        if 2 * d == n:
            far = self.chunk(d)
            return far[: self.half], far[self.half :]
        fore, back = self.came if self.came else (None, None)
        return self.plus(self.chunk(n - d), fore, 0), self.plus(self.chunk(d), back, self.start())

    def start(self):
        return self.half if 2 * (self.d + 1) == self.net.tp else 0

    def launch(self, sends):
        if self.done():
            return
        self.d -= 1
        self.came = self.net.shift(sends[0], 1), self.net.shift(sends[1], -1)

    def result(self):
        while not self.done():
            self.launch(self.sends())
        own = self.chunk(0)
        start = self.start()
        return self.plus(self.plus(own, self.came[0], 0), self.came[1], start)


SMEM_SPEC = pl.BlockSpec(memory_space=pltpu.SMEM)
VMEM_SPEC = pl.BlockSpec(memory_space=pltpu.VMEM)


def norm_tokens(blocks, gain, rows):
    count, _, cols = blocks.shape
    width = count * cols

    def body(gain_ref, in_ref, x_ref, n_ref):
        total = jnp.zeros((rows, 1), F32)
        for k in range(count):
            c = in_ref[k, :rows].astype(F32)
            total += jnp.sum(c * c, axis=-1, keepdims=True)
        r = lax.rsqrt(total / width + EPS)
        for k in range(count):
            c = in_ref[k, :rows]
            at = slice(k * cols, (k + 1) * cols)
            x_ref[:, at] = c
            n_ref[:, at] = (c.astype(F32) * r * gain_ref[:, at]).astype(BF16)

    return pl.pallas_call(
        body,
        out_shape=[jax.ShapeDtypeStruct((rows, width), BF16)] * 2,
        in_specs=[VMEM_SPEC] * 2,
        out_specs=[VMEM_SPEC] * 2,
        compiler_params=params(),
    )(gain.reshape(1, width), blocks)


def mask_rows(blocks, live):
    count, rows, cols = blocks.shape
    width = count * cols

    def body(live_ref, in_ref, x_ref):
        for k in range(count):
            at = slice(k * cols, (k + 1) * cols)
            x_ref[:, at] = (in_ref[k].astype(F32) * live_ref[...]).astype(BF16)

    return pl.pallas_call(
        body,
        out_shape=jax.ShapeDtypeStruct((rows, width), BF16),
        in_specs=[VMEM_SPEC] * 2,
        out_specs=VMEM_SPEC,
        compiler_params=params(),
    )(live, blocks)


def tile_scan(decay, drive):
    place = lax.broadcasted_iota(jnp.int32, decay.shape, 0)
    for step in (1, 2, 4):
        inside = place >= step
        before_decay = jnp.where(inside, pltpu.roll(decay, step, 0), 1.0)
        before_drive = jnp.where(inside, pltpu.roll(drive, step, 0), 0.0)
        drive = drive + decay * before_drive
        decay = decay * before_decay
    return decay, drive


def tile_scan_up(decay, drive):
    place = lax.broadcasted_iota(jnp.int32, decay.shape, 0)
    for step in (1, 2, 4):
        inside = place < 8 - step
        before_decay = jnp.where(inside, pltpu.roll(decay, 8 - step, 0), 1.0)
        before_drive = jnp.where(inside, pltpu.roll(drive, 8 - step, 0), 0.0)
        drive = drive + decay * before_drive
        decay = decay * before_decay
    return decay, drive


def gates(pre_in, pre_fg, bound):
    sig_f = fast_sigmoid(pre_fg)
    forget = bound + (1.0 - bound) * sig_f
    sig_in = fast_sigmoid(pre_in)
    act_in = pre_in * sig_in
    slope_in = sig_in * (1.0 + pre_in * (1.0 - sig_in))
    keep = (1.0 - bound) * (1.0 - sig_f)
    return sig_f, forget, act_in, slope_in, keep


class Weights:
    def __init__(self):
        self.arrays, self.takes, self.shapes = [], [], []

    def add(self, ring, parts, stride, canonical):
        held, n = len(self.shapes), ring.net.tp
        width = ring.blocks[0][0][0].shape[1]
        self.shapes.append((len(parts) * n * stride, width))
        if stride % 16:
            for start, at in parts:
                rows = ring.rows(start, stride)
                whole = jnp.stack(rows, 0)
                if canonical:
                    whole = whole[ring.net.inverse]
                self.takes.append((len(self.arrays), 0, n * stride, held, None, at))
                self.arrays.append(whole.reshape(n * stride, width))
            return
        seen = {id(a): i for i, a in enumerate(self.arrays)}
        for d, block in enumerate(ring.blocks):
            for array, first in block:
                if id(array) not in seen:
                    seen[id(array)] = len(self.arrays)
                    self.arrays.append(array)
                for start, at in parts:
                    low, high = max(start, first), min(start + stride, first + array.shape[0])
                    if low < high:
                        place = (d, stride) if canonical else None
                        row = at + (low - start) + (0 if canonical else d * stride)
                        self.takes.append((seen[id(array)], low - first, high - low, held, place, row))

    def copies(self, order_ref, refs, held, sems):
        out = []
        for k, (source, first, size, to, place, row) in enumerate(self.takes):
            if place is not None:
                row = pl.multiple_of(order_ref[place[0]] * place[1] + row, 16)
            out.append(
                pltpu.make_async_copy(refs[source].at[pl.ds(first, size)], held[to].at[pl.ds(row, size)], sems.at[k])
            )
        return out


def step_kernel(body, order, count, rows, blocks, weights, ins, outs, width, cost, onto=()):
    any_spec = pl.BlockSpec(memory_space=pl.ANY)
    n_x, n_w, n_in, n_out = len(blocks), len(weights.arrays), len(ins), len(outs)
    n_part = count if width else 0
    n_held, n_onto = len(weights.shapes), len(onto)

    def kernel(order_ref, *refs):
        refs = list(refs)

        def take(k):
            out = refs[:k]
            del refs[:k]
            return out

        x_refs, w_refs, in_refs, _ = take(n_x), take(n_w), take(n_in), take(n_onto)
        out_refs, part_refs = take(n_out), take(n_part)
        held, w_sems = take(n_held), take(1)[0]
        xs, x_sems = take(2) if n_x else (None, None)
        kept, part_sems = take(2) if n_part else (None, None)
        j = pl.program_id(0)
        loads = weights.copies(order_ref, w_refs, held, w_sems)
        x_loads = [pltpu.make_async_copy(x_refs[k], xs.at[k], x_sems.at[k]) for k in range(n_x)]

        @pl.when(j == 0)
        def _():
            for load in loads + x_loads:
                load.start()
            for load in loads:
                load.wait()

        for k in range(n_x):

            @pl.when(j == k)
            def _(k=k):
                x_loads[k].wait()

        x = xs[j] if n_x else None
        part = body(x, held, in_refs, out_refs)
        stores = [pltpu.make_async_copy(kept.at[k % 2], part_refs[k], part_sems.at[k]) for k in range(n_part)]
        for k in range(n_part):

            @pl.when(j == k)
            def _(k=k):
                if k >= 2:
                    stores[k - 2].wait()
                kept[k % 2] = part
                stores[k].start()
                if k == n_part - 1:
                    for store in stores[max(k - 1, 0) :]:
                        store.wait()

    scratch = [pltpu.VMEM(shape, BF16) for shape in weights.shapes]
    scratch.append(pltpu.SemaphoreType.DMA((max(len(weights.takes), 1),)))
    if n_x:
        scratch += [pltpu.VMEM((n_x,) + blocks[0].shape, BF16), pltpu.SemaphoreType.DMA((n_x,))]
    if n_part:
        scratch += [pltpu.VMEM((2, rows, width), BF16), pltpu.SemaphoreType.DMA((n_part,))]
    out = pl.pallas_call(
        kernel,
        grid=(count,),
        out_shape=[shape for shape, _ in outs] + [jax.ShapeDtypeStruct((rows, width), BF16)] * n_part,
        in_specs=[SMEM_SPEC] + [any_spec] * (n_x + n_w) + [spec for _, spec in ins] + [any_spec] * n_onto,
        out_specs=[spec for _, spec in outs] + [any_spec] * n_part,
        input_output_aliases={1 + n_x + n_w + n_in + i: i for i in range(n_onto)},
        scratch_shapes=scratch,
        compiler_params=params(),
        cost_estimate=pl.CostEstimate(flops=cost // 1000, bytes_accessed=1024, transcendentals=0),
    )(order, *blocks, *weights.arrays, *[a for a, _ in ins], *onto)
    return list(out[:n_out]), list(out[n_out:])


def shape_of(*shape, dtype=F32):
    return jax.ShapeDtypeStruct(shape, dtype)


def by_block(rows, wide, first=0, column=0):
    return pl.BlockSpec((rows, wide), lambda b: (b + first, column))


def whole_row(wide):
    return pl.BlockSpec((1, wide), lambda b: (0, 0))


def by_slot(slots, wide, first=0):
    return pl.BlockSpec((1, slots, wide), lambda b: (b + first, 0, 0))


def columns(wide):
    return [slice(c, min(c + 256, wide)) for c in range(0, wide, 256)]


def mixer_in(order, blocks, weights, bound, slots, pos_n):
    count, (rows, depth), wide = len(blocks), blocks[0].shape, bound.shape[1]

    def body(x, held, ins, outs):
        pre_ref, all_ref, decay_ref, end_ref = outs
        low = ins[0][...]
        all_ref[...] = x
        pre_ref[...] = dot_nt(x, held[0][...])

        def one(i, carry):
            out = []
            for k in range(slots):
                at = pl.ds(pl.multiple_of(k * pos_n + i * 8, 8), 8)
                _, forget, act, _, keep = gates(pre_ref[at, :wide], pre_ref[at, wide : 2 * wide], low)
                decay, local = tile_scan(forget, act * keep)
                a, h = carry[k]
                out.append((a * decay[7:8, :], decay[7:8, :] * h + local[7:8, :]))
            return tuple(out)

        start = (jnp.ones((1, wide), F32), jnp.zeros((1, wide), F32))
        ends = lax.fori_loop(0, pos_n // 8, one, (start,) * slots)
        for k in range(slots):
            decay_ref[0, k : k + 1] = ends[k][0]
            end_ref[0, k : k + 1] = ends[k][1]

    outs = [
        (shape_of(count * rows, 3 * wide), by_block(rows, 3 * wide)),
        (shape_of(count * rows, depth, dtype=BF16), by_block(rows, depth)),
        (shape_of(count, slots, wide), by_slot(slots, wide)),
        (shape_of(count, slots, wide), by_slot(slots, wide)),
    ]
    return step_kernel(
        body, order, count, rows, blocks, weights, [(bound, whole_row(wide))], outs, 0, 6 * count * rows * wide * depth
    )[0]


def scan_heads(place, before, whole, reverse):
    count, slots, wide = whole[0].shape

    def body(place_ref, pa_ref, pb_ref, wa_ref, wb_ref, head_ref):
        state = jnp.zeros((slots, wide), F32)
        for i in range(count):
            j = lax.bitwise_xor(place_ref[0], count - 1 - i if reverse else i)
            head_ref[j] = pa_ref[j] * state + pb_ref[j]
            state = wa_ref[j] * state + wb_ref[j]

    return pl.pallas_call(
        body,
        out_shape=shape_of(count, slots, wide),
        in_specs=[SMEM_SPEC] + [VMEM_SPEC] * 4,
        out_specs=VMEM_SPEC,
        compiler_params=params(),
    )(place, *before, *whole)


def mixer_out(order, pre, bound, gain, head, weights, pos_n):
    wide = bound.shape[1]
    count, slots, _ = head.shape
    rows = slots * pos_n
    depth = weights.shapes[0][1]

    def body(x, held, ins, outs):
        pre_ref, bound_ref, gain_ref, head_ref = ins
        state_ref, mix_ref, sum_ref = outs
        low = bound_ref[...]

        def one(i, carry):
            out = []
            for k in range(slots):
                at = pl.ds(pl.multiple_of(k * pos_n + i * 8, 8), 8)
                _, forget, act, _, keep = gates(pre_ref[at, :wide], pre_ref[at, wide : 2 * wide], low)
                decay, local = tile_scan(forget, act * keep)
                state = local + decay * carry[k]
                state_ref[at, :] = state
                square = state * state
                sum_ref[at, :] = sum(square[:, c : c + 128] for c in range(0, wide, 128))
                out.append(state[7:8, :])
            return tuple(out)

        lax.fori_loop(0, pos_n // 8, one, tuple(head_ref[0, k : k + 1] for k in range(slots)))
        og = pre_ref[:, 2 * wide :]
        mix = (state_ref[...] * gain_ref[...] * (og * fast_sigmoid(og))).astype(BF16)
        mix_ref[...] = mix
        return dot_nn(mix, held[0][...]).astype(BF16)

    ins = [
        (pre, by_block(rows, 3 * wide)),
        (bound, whole_row(wide)),
        (gain, whole_row(wide)),
        (head, by_slot(slots, wide)),
    ]
    outs = [
        (shape_of(count * rows, wide), by_block(rows, wide)),
        (shape_of(count * rows, wide, dtype=BF16), by_block(rows, wide)),
        (shape_of(count * rows, 128), by_block(rows, 128)),
    ]
    return step_kernel(body, order, count, rows, [], weights, ins, outs, depth, 2 * count * rows * wide * depth)


def feed_forward(order, blocks, weights, first, count, onto=()):
    (rows, depth), wide = blocks[0].shape, weights.shapes[0][0]

    def body(x, held, ins, outs):
        hid_ref, slope_ref, act_ref, all_ref = outs
        all_ref[...] = x
        for at in columns(wide):
            gate = dot_nt(x, held[0][at, :])
            up = dot_nt(x, held[1][at, :])
            sig = fast_sigmoid(gate)
            act = gate * sig
            hid_ref[:, at] = (act * up).astype(BF16)
            slope_ref[:, at] = (up * (sig * (1.0 + gate * (1.0 - sig)))).astype(BF16)
            act_ref[:, at] = act.astype(BF16)

    outs = [(shape_of(count * rows, wide, dtype=BF16), by_block(rows, wide, first))] * 3
    outs = outs + [(shape_of(count * rows, depth, dtype=BF16), by_block(rows, depth, first))]
    cost = 4 * len(blocks) * rows * wide * depth
    return step_kernel(body, order, len(blocks), rows, blocks, weights, [], outs, 0, cost, onto)[0]


def down_parts(order, hidden, weights, rows):
    wide, depth = weights.shapes[0]
    count = hidden.shape[0] // rows

    def body(x, held, ins, outs):
        return dot_nn(ins[0][...], held[0][...]).astype(BF16)

    return step_kernel(
        body, order, count, rows, [], weights, [(hidden, by_block(rows, wide))], [], depth, 2 * count * rows * wide * depth
    )[1]


def back_hidden(order, g, weights, slope, act, rows):
    wide, depth = weights.shapes[0]
    count = g.shape[0] // rows

    def body(x, held, ins, outs):
        g_ref, slope_ref, act_ref = ins
        for at in columns(wide):
            hid = dot_nt(g_ref[...], held[0][at, :])
            outs[0][:, at] = (hid * slope_ref[:, at].astype(F32)).astype(BF16)
            outs[1][:, at] = (hid * act_ref[:, at].astype(F32)).astype(BF16)

    block = by_block(rows, wide)
    ins = [(g, by_block(rows, depth)), (slope, block), (act, block)]
    outs = [(shape_of(count * rows, wide, dtype=BF16), block)] * 2
    return step_kernel(body, order, count, rows, [], weights, ins, outs, 0, 2 * count * rows * wide * depth)[0]


def back_pair(order, a, b, weights, rows, first, count):
    wide, depth = weights.shapes[0]

    def body(x, held, ins, outs):
        return (dot_nn(ins[0][...], held[0][...]) + dot_nn(ins[1][...], held[1][...])).astype(BF16)

    block = by_block(rows, wide, first)
    return step_kernel(
        body, order, count, rows, [], weights, [(a, block), (b, block)], [], depth, 4 * count * rows * wide * depth
    )[1]


def back_mixer(order, blocks, weights, pre, state, mix, r_mix, gain):
    count, (rows, depth), wide = len(blocks), blocks[0].shape, gain.shape[1]

    def body(x, held, ins, outs):
        og_ref, state_ref, mix_ref, r_ref, gain_ref = ins
        norm_ref, og_out, mix_out, all_ref, inner_ref, sum_ref = outs
        all_ref[...] = x
        mix_out[...] = (mix_ref[...].astype(F32) * r_ref[...]).astype(BF16)
        g = dot_nt(x, held[0][...])
        og, state = og_ref[...], state_ref[...]
        sig = fast_sigmoid(og)
        act = og * sig
        g_state = g * (state * r_ref[...])
        sum_ref[0] = jnp.sum((g_state * act).reshape(rows // 8, 8, wide), 0)
        og_out[...] = (g_state * gain_ref[...] * (sig * (1.0 + og * (1.0 - sig)))).astype(BF16)
        norm = g * gain_ref[...] * act
        norm_ref[...] = norm
        inner = state * norm
        inner_ref[...] = sum(inner[:, c : c + 128] for c in range(0, wide, 128))

    ins = [
        (pre, pl.BlockSpec((rows, wide), lambda b: (b, 2))),
        (state, by_block(rows, wide)),
        (mix, by_block(rows, wide)),
        (r_mix, by_block(rows, 1)),
        (gain, whole_row(wide)),
    ]
    outs = [
        (shape_of(count * rows, wide), by_block(rows, wide)),
        (shape_of(count * rows, wide, dtype=BF16), by_block(rows, wide)),
        (shape_of(count * rows, wide, dtype=BF16), by_block(rows, wide)),
        (shape_of(count * rows, depth, dtype=BF16), by_block(rows, depth)),
        (shape_of(count * rows, 128), by_block(rows, 128)),
        (shape_of(count, 8, wide), by_slot(8, wide)),
    ]
    return step_kernel(body, order, count, rows, blocks, weights, ins, outs, 0, 2 * count * rows * wide * depth)[0]


def back_ends(pre, bound, norm, state, r_mix, coef, slots, pos_n):
    wide = norm.shape[1]
    rows = slots * pos_n
    count = norm.shape[0] // rows
    tiles = pos_n // 8

    def body(fg_ref, norm_ref, state_ref, r_ref, coef_ref, bound_ref, end_ref):
        low = bound_ref[...]

        def one(i, carry):
            out = []
            for k in range(slots):
                at = pl.ds(pl.multiple_of(k * pos_n + (tiles - 1 - i) * 8, 8), 8)
                local = r_ref[at, :] * norm_ref[at, :] - coef_ref[at, :] * state_ref[at, :]
                forget = low + (1.0 - low) * fast_sigmoid(fg_ref[at, :])
                decay, part = tile_scan_up(forget, forget * local)
                out.append(decay[0:1, :] * carry[k] + part[0:1, :])
            return tuple(out)

        ends = lax.fori_loop(0, tiles, one, (jnp.zeros((1, wide), F32),) * slots)
        for k in range(slots):
            end_ref[0, k : k + 1] = ends[k]

    block = by_block(rows, wide)
    return pl.pallas_call(
        body,
        grid=(count,),
        out_shape=shape_of(count, slots, wide),
        in_specs=[
            pl.BlockSpec((rows, wide), lambda b: (b, 1)),
            block,
            block,
            by_block(rows, 1),
            by_block(rows, 1),
            whole_row(wide),
        ],
        out_specs=by_slot(slots, wide),
        compiler_params=params(),
    )(pre, norm, state, r_mix, coef, bound)


def back_states(order, pre, bound, norm, state, g_og, r_mix, coef, head, tail, weights, pos_n, first, count):
    wide = norm.shape[1]
    slots = head.shape[1]
    rows = slots * pos_n
    pairs = pos_n // 16
    depth = weights.shapes[0][1]

    def body(x, held, ins, outs):
        in_ref, fg_ref, bound_ref, norm_ref, state_ref, og_ref, r_ref, coef_ref, head_ref, tail_ref = ins
        gin_ref, gfg_ref, low_ref = outs
        low = bound_ref[...]
        place = lax.broadcasted_iota(jnp.int32, (8, wide), 0)
        low_ref[0] = jnp.zeros((8, wide), F32)

        def half(k, tile, g):
            at = pl.ds(pl.multiple_of(k * pos_n + tile * 8, 8), 8)
            sig_f, forget, act, slope, keep = gates(in_ref[at, :], fg_ref[at, :], low)
            now = state_ref[at, :]
            local = r_ref[at, :] * norm_ref[at, :] - coef_ref[at, :] * now
            decay, part = tile_scan_up(forget, forget * local)
            whole = part + decay * g
            g_state = local + jnp.where(place == 7, g, pltpu.roll(whole, 7, 0))
            last = jnp.maximum(k * pos_n + tile * 8 - 1, 0)
            entry = jnp.where(tile == 0, head_ref[0, k : k + 1], state_ref[pl.ds(last, 1), :])
            before = jnp.where(place == 0, entry, pltpu.roll(now, 1, 0))
            g_forget = g_state * (before - act)
            return g_state * keep * slope, g_forget * keep * sig_f, whole[0:1, :], g_forget * (1.0 - sig_f)

        def one(i, carry):
            pair = pairs - 1 - i
            out, total = [], low_ref[0]
            for k in range(slots):
                in_2, fg_2, g, low_2 = half(k, 2 * pair + 1, carry[k])
                in_1, fg_1, g, low_1 = half(k, 2 * pair, g)
                at = pl.ds(pl.multiple_of(k * pos_n + pair * 16, 16), 16)
                gin_ref[at, :] = jnp.concatenate([in_1, in_2], 0).astype(BF16)
                gfg_ref[at, :] = jnp.concatenate([fg_1, fg_2], 0).astype(BF16)
                total = total + low_1 + low_2
                out.append(g)
            low_ref[0] = total
            return tuple(out)

        lax.fori_loop(0, pairs, one, tuple(tail_ref[0, k : k + 1] for k in range(slots)))
        part = dot_nn(gin_ref[...], held[0][:wide]) + dot_nn(gfg_ref[...], held[0][wide : 2 * wide])
        return (part + dot_nn(og_ref[...], held[0][2 * wide :])).astype(BF16)

    block, edge, one_lane = by_block(rows, wide, first), by_slot(slots, wide, first), by_block(rows, 1, first)
    ins = [
        (pre, block),
        (pre, by_block(rows, wide, first, 1)),
        (bound, whole_row(wide)),
        (norm, block),
        (state, block),
        (g_og, block),
        (r_mix, one_lane),
        (coef, one_lane),
        (head, edge),
        (tail, edge),
    ]
    outs = [(shape_of(count * rows, wide, dtype=BF16), by_block(rows, wide))] * 2
    outs = outs + [(shape_of(count, 8, wide), by_slot(8, wide))]
    return step_kernel(body, order, count, rows, [], weights, ins, outs, depth, 6 * count * rows * wide * depth)


def order_rows(blocks, place):
    count = len(blocks)
    q, width = blocks[0].shape
    tile = 512

    def body(place_ref, *refs):
        out_ref = refs[count]
        for j in range(count):
            at = pl.multiple_of(lax.bitwise_xor(place_ref[0], j) * q, 16)
            out_ref[pl.ds(at, q), :] = refs[j][...].astype(F32)

    return pl.pallas_call(
        body,
        grid=(width // tile,),
        out_shape=shape_of(count * q, width),
        in_specs=[SMEM_SPEC] + [pl.BlockSpec((q, tile), lambda i: (0, i))] * count,
        out_specs=pl.BlockSpec((count * q, tile), lambda i: (0, i)),
        compiler_params=params(),
    )(place, *blocks)


def turn_rows(blocks, place):
    count = len(blocks)
    q, width = blocks[0].shape
    tile = 256

    def body(place_ref, *refs):
        out_ref, held = refs[count], refs[count + 1]
        for j in range(count):
            held[lax.bitwise_xor(place_ref[0], j)] = refs[j][...].astype(F32)
        out_ref[...] = held[...].reshape(count * q, tile).T

    return pl.pallas_call(
        body,
        grid=(width // tile,),
        out_shape=shape_of(width, count * q),
        in_specs=[SMEM_SPEC] + [pl.BlockSpec((q, tile), lambda i: (0, i))] * count,
        out_specs=pl.BlockSpec((tile, count * q), lambda i: (i, 0)),
        scratch_shapes=[pltpu.VMEM((count, q, tile), F32)],
        compiler_params=params(),
    )(place, *blocks)


def dot_nt(a, b):
    return lax.dot_general(a, b, (((1,), (1,)), ((), ())), preferred_element_type=F32)


def dot_nn(a, b):
    return lax.dot_general(a, b, (((1,), (0,)), ((), ())), preferred_element_type=F32)


def dot_tn(a, b):
    return lax.dot_general(a, b, (((0,), (0,)), ((), ())), preferred_element_type=F32)


def on_device(
    net,
    tokens,
    cotangent,
    lengths,
    in_gain,
    w_input,
    w_forget,
    w_output_gate,
    lower_bound,
    mix_gain,
    w_out,
    mlp_gain,
    w_gate,
    w_up,
    w_down,
):
    s, t = net.places()
    n_seq, n_tp = net.seq, net.tp
    slots, group, cols = tokens.shape
    width = cols * n_tp
    pos_n = group // n_tp
    rows = slots * pos_n
    dq = cols // n_seq
    fq = w_down.shape[0] // n_seq
    chan, hid = dq * n_tp, fq * n_tp
    place = s.reshape(1)
    order = net.order

    def quarter_t(w, q):
        return lax.dynamic_slice_in_dim(w, s * q, q, 1).T

    def by_owner(x):
        return x.reshape(slots, n_tp, pos_n, cols).transpose(1, 0, 2, 3).reshape(n_tp, rows, cols)

    def to_owner(x):
        return lax.all_to_all(x, "tp", 0, 0, tiled=True)

    def in_place(x):
        return x.reshape(n_tp, slots, pos_n, cols).transpose(1, 0, 2, 3).reshape(tokens.shape)

    def total(terms):
        return sum(p.astype(F32) for p in terms)

    where = s * group + t * pos_n + jnp.arange(pos_n, dtype=jnp.int32)
    live = (where[None, :] < lengths[:, None]).astype(F32).reshape(rows, 1)

    small = jnp.concatenate(
        [lax.dynamic_slice_in_dim(v, s * dq, dq) for v in (lower_bound, mix_gain)] + [mlp_gain], 0
    )
    terms, rest = [], small
    for _ in range(3):
        terms.append(hold(rest.astype(BF16))[0])
        rest = rest - terms[-1].astype(F32)
    terms = jnp.pad(jnp.concatenate(terms, 0), (0, 16 * cols - 3 * small.shape[0])).reshape(1, 16, cols)
    token_blocks = to_owner(jnp.concatenate([by_owner(tokens), jnp.broadcast_to(terms, (n_tp, 16, cols))], 1))
    small = token_blocks[:, rows:].reshape(n_tp, 16 * cols)[:, : 3 * small.shape[0]].astype(F32).reshape(n_tp, 3, -1)
    small = small[:, 0] + small[:, 1] + small[:, 2]
    bound = small[:, :dq].reshape(1, chan)
    gain = small[:, dq : 2 * dq].reshape(1, chan)
    mlp_full = small[:, 2 * dq :].reshape(1, width)
    mix_w = jnp.concatenate(
        [quarter_t(w, dq) for w in (w_input, w_forget, w_output_gate)]
        + [lax.dynamic_slice_in_dim(w_out, s * dq, dq, 0)],
        0,
    )
    tok, normed_own = norm_tokens(token_blocks, in_gain, rows)
    mix_ring = RingGather(net, after(mix_w, normed_own))
    mix_ring.launch(mix_ring.sends())
    normed = net.gather_rest(net.gather_first(normed_own))
    mix_ring.finish()
    w3, wo = Weights(), Weights()
    w3.add(mix_ring, [(i * dq, i * chan) for i in range(3)], dq, True)
    wo.add(mix_ring, [(3 * dq, 0)], dq, True)
    gate_w = jnp.concatenate([quarter_t(w_gate, fq), quarter_t(w_up, fq)], 0)
    gate_ring = RingGather(net, after(gate_w, *mix_ring.came))
    gate_ring.launch(gate_ring.sends())

    pre, normed_all, decay, end = mixer_in(order, normed, w3, bound, slots, pos_n)

    def spread(pair, reverse):
        def joined(earlier, later):
            return earlier[0] * later[0], later[0] * earlier[1] + later[1]

        whole = pair
        before = (jnp.ones_like(pair[0]), jnp.zeros_like(pair[1]))
        for bit in net.tp_bits:
            moved = net.cross(jnp.stack(whole, 0), bit)
            moved = (moved[0], moved[1])
            upper = (jnp.bitwise_and(t, bit) != 0) != reverse
            ahead, behind = joined(moved, whole), joined(whole, moved)
            longer = joined(moved, before)
            before = tuple(jnp.where(upper, a, b) for a, b in zip(longer, before))
            whole = tuple(jnp.where(upper, a, b) for a, b in zip(ahead, behind))
        return before, whole

    (decay, end), gate_ring.came = hold((decay, end), gate_ring.came)
    head = scan_heads(place, *spread((decay, end), False), False)
    head, sends, cot_sent = hold(head, gate_ring.sends(), by_owner(cotangent))
    gate_ring.launch(sends)
    cot_blocks = to_owner(cot_sent)
    (state, mix, squares), parts = mixer_out(order, pre, bound, gain, head, wo, pos_n)
    parts, sum_all = hold(parts, jnp.sum(squares, -1).reshape(n_seq, rows))
    sum_all = net.total_near(sum_all)
    near, sum_all = hold(net.quad_near(parts), sum_all)
    branch, sum_all = net.quad_far(near), net.total_far(sum_all)
    branch, sum_all, gate_ring.came = hold(branch, sum_all, gate_ring.came)
    gate_ring.launch(gate_ring.sends())
    r_mix = lax.rsqrt(sum_all / width + EPS).reshape(n_seq * rows, 1)
    branch = total(branch)
    resid = tok.astype(F32) + r_mix[:rows] * branch
    r_mlp = lax.rsqrt(jnp.mean(resid * resid, axis=-1, keepdims=True) + EPS)
    scaled = resid * r_mlp
    mlp_own = (scaled * mlp_full).astype(BF16)
    mlp_in = net.gather_first(mlp_own)
    cot = mask_rows(after(cot_blocks, mlp_own), live)
    half = n_seq // 2
    mlp_in, gate_ring.came, cot = hold(mlp_in, gate_ring.came, cot)
    gate_ring.launch(gate_ring.sends())
    gate_ring.finish()
    mlp_in = net.gather_rest(mlp_in)
    grad_out = net.gather_first(cot)
    wgu = Weights()
    wgu.add(gate_ring, [(0, 0)], fq, False)
    wgu.add(gate_ring, [(fq, 0)], fq, False)
    down_w = lax.dynamic_slice_in_dim(w_down, s * fq, fq, 0)
    mlp_in, down_w, _ = hold(mlp_in, down_w, gate_ring.came)

    down_ring = RingGather(net, down_w)
    down_ring.launch(down_ring.sends())
    some = feed_forward(order, mlp_in[:half], wgu, 0, n_seq)
    some, down_ring.came, far_in = hold(some, down_ring.came, mlp_in[half:])
    down_ring.launch(down_ring.sends())
    hidden, slope_up, act, mlp_all = feed_forward(order, far_in, wgu, half, n_seq, some)
    hidden, down_ring.came, grad_out = hold(hidden, down_ring.came, grad_out)
    down_ring.launch(down_ring.sends())
    grad_out = net.gather_rest(grad_out)
    grad_out, hidden, sends = hold(grad_out, hidden, down_ring.sends())
    down_ring.launch(sends)
    down_ring.finish()
    grad_all = jnp.concatenate(grad_out, 0)

    def ring_sum(wholes, canonical, *others):
        def chunk(d):
            out = []
            for w in wholes:
                q = w.shape[0] // n_tp
                if canonical:
                    out.append(lax.dynamic_slice_in_dim(w, net.behind[d] * q, q, 0))
                else:
                    out.append(w[d * q : (d + 1) * q])
            return jnp.concatenate(out, 0) if len(out) > 1 else out[0]

        return RingScatter(net, chunk)

    def to_output(blocks, turned):
        q = blocks[0].shape[0]
        if q % 16 == 0:
            return turn_rows(blocks, place) if turned else order_rows(blocks, place)
        out = jnp.zeros((n_seq, q, width), F32)
        for j in range(n_seq):
            out = lax.dynamic_update_index_in_dim(out, blocks[j].astype(F32), lax.bitwise_xor(s, j), 0)
        out = out.reshape(n_seq * q, width)
        return out.T if turned else out

    dw_down = dot_tn(hidden, grad_all).astype(BF16)
    down_sum = ring_sum([dw_down], False)
    wd = Weights()
    wd.add(down_ring, [(0, 0)], fq, False)
    sends, grad_all, _ = hold(down_sum.sends(), grad_all, down_ring.came)
    down_sum.launch(sends)
    grad_gate, grad_up = back_hidden(order, grad_all, wd, slope_up, act, rows)
    grad_gate, down_sum.came = hold(grad_gate, down_sum.came)
    sends, grad_gate = hold(down_sum.sends(), grad_gate)
    down_sum.launch(sends)
    dw_gate = dot_tn(grad_gate, mlp_all).astype(BF16)
    dw_gate, down_sum.came = hold(dw_gate, down_sum.came)
    sends, grad_up = hold(down_sum.sends(), grad_up)
    down_sum.launch(sends)
    dw_up = dot_tn(grad_up, mlp_all).astype(BF16)
    dw_up, down_sum.came = hold(dw_up, down_sum.came)
    sends, grad_gate = hold(down_sum.sends(), grad_gate)
    down_sum.launch(sends)
    far = back_pair(order, grad_gate, grad_up, wgu, rows, half, half)
    far, down_sum.came = hold(far, down_sum.came)
    near_far = net.quad_far_part(far)
    down_own = down_sum.result()
    gu_sum = ring_sum([dw_gate, dw_up], False)
    near_far, down_own, grad_gate, sends = hold(near_far, down_own, grad_gate, gu_sum.sends())
    gu_sum.launch(sends)
    moved_far = net.swap(near_far, net.bits[-1])
    parts = back_pair(order, grad_gate, grad_up, wgu, rows, 0, half)
    parts, gu_sum.came = hold(parts, gu_sum.came)
    near_own = net.quad_far_part(parts)
    sends, near_own, hidden = hold(gu_sum.sends(), near_own, hidden)
    gu_sum.launch(sends)
    ffn_parts = down_parts(order, hidden, wd, rows)
    moved_far, near_own, ffn_parts = hold(moved_far, near_own, ffn_parts)
    grad_mlp_in = total([near_own, moved_far])

    grad_mlp_gain = jnp.sum(grad_mlp_in * scaled, axis=0)
    grad_scaled = grad_mlp_in * mlp_full
    inner = jnp.sum(resid * grad_scaled, axis=-1, keepdims=True)
    grad_resid = cot.astype(F32) + r_mlp * grad_scaled - resid * r_mlp**3 * inner / width
    branch_own = grad_resid.astype(BF16)
    grad_branch = net.gather_first(branch_own)
    branch_own, gu_sum.came = hold(branch_own, gu_sum.came)
    sends = hold(gu_sum.sends())[0]
    gu_sum.launch(sends)
    down_blocks = net.gather_first(after(down_own, *sends))

    grad_branch, gu_sum.came, down_blocks = hold(grad_branch, gu_sum.came, down_blocks)
    grad_branch, down_blocks = net.gather_rest(grad_branch), net.gather_rest(down_blocks)
    sends, grad_branch = hold(gu_sum.sends(), grad_branch)
    gu_sum.launch(sends)
    g_norm, grad_og, mixed_out, branch_all, inner_lanes, gain_sums = back_mixer(
        order, grad_branch, wo, pre, state, mix, r_mix, gain
    )
    inner = net.total_far(net.total_near(jnp.sum(inner_lanes, -1).reshape(n_seq, rows))).reshape(-1, 1)
    ffn = net.quad_far(net.quad_near([after(p, inner) for p in ffn_parts]))
    coef = r_mix**3 * inner / width
    back_end = back_ends(pre, bound, g_norm, state, r_mix, coef, slots, pos_n)
    dw_out = dot_tn(after(mixed_out, back_end), branch_all).astype(BF16)
    dw_og = dot_tn(after(grad_og, dw_out), normed_all).astype(BF16)
    back_end, gu_sum.came, dw_og = hold(back_end, gu_sum.came, dw_og)
    tail = scan_heads(place, *spread((decay, back_end), True), True)
    gu_own = gu_sum.result()
    mixed = (live * (resid + total(ffn))).astype(BF16)
    mixed_sent = mixed.reshape(rows, n_tp, cols).transpose(1, 0, 2)
    first_sum = ring_sum([dw_out, dw_og], True)
    tail, gu_own, mixed_sent, sends = hold(tail, gu_own, mixed_sent, first_sum.sends())
    first_sum.launch(sends)
    mixed_got = to_owner(mixed_sent)

    def back(start, tail):
        return back_states(
            order, pre, bound, g_norm, state, grad_og, r_mix, coef, head, tail, w3, pos_n, start, half
        )

    (far_in, far_fg, far_low), far = back(half, tail)
    far, far_in, first_sum.came = hold(far, far_in, first_sum.came)
    near_far = net.quad_far_part(far)
    near_far, sends, tail = hold(near_far, first_sum.sends(), tail)
    moved_far = net.swap(near_far, net.bits[-1])
    first_sum.launch(sends)
    (grad_in, grad_fg, low_sums), parts = back(0, tail)
    near_own = net.quad_far_part(parts)
    low_sums = low_sums + far_low
    grad_in, grad_fg = (jnp.concatenate([a, b], 0) for a, b in ((grad_in, far_in), (grad_fg, far_fg)))
    near_own, first_sum.came, grad_in = hold(near_own, first_sum.came, grad_in)
    sends, grad_in = hold(first_sum.sends(), grad_in)
    first_sum.launch(sends)
    dw_in = dot_tn(grad_in, normed_all).astype(BF16)
    dw_fg = dot_tn(after(grad_fg, dw_in), normed_all).astype(BF16)
    last_sum = ring_sum([dw_in, dw_fg], True)
    dw_fg, first_sum.came, last_sends, moved_far = hold(dw_fg, first_sum.came, last_sum.sends(), moved_far)
    first_sum.launch(first_sum.sends())
    last_sum.launch(last_sends)
    moved = [near_own, moved_far]
    gu_blocks = net.gather_first(after(gu_own, moved_far))
    grad_w_down = to_output(down_blocks, False)

    grad_normed = total(moved)
    x = tok.astype(F32)
    r_in = lax.rsqrt(jnp.mean(x * x, axis=-1, keepdims=True) + EPS)
    grad_in_gain = jnp.sum(grad_normed * x * r_in, axis=0)
    scaled_g = grad_normed * in_gain
    inner = jnp.sum(x * scaled_g, axis=-1, keepdims=True)
    grad_tok = grad_resid + r_in * scaled_g - x * r_in**3 * inner / width

    gains = jnp.stack([grad_in_gain, grad_mlp_gain], 0)
    high = hold(gains.astype(BF16))[0]
    low = (gains - high.astype(F32)).astype(BF16)
    extra = jnp.concatenate([high, low, jnp.zeros((12, width), BF16)], 0)
    sent = jnp.concatenate([grad_tok.astype(BF16), extra], 0).reshape(-1, n_tp, cols).transpose(1, 0, 2)
    sent, first_sum.came, last_sum.came = hold(sent, first_sum.came, last_sum.came)
    got = to_owner(sent)
    first_own = first_sum.result()
    last_own = last_sum.result()
    first_blocks = net.gather_rest(net.gather_first(first_own))
    gu_blocks = net.gather_rest(gu_blocks)
    last_blocks = net.gather_rest(net.gather_first(last_own))
    grad_w_gate = to_output([b[:fq] for b in gu_blocks], False).T
    grad_w_up = to_output([b[fq:] for b in gu_blocks], False).T
    grad_w_out = to_output([b[:dq] for b in first_blocks], False)
    grad_w_og = to_output([b[dq:] for b in first_blocks], True)
    grad_w_in = to_output([b[:dq] for b in last_blocks], True)
    grad_w_fg = to_output([b[dq:] for b in last_blocks], True)
    mine = jnp.sum(got[:, rows : rows + 4].astype(F32), 0)
    mine = mine[:2] + mine[2:]
    sums = jnp.stack([jnp.sum(low_sums, axis=(0, 1)), jnp.sum(gain_sums, axis=(0, 1))], 0).reshape(2, n_tp, dq)
    for bit in reversed(net.tp_bits):
        sums = sums.reshape(2, 2, bit, dq)
        upper = jnp.bitwise_and(t, bit) != 0
        keep = jnp.where(upper, sums[:, 1], sums[:, 0])
        send = jnp.where(upper, sums[:, 0], sums[:, 1])
        sums = keep + net.cross(send, bit)
    chans = sums.reshape(1, 2, dq)
    for bit in net.bits:
        chans = jnp.concatenate([chans, net.swap(chans, bit)], 0)
        mine = mine + net.swap(mine, bit)
    chans = chans[lax.bitwise_xor(s, jnp.arange(n_seq, dtype=jnp.int32))]
    return (
        in_place(mixed_got),
        in_place(got[:, :rows]).astype(F32),
        mine[0],
        grad_w_in,
        grad_w_fg,
        grad_w_og,
        chans[:, 0].reshape(-1),
        chans[:, 1].reshape(-1),
        grad_w_out,
        mine[1],
        grad_w_gate,
        grad_w_up,
        grad_w_down,
    )


def solution(mesh):
    return jax.shard_map(
        functools.partial(on_device, Net(mesh)),
        mesh=mesh,
        in_specs=(
            P(None, "seq", "tp"),
            P(None, "seq", "tp"),
            P(),
            P(),
            P(None, "tp"),
            P(None, "tp"),
            P(None, "tp"),
            P("tp"),
            P("tp"),
            P("tp", None),
            P("tp"),
            P(None, "tp"),
            P(None, "tp"),
            P("tp", None),
        ),
        out_specs=(
            P(None, "seq", "tp"),
            P(None, "seq", "tp"),
            P("tp"),
            P(None, "tp"),
            P(None, "tp"),
            P(None, "tp"),
            P("tp"),
            P("tp"),
            P("tp", None),
            P("tp"),
            P(None, "tp"),
            P(None, "tp"),
            P("tp", None),
        ),
        check_vma=False,
    )
```

```python
import functools

import jax
import jax.numpy as jnp
import numpy as np
from jax import lax
from jax.experimental import pallas as pl
from jax.experimental.pallas import tpu as pltpu
from jax.sharding import PartitionSpec as P

EPS = 1e-06
F32, BF16 = jnp.float32, jnp.bfloat16
VMEM_LIMIT = 56 * 1024 * 1024
NO_COST = pl.CostEstimate(flops=1, bytes_accessed=1, transcendentals=0)
LONG = pl.CostEstimate(flops=10**12, bytes_accessed=10**9, transcendentals=0)


def params(**more):
    return pltpu.CompilerParams(vmem_limit_bytes=VMEM_LIMIT, **more)


def sigmoid(v):
    return 1.0 / (1.0 + jnp.exp(-v))


def fast_sigmoid(v):
    d = 1.0 + jnp.exp(jnp.minimum(-v, 80.0))
    r = pl.reciprocal(d, approx=True)
    return r * (2.0 - d * r)


def ring_of(mesh):
    count = mesh.shape["tp"]
    try:
        coords = [tuple(d.coords) for d in mesh.devices[0]]
        ys = len({c[1] for c in coords})
    except (AttributeError, TypeError):
        ys = 2 if count % 2 == 0 else 1
    zs = count // ys
    if zs * ys != count or zs % 2 or ys < 2:
        return list(range(count))
    cycle = [(z, 0) for z in range(zs)]
    for turn, z in enumerate(reversed(range(zs))):
        across = range(1, ys) if turn % 2 == 0 else reversed(range(1, ys))
        cycle += [(z, y) for y in across]
    return [z * ys + y for z, y in cycle]


class Net:
    def __init__(self, mesh):
        self.seq, self.tp = mesh.shape["seq"], mesh.shape["tp"]
        self.cycle = ring_of(mesh)
        self.bits = [1 << b for b in range(self.seq.bit_length() - 1)]
        self.tp_bits = [1 << b for b in range(self.tp.bit_length() - 1)]

    def places(self):
        s, t = lax.axis_index("seq"), lax.axis_index("tp")
        where = np.zeros(self.tp, np.int32)
        for i, index in enumerate(self.cycle):
            where[index] = i
        pos = jnp.asarray(where)[t]
        steps = [[self.cycle[(i - d) % self.tp] for d in range(self.tp)] for i in where]
        self.order = lax.dynamic_index_in_dim(jnp.asarray(np.array(steps, np.int32)), t, 0, False)
        self.behind = [self.order[d] for d in range(self.tp)]
        self.inverse = (pos - jnp.asarray(where)) % self.tp
        return s, t

    def shift(self, x, k):
        n = self.tp
        return lax.ppermute(x, "tp", [(self.cycle[i], self.cycle[(i + k) % n]) for i in range(n)])

    def cross(self, x, bit):
        return lax.ppermute(x, "tp", [(i, i ^ bit) for i in range(self.tp)])

    def swap(self, x, bit):
        return lax.ppermute(x, "seq", [(i, i ^ bit) for i in range(self.seq)])

    def halves(self, size):
        half = size // 2
        return half // 16 * 16 if size >= 32 else half

    def gather_first(self, x):
        out = [x] + [None] * (self.seq - 1)
        for bit in reversed(self.bits):
            out[bit] = self.swap(x, bit)
        return out

    def gather_rest(self, out, end=None):
        out = list(out)
        for j in range(end or self.seq):
            if out[j] is None:
                out[j] = self.swap(out[j & (j - 1)], j & -j)
        return out

    def gather_near(self, x):
        out = [x]
        for bit in self.bits[:-1]:
            out = out + [self.swap(y, bit) for y in out]
        return out

    def halved(self, x):
        half = x.shape[0] // 2
        return [x[:half], x[half:]]

    def quad_far_part(self, parts):
        parts = list(parts)
        for bit in self.bits[:-1]:
            for j in reversed(range(0, len(parts), 2 * bit)):
                moved = self.swap(parts[j ^ bit], bit)
                parts[j] = (parts[j].astype(F32) + moved.astype(F32)).astype(BF16)
        return parts[0]

    def quad_near(self, parts):
        half = self.seq // 2
        far = self.quad_far_part(parts[half:])
        return [self.quad_far_part(parts[:half]), far]

    def quad_far(self, near):
        return [near[0], self.swap(near[1], self.bits[-1])]

    def total_step(self, x, bit):
        moved = self.swap(x, bit)
        return x + jnp.stack([moved[j ^ bit] for j in range(self.seq)], 0)

    def total_near(self, x):
        for bit in self.bits[:-1]:
            x = self.total_step(x, bit)
        return x

    def total_far(self, x):
        return self.total_step(x, self.bits[-1])


def after(x, *others):
    return lax.optimization_barrier((x,) + others)[0]


def hold(*trees):
    return lax.optimization_barrier(trees)


class RingGather:
    def __init__(self, net, x):
        self.net, self.size = net, x.shape[0]
        n = net.tp
        self.blocks = [[(x, 0)]] + [None] * (n - 1)
        self.full = (n - 1) // 2
        self.made = 0
        self.came = (x, x)

    def done(self):
        return self.made == self.net.tp // 2

    def sends(self):
        if self.done():
            return ()
        fore, back = self.came
        if self.made < self.full:
            return fore, back
        half = self.net.halves(self.size)
        return fore[:half], back[half:]

    def launch(self, sends):
        if self.done():
            return
        net, n = self.net, self.net.tp
        self.made += 1
        d = self.made
        self.came = net.shift(sends[0], 1), net.shift(sends[1], -1)
        if d <= self.full:
            self.blocks[d], self.blocks[n - d] = [(self.came[0], 0)], [(self.came[1], 0)]
        else:
            self.blocks[d] = [(self.came[0], 0), (self.came[1], net.halves(self.size))]

    def finish(self):
        while not self.done():
            self.launch(self.sends())

    def rows(self, start, q):
        out = []
        for block in self.blocks:
            whole = jnp.concatenate([a for a, _ in block], 0) if len(block) > 1 else block[0][0]
            out.append(whole[start : start + q])
        return out


class RingScatter:
    def __init__(self, net, wholes, canonical):
        self.net, self.wholes, self.canonical = net, wholes, canonical
        self.sizes = [w.shape[0] // net.tp for w in wholes]
        self.size = sum(self.sizes)
        self.d = net.tp // 2
        self.came = ()
        self.half = net.halves(self.size) if net.tp % 2 == 0 else 0

    def done(self):
        return self.d == 0

    def make(self, outs):
        net = self.net
        made = []
        for d, low, high, adds in outs:
            rows = []
            for w, q in zip(self.wholes, self.sizes):
                at = net.behind[d] * q if self.canonical else d * q
                rows.append(lax.dynamic_slice_in_dim(w, at, q, 0))
            whole = jnp.concatenate(rows, 0)[low:high]
            for part, start in adds:
                first = start - low
                part = jnp.pad(part.astype(F32), ((first, high - low - first - part.shape[0]), (0, 0)))
                whole = whole.astype(F32) + part
            made.append(whole.astype(BF16))
        return made

    def adds(self, which):
        if not self.came:
            return []
        after_half = which == 1 and 2 * (self.d + 1) == self.net.tp
        return [(self.came[which], self.half if after_half else 0)]

    def sends(self):
        if self.done():
            return ()
        n, d = self.net.tp, self.d
        if 2 * d == n:
            return self.make([(d, 0, self.half, []), (d, self.half, self.size, [])])
        return self.make([(n - d, 0, self.size, self.adds(0)), (d, 0, self.size, self.adds(1))])

    def launch(self, sends):
        if self.done():
            return
        self.d -= 1
        self.came = self.net.shift(sends[0], 1), self.net.shift(sends[1], -1)

    def result(self):
        while not self.done():
            self.launch(self.sends())
        return self.make([(0, 0, self.size, self.adds(0) + self.adds(1))])[0]


SMEM_SPEC = pl.BlockSpec(memory_space=pltpu.SMEM)
VMEM_SPEC = pl.BlockSpec(memory_space=pltpu.VMEM)


def norm_tokens(blocks, gain, rows):
    count, _, cols = blocks.shape
    width = count * cols

    def body(gain_ref, in_ref, x_ref, n_ref):
        total = jnp.zeros((rows, 1), F32)
        for k in range(count):
            c = in_ref[k, :rows].astype(F32)
            total += jnp.sum(c * c, axis=-1, keepdims=True)
        r = lax.rsqrt(total / width + EPS)
        for k in range(count):
            c = in_ref[k, :rows]
            at = slice(k * cols, (k + 1) * cols)
            x_ref[:, at] = c
            n_ref[:, at] = (c.astype(F32) * r * gain_ref[:, at]).astype(BF16)

    return pl.pallas_call(
        body,
        out_shape=[jax.ShapeDtypeStruct((rows, width), BF16)] * 2,
        in_specs=[VMEM_SPEC] * 2,
        out_specs=[VMEM_SPEC] * 2,
        compiler_params=params(),
        cost_estimate=NO_COST,
    )(gain.reshape(1, width), blocks)


def mask_rows(blocks, live):
    count, rows, cols = blocks.shape
    width = count * cols

    def body(live_ref, in_ref, x_ref):
        for k in range(count):
            at = slice(k * cols, (k + 1) * cols)
            x_ref[:, at] = (in_ref[k].astype(F32) * live_ref[...]).astype(BF16)

    return pl.pallas_call(
        body,
        out_shape=jax.ShapeDtypeStruct((rows, width), BF16),
        in_specs=[VMEM_SPEC] * 2,
        out_specs=VMEM_SPEC,
        compiler_params=params(),
        cost_estimate=NO_COST,
    )(live, blocks)


def tile_scan(decay, drive):
    place = lax.broadcasted_iota(jnp.int32, decay.shape, 0)
    for step in (1, 2, 4):
        inside = place >= step
        before_decay = jnp.where(inside, pltpu.roll(decay, step, 0), 1.0)
        before_drive = jnp.where(inside, pltpu.roll(drive, step, 0), 0.0)
        drive = drive + decay * before_drive
        decay = decay * before_decay
    return decay, drive


def tile_scan_up(decay, drive):
    place = lax.broadcasted_iota(jnp.int32, decay.shape, 0)
    for step in (1, 2, 4):
        inside = place < 8 - step
        before_decay = jnp.where(inside, pltpu.roll(decay, 8 - step, 0), 1.0)
        before_drive = jnp.where(inside, pltpu.roll(drive, 8 - step, 0), 0.0)
        drive = drive + decay * before_drive
        decay = decay * before_decay
    return decay, drive


def gates(pre_in, pre_fg, bound):
    sig_f = fast_sigmoid(pre_fg)
    forget = bound + (1.0 - bound) * sig_f
    sig_in = fast_sigmoid(pre_in)
    act_in = pre_in * sig_in
    slope_in = sig_in * (1.0 + pre_in * (1.0 - sig_in))
    keep = (1.0 - bound) * (1.0 - sig_f)
    return sig_f, forget, act_in, slope_in, keep


class Weights:
    def __init__(self):
        self.arrays, self.takes, self.shapes = [], [], []

    def add(self, ring, parts, stride, canonical):
        held, n = len(self.shapes), ring.net.tp
        width = ring.blocks[0][0][0].shape[1]
        self.shapes.append((len(parts) * n * stride, width))
        if stride % 16:
            for start, at in parts:
                rows = ring.rows(start, stride)
                whole = jnp.stack(rows, 0)
                if canonical:
                    whole = whole[ring.net.inverse]
                self.takes.append((len(self.arrays), 0, n * stride, held, None, at))
                self.arrays.append(whole.reshape(n * stride, width))
            return
        seen = {id(a): i for i, a in enumerate(self.arrays)}
        for d, block in enumerate(ring.blocks):
            for array, first in block:
                if id(array) not in seen:
                    seen[id(array)] = len(self.arrays)
                    self.arrays.append(array)
                for start, at in parts:
                    low, high = max(start, first), min(start + stride, first + array.shape[0])
                    if low < high:
                        place = (d, stride) if canonical else None
                        row = at + (low - start) + (0 if canonical else d * stride)
                        self.takes.append((seen[id(array)], low - first, high - low, held, place, row))

    def copies(self, order_ref, refs, held, sems):
        out = []
        for k, (source, first, size, to, place, row) in enumerate(self.takes):
            if place is not None:
                row = pl.multiple_of(order_ref[place[0]] * place[1] + row, 16)
            out.append(
                pltpu.make_async_copy(refs[source].at[pl.ds(first, size)], held[to].at[pl.ds(row, size)], sems.at[k])
            )
        return out


def step_kernel(body, order, count, rows, blocks, weights, ins, outs, width, onto=(), long=True):
    any_spec = pl.BlockSpec(memory_space=pl.ANY)
    pieces = [(j, i, sum(a.shape[0] for a in block[:i]), a) for j, block in enumerate(blocks) for i, a in enumerate(block)]
    n_x, n_w, n_in, n_out = len(pieces), len(weights.arrays), len(ins), len(outs)
    n_part = count if width else 0
    n_held, n_onto = len(weights.shapes), len(onto)

    def kernel(order_ref, *refs):
        refs = list(refs)

        def take(k):
            out = refs[:k]
            del refs[:k]
            return out

        x_refs, w_refs, in_refs, _ = take(n_x), take(n_w), take(n_in), take(n_onto)
        out_refs, part_refs = take(n_out), take(n_part)
        held, w_sems = take(n_held), take(1)[0]
        xs, x_sems = take(2) if n_x else (None, None)
        kept, part_sems = take(2) if n_part else (None, None)
        j = pl.program_id(0)
        loads = weights.copies(order_ref, w_refs, held, w_sems)
        x_loads = [
            pltpu.make_async_copy(x_refs[k], xs.at[at, pl.ds(start, a.shape[0])], x_sems.at[k])
            for k, (at, _, start, a) in enumerate(pieces)
        ]

        @pl.when(j == 0)
        def _():
            for load in loads + x_loads:
                load.start()
            for load in loads:
                load.wait()

        for k in range(n_x):

            @pl.when(j == pieces[k][0])
            def _(k=k):
                x_loads[k].wait()

        x = xs[j] if n_x else None
        part = body(x, held, in_refs, out_refs)
        stores = [pltpu.make_async_copy(kept.at[k % 2], part_refs[k], part_sems.at[k]) for k in range(n_part)]
        for k in range(n_part):

            @pl.when(j == k)
            def _(k=k):
                if k >= 2:
                    stores[k - 2].wait()
                kept[k % 2] = part
                stores[k].start()
                if k == n_part - 1:
                    for store in stores[max(k - 1, 0) :]:
                        store.wait()

    scratch = [pltpu.VMEM(shape, BF16) for shape in weights.shapes]
    scratch.append(pltpu.SemaphoreType.DMA((max(len(weights.takes), 1),)))
    if n_x:
        scratch += [pltpu.VMEM((len(blocks), rows, pieces[0][3].shape[1]), BF16), pltpu.SemaphoreType.DMA((n_x,))]
    if n_part:
        scratch += [pltpu.VMEM((2, rows, width), BF16), pltpu.SemaphoreType.DMA((n_part,))]
    out = pl.pallas_call(
        kernel,
        grid=(count,),
        out_shape=[shape for shape, _ in outs] + [jax.ShapeDtypeStruct((rows, width), BF16)] * n_part,
        in_specs=[SMEM_SPEC] + [any_spec] * (n_x + n_w) + [spec for _, spec in ins] + [any_spec] * n_onto,
        out_specs=[spec for _, spec in outs] + [any_spec] * n_part,
        input_output_aliases={1 + n_x + n_w + n_in + i: i for i in range(n_onto)},
        scratch_shapes=scratch,
        compiler_params=params(),
        cost_estimate=LONG if long else NO_COST,
    )(order, *[a for _, _, _, a in pieces], *weights.arrays, *[a for a, _ in ins], *onto)
    return list(out[:n_out]), list(out[n_out:])


def shape_of(*shape, dtype=F32):
    return jax.ShapeDtypeStruct(shape, dtype)


def by_block(rows, wide, first=0, column=0):
    return pl.BlockSpec((rows, wide), lambda b: (b + first, column))


def whole_row(wide):
    return pl.BlockSpec((1, wide), lambda b: (0, 0))


def by_slot(slots, wide, first=0):
    return pl.BlockSpec((1, slots, wide), lambda b: (b + first, 0, 0))


def columns(wide):
    return [slice(c, min(c + 256, wide)) for c in range(0, wide, 256)]


def mixer_in(order, blocks, weights, bound, slots, pos_n):
    count, (rows, depth), wide = len(blocks), blocks[0].shape, bound.shape[1]

    def body(x, held, ins, outs):
        pre_ref, all_ref, decay_ref, end_ref = outs
        low = ins[0][...]
        all_ref[...] = x
        pre_ref[...] = dot_nt(x, held[0][...])

        def one(i, carry):
            out = []
            for k in range(slots):
                at = pl.ds(pl.multiple_of(k * pos_n + i * 8, 8), 8)
                _, forget, act, _, keep = gates(pre_ref[at, :wide], pre_ref[at, wide : 2 * wide], low)
                decay, local = tile_scan(forget, act * keep)
                a, h = carry[k]
                out.append((a * decay[7:8, :], decay[7:8, :] * h + local[7:8, :]))
            return tuple(out)

        start = (jnp.ones((1, wide), F32), jnp.zeros((1, wide), F32))
        ends = lax.fori_loop(0, pos_n // 8, one, (start,) * slots)
        for k in range(slots):
            decay_ref[0, k : k + 1] = ends[k][0]
            end_ref[0, k : k + 1] = ends[k][1]

    outs = [
        (shape_of(count * rows, 3 * wide), by_block(rows, 3 * wide)),
        (shape_of(count * rows, depth, dtype=BF16), by_block(rows, depth)),
        (shape_of(count, slots, wide), by_slot(slots, wide)),
        (shape_of(count, slots, wide), by_slot(slots, wide)),
    ]
    return step_kernel(
        body, order, count, rows, [[x] for x in blocks], weights, [(bound, whole_row(wide))], outs, 0
    )[0]


def scan_heads(place, before, whole, reverse):
    count, slots, wide = whole[0].shape

    def body(place_ref, pa_ref, pb_ref, wa_ref, wb_ref, head_ref):
        state = jnp.zeros((slots, wide), F32)
        for i in range(count):
            j = lax.bitwise_xor(place_ref[0], count - 1 - i if reverse else i)
            head_ref[j] = pa_ref[j] * state + pb_ref[j]
            state = wa_ref[j] * state + wb_ref[j]

    return pl.pallas_call(
        body,
        out_shape=shape_of(count, slots, wide),
        in_specs=[SMEM_SPEC] + [VMEM_SPEC] * 4,
        out_specs=VMEM_SPEC,
        compiler_params=params(),
        cost_estimate=NO_COST,
    )(place, *before, *whole)


def mixer_out(order, pre, bound, gain, head, weights, pos_n, first, steps, onto=(), long=True):
    wide = bound.shape[1]
    count, slots, _ = head.shape
    rows = slots * pos_n
    depth = weights.shapes[0][1]

    def body(x, held, ins, outs):
        pre_ref, bound_ref, gain_ref, head_ref = ins
        state_ref, mix_ref, sum_ref = outs
        low = bound_ref[...]

        def one(i, carry):
            out = []
            for k in range(slots):
                at = pl.ds(pl.multiple_of(k * pos_n + i * 8, 8), 8)
                _, forget, act, _, keep = gates(pre_ref[at, :wide], pre_ref[at, wide : 2 * wide], low)
                decay, local = tile_scan(forget, act * keep)
                state = local + decay * carry[k]
                state_ref[at, :] = state
                square = state * state
                sum_ref[at, :] = sum(square[:, c : c + 128] for c in range(0, wide, 128))
                out.append(state[7:8, :])
            return tuple(out)

        lax.fori_loop(0, pos_n // 8, one, tuple(head_ref[0, k : k + 1] for k in range(slots)))
        og = pre_ref[:, 2 * wide :]
        mix = (state_ref[...] * gain_ref[...] * (og * fast_sigmoid(og))).astype(BF16)
        mix_ref[...] = mix
        return dot_nn(mix, held[0][...]).astype(BF16)

    ins = [
        (pre, by_block(rows, 3 * wide, first)),
        (bound, whole_row(wide)),
        (gain, whole_row(wide)),
        (head, by_slot(slots, wide, first)),
    ]
    outs = [
        (shape_of(count * rows, wide), by_block(rows, wide, first)),
        (shape_of(count * rows, wide, dtype=BF16), by_block(rows, wide, first)),
        (shape_of(count * rows, 128), by_block(rows, 128, first)),
    ]
    return step_kernel(body, order, steps, rows, [], weights, ins, outs, depth, onto, long)


def feed_forward(order, blocks, weights, first, count, onto=(), long=True):
    (rows, depth), wide = blocks[0].shape, weights.shapes[0][0]

    def body(x, held, ins, outs):
        hid_ref, slope_ref, act_ref, all_ref = outs
        all_ref[...] = x
        for at in columns(wide):
            gate = dot_nt(x, held[0][at, :])
            up = dot_nt(x, held[1][at, :])
            sig = fast_sigmoid(gate)
            act = gate * sig
            hid_ref[:, at] = (act * up).astype(BF16)
            slope_ref[:, at] = (up * (sig * (1.0 + gate * (1.0 - sig)))).astype(BF16)
            act_ref[:, at] = act.astype(BF16)

    outs = [(shape_of(count * rows, wide, dtype=BF16), by_block(rows, wide, first))] * 3
    outs = outs + [(shape_of(count * rows, depth, dtype=BF16), by_block(rows, depth, first))]
    return step_kernel(body, order, len(blocks), rows, [[x] for x in blocks], weights, [], outs, 0, onto, long)[0]


def down_parts(order, hidden, weights, rows):
    wide, depth = weights.shapes[0]
    count = hidden.shape[0] // rows

    def body(x, held, ins, outs):
        return dot_nn(ins[0][...], held[0][...]).astype(BF16)

    return step_kernel(
        body, order, count, rows, [], weights, [(hidden, by_block(rows, wide))], [], depth
    )[1]


def back_hidden(order, g, weights, slope, act, rows):
    wide, depth = weights.shapes[0]
    count = g.shape[0] // rows

    def body(x, held, ins, outs):
        g_ref, slope_ref, act_ref = ins
        for at in columns(wide):
            hid = dot_nt(g_ref[...], held[0][at, :])
            outs[0][:, at] = (hid * slope_ref[:, at].astype(F32)).astype(BF16)
            outs[1][:, at] = (hid * act_ref[:, at].astype(F32)).astype(BF16)

    block = by_block(rows, wide)
    ins = [(g, by_block(rows, depth)), (slope, block), (act, block)]
    outs = [(shape_of(count * rows, wide, dtype=BF16), block)] * 2
    return step_kernel(body, order, count, rows, [], weights, ins, outs, 0)[0]


def back_pair(order, a, b, weights, rows, first, count):
    wide, depth = weights.shapes[0]

    def body(x, held, ins, outs):
        return (dot_nn(ins[0][...], held[0][...]) + dot_nn(ins[1][...], held[1][...])).astype(BF16)

    block = by_block(rows, wide, first)
    return step_kernel(
        body, order, count, rows, [], weights, [(a, block), (b, block)], [], depth
    )[1]


def back_mixer(order, blocks, rows, weights, pre, state, mix, r_mix, gain):
    count, depth, wide = len(blocks), blocks[0][0].shape[1], gain.shape[1]

    def body(x, held, ins, outs):
        og_ref, state_ref, mix_ref, r_ref, gain_ref = ins
        norm_ref, og_out, mix_out, all_ref, inner_ref, sum_ref = outs
        all_ref[...] = x
        mix_out[...] = (mix_ref[...].astype(F32) * r_ref[...]).astype(BF16)
        g = dot_nt(x, held[0][...])
        og, state = og_ref[...], state_ref[...]
        sig = fast_sigmoid(og)
        act = og * sig
        g_state = g * (state * r_ref[...])
        sum_ref[0] = jnp.sum((g_state * act).reshape(rows // 8, 8, wide), 0)
        og_out[...] = (g_state * gain_ref[...] * (sig * (1.0 + og * (1.0 - sig)))).astype(BF16)
        norm = g * gain_ref[...] * act
        norm_ref[...] = norm
        inner = state * norm
        inner_ref[...] = sum(inner[:, c : c + 128] for c in range(0, wide, 128))

    ins = [
        (pre, pl.BlockSpec((rows, wide), lambda b: (b, 2))),
        (state, by_block(rows, wide)),
        (mix, by_block(rows, wide)),
        (r_mix, by_block(rows, 1)),
        (gain, whole_row(wide)),
    ]
    outs = [
        (shape_of(count * rows, wide), by_block(rows, wide)),
        (shape_of(count * rows, wide, dtype=BF16), by_block(rows, wide)),
        (shape_of(count * rows, wide, dtype=BF16), by_block(rows, wide)),
        (shape_of(count * rows, depth, dtype=BF16), by_block(rows, depth)),
        (shape_of(count * rows, 128), by_block(rows, 128)),
        (shape_of(count, 8, wide), by_slot(8, wide)),
    ]
    return step_kernel(body, order, count, rows, blocks, weights, ins, outs, 0)[0]


def back_ends(pre, bound, norm, state, r_mix, coef, slots, pos_n):
    wide = norm.shape[1]
    rows = slots * pos_n
    count = norm.shape[0] // rows
    tiles = pos_n // 8

    def body(fg_ref, norm_ref, state_ref, r_ref, coef_ref, bound_ref, end_ref):
        low = bound_ref[...]

        def one(i, carry):
            out = []
            for k in range(slots):
                at = pl.ds(pl.multiple_of(k * pos_n + (tiles - 1 - i) * 8, 8), 8)
                local = r_ref[at, :] * norm_ref[at, :] - coef_ref[at, :] * state_ref[at, :]
                forget = low + (1.0 - low) * fast_sigmoid(fg_ref[at, :])
                decay, part = tile_scan_up(forget, forget * local)
                out.append(decay[0:1, :] * carry[k] + part[0:1, :])
            return tuple(out)

        ends = lax.fori_loop(0, tiles, one, (jnp.zeros((1, wide), F32),) * slots)
        for k in range(slots):
            end_ref[0, k : k + 1] = ends[k]

    block = by_block(rows, wide)
    return pl.pallas_call(
        body,
        grid=(count,),
        out_shape=shape_of(count, slots, wide),
        in_specs=[
            pl.BlockSpec((rows, wide), lambda b: (b, 1)),
            block,
            block,
            by_block(rows, 1),
            by_block(rows, 1),
            whole_row(wide),
        ],
        out_specs=by_slot(slots, wide),
        compiler_params=params(),
        cost_estimate=NO_COST,
    )(pre, norm, state, r_mix, coef, bound)


def back_states(order, pre, bound, norm, state, g_og, r_mix, coef, head, tail, weights, pos_n, first, count, long=True):
    wide = norm.shape[1]
    slots = head.shape[1]
    rows = slots * pos_n
    pairs = pos_n // 16
    depth = weights.shapes[0][1]

    def body(x, held, ins, outs):
        in_ref, fg_ref, bound_ref, norm_ref, state_ref, og_ref, r_ref, coef_ref, head_ref, tail_ref = ins
        gin_ref, gfg_ref, low_ref = outs
        low = bound_ref[...]
        place = lax.broadcasted_iota(jnp.int32, (8, wide), 0)
        low_ref[0] = jnp.zeros((8, wide), F32)

        def half(k, tile, g):
            at = pl.ds(pl.multiple_of(k * pos_n + tile * 8, 8), 8)
            sig_f, forget, act, slope, keep = gates(in_ref[at, :], fg_ref[at, :], low)
            now = state_ref[at, :]
            local = r_ref[at, :] * norm_ref[at, :] - coef_ref[at, :] * now
            decay, part = tile_scan_up(forget, forget * local)
            whole = part + decay * g
            g_state = local + jnp.where(place == 7, g, pltpu.roll(whole, 7, 0))
            last = jnp.maximum(k * pos_n + tile * 8 - 1, 0)
            entry = jnp.where(tile == 0, head_ref[0, k : k + 1], state_ref[pl.ds(last, 1), :])
            before = jnp.where(place == 0, entry, pltpu.roll(now, 1, 0))
            g_forget = g_state * (before - act)
            return g_state * keep * slope, g_forget * keep * sig_f, whole[0:1, :], g_forget * (1.0 - sig_f)

        def one(i, carry):
            pair = pairs - 1 - i
            out, total = [], low_ref[0]
            for k in range(slots):
                in_2, fg_2, g, low_2 = half(k, 2 * pair + 1, carry[k])
                in_1, fg_1, g, low_1 = half(k, 2 * pair, g)
                at = pl.ds(pl.multiple_of(k * pos_n + pair * 16, 16), 16)
                gin_ref[at, :] = jnp.concatenate([in_1, in_2], 0).astype(BF16)
                gfg_ref[at, :] = jnp.concatenate([fg_1, fg_2], 0).astype(BF16)
                total = total + low_1 + low_2
                out.append(g)
            low_ref[0] = total
            return tuple(out)

        lax.fori_loop(0, pairs, one, tuple(tail_ref[0, k : k + 1] for k in range(slots)))
        part = dot_nn(gin_ref[...], held[0][:wide]) + dot_nn(gfg_ref[...], held[0][wide : 2 * wide])
        return (part + dot_nn(og_ref[...], held[0][2 * wide :])).astype(BF16)

    block, edge, one_lane = by_block(rows, wide, first), by_slot(slots, wide, first), by_block(rows, 1, first)
    ins = [
        (pre, block),
        (pre, by_block(rows, wide, first, 1)),
        (bound, whole_row(wide)),
        (norm, block),
        (state, block),
        (g_og, block),
        (r_mix, one_lane),
        (coef, one_lane),
        (head, edge),
        (tail, edge),
    ]
    outs = [(shape_of(count * rows, wide, dtype=BF16), by_block(rows, wide))] * 2
    outs = outs + [(shape_of(count, 8, wide), by_slot(8, wide))]
    return step_kernel(body, order, count, rows, [], weights, ins, outs, depth, (), long)


def joined(refs):
    return jnp.concatenate([r[...].astype(F32) for r in refs], 0)


def whole_kernel(body, outs, *arrays):
    return pl.pallas_call(
        body,
        out_shape=outs,
        in_specs=[VMEM_SPEC] * len(arrays),
        out_specs=[VMEM_SPEC] * len(outs),
        compiler_params=params(),
        cost_estimate=NO_COST,
    )(*arrays)


def residual(near, moved, tok, r_mix, gain):
    rows, width = tok.shape

    def body(near_ref, moved_ref, tok_ref, r_ref, gain_ref, resid_ref, out_ref):
        branch = near_ref[...].astype(F32) + moved_ref[...].astype(F32)
        resid = tok_ref[...].astype(F32) + r_ref[...] * branch
        resid_ref[...] = resid
        r = lax.rsqrt(jnp.sum(resid * resid, axis=-1, keepdims=True) / width + EPS)
        out_ref[...] = (resid * r * gain_ref[...]).astype(BF16)

    outs = [shape_of(rows, width), shape_of(rows, width, dtype=BF16)]
    return whole_kernel(body, outs, near, moved, tok, r_mix, gain)


def back_residual(near, moved, resid, cot, gain):
    rows, width = resid.shape

    def body(near_ref, first_ref, second_ref, resid_ref, cot_ref, gain_ref, grad_ref, out_ref, sum_ref):
        g = near_ref[...].astype(F32) + joined((first_ref, second_ref))
        resid = resid_ref[...]
        r = lax.rsqrt(jnp.sum(resid * resid, axis=-1, keepdims=True) / width + EPS)
        scaled = resid * r
        sum_ref[...] = jnp.sum(g * scaled, axis=0, keepdims=True)
        g = g * gain_ref[...]
        inner = jnp.sum(resid * g, axis=-1, keepdims=True)
        grad = cot_ref[...].astype(F32) + r * g - resid * (r * r * r * inner / width)
        grad_ref[...] = grad
        out_ref[...] = grad.astype(BF16)

    outs = [shape_of(rows, width), shape_of(rows, width, dtype=BF16), shape_of(1, width)]
    return whole_kernel(body, outs, near, *moved, resid, cot, gain)


def block_output(near, moved, resid, live, count):
    rows, width = resid.shape
    cols = width // count

    def body(near_ref, moved_ref, resid_ref, live_ref, out_ref):
        for k in range(count):
            at = slice(k * cols, (k + 1) * cols)
            ffn = near_ref[:, at].astype(F32) + moved_ref[:, at].astype(F32)
            out_ref[k] = (live_ref[...] * (resid_ref[:, at] + ffn)).astype(BF16)

    return whole_kernel(body, [shape_of(count, rows, cols, dtype=BF16)], near, moved, resid, live)[0]


def back_tokens(near, moved, tok, grad_resid, in_gain, mlp_sum, chan_rows):
    rows, width = tok.shape
    count, _, cols = chan_rows.shape

    def body(near_ref, first_ref, second_ref, tok_ref, grad_ref, gain_ref, mlp_ref, chan_ref, out_ref):
        g = near_ref[...].astype(F32) + joined((first_ref, second_ref))
        x = tok_ref[...].astype(F32)
        r = lax.rsqrt(jnp.sum(x * x, axis=-1, keepdims=True) / width + EPS)
        in_sum = jnp.sum(g * x * r, axis=0, keepdims=True)
        g = g * gain_ref[...]
        inner = jnp.sum(x * g, axis=-1, keepdims=True)
        grad = (grad_ref[...] + r * g - x * (r * r * r * inner / width)).astype(BF16)
        place = lax.broadcasted_iota(jnp.int32, (16, cols), 0)
        for k in range(count):
            at = slice(k * cols, (k + 1) * cols)
            out_ref[k, :rows, :] = grad[:, at]
            extra = jnp.zeros((16, cols), F32)
            for i, total in enumerate((in_sum[:, at], mlp_ref[:, at])):
                high = total.astype(BF16).astype(F32)
                extra = jnp.where(place == i, high, jnp.where(place == 2 + i, total - high, extra))
            extra = jnp.where(place == 4, chan_ref[k], extra)
            out_ref[k, rows:, :] = extra.astype(BF16)

    outs = [shape_of(count, rows + 16, cols, dtype=BF16)]
    return whole_kernel(body, outs, near, *moved, tok, grad_resid, in_gain, mlp_sum, chan_rows)[0]


def order_rows(blocks, place):
    count = len(blocks)
    q, width = blocks[0].shape
    tile = 512

    def body(place_ref, *refs):
        out_ref = refs[count]
        for j in range(count):
            at = pl.multiple_of(lax.bitwise_xor(place_ref[0], j) * q, 16)
            out_ref[pl.ds(at, q), :] = refs[j][...].astype(F32)

    return pl.pallas_call(
        body,
        grid=(width // tile,),
        out_shape=shape_of(count * q, width),
        in_specs=[SMEM_SPEC] + [pl.BlockSpec((q, tile), lambda i: (0, i))] * count,
        out_specs=pl.BlockSpec((count * q, tile), lambda i: (0, i)),
        compiler_params=params(),
        cost_estimate=NO_COST,
    )(place, *blocks)


def turn_rows(blocks, place):
    count = len(blocks)
    q, width = blocks[0].shape
    tile = 256

    def body(place_ref, *refs):
        out_ref, held = refs[count], refs[count + 1]
        for j in range(count):
            held[lax.bitwise_xor(place_ref[0], j)] = refs[j][...].astype(F32)
        out_ref[...] = held[...].reshape(count * q, tile).T

    return pl.pallas_call(
        body,
        grid=(width // tile,),
        out_shape=shape_of(width, count * q),
        in_specs=[SMEM_SPEC] + [pl.BlockSpec((q, tile), lambda i: (0, i))] * count,
        out_specs=pl.BlockSpec((tile, count * q), lambda i: (i, 0)),
        scratch_shapes=[pltpu.VMEM((count, q, tile), F32)],
        compiler_params=params(),
        cost_estimate=NO_COST,
    )(place, *blocks)


def dot_nt(a, b):
    return lax.dot_general(a, b, (((1,), (1,)), ((), ())), preferred_element_type=F32)


def dot_nn(a, b):
    return lax.dot_general(a, b, (((1,), (0,)), ((), ())), preferred_element_type=F32)


def dot_tn(a, b):
    return lax.dot_general(a, b, (((0,), (0,)), ((), ())), preferred_element_type=F32)


def on_device(
    net,
    tokens,
    cotangent,
    lengths,
    in_gain,
    w_input,
    w_forget,
    w_output_gate,
    lower_bound,
    mix_gain,
    w_out,
    mlp_gain,
    w_gate,
    w_up,
    w_down,
):
    s, t = net.places()
    n_seq, n_tp = net.seq, net.tp
    slots, group, cols = tokens.shape
    width = cols * n_tp
    pos_n = group // n_tp
    rows = slots * pos_n
    dq = cols // n_seq
    fq = w_down.shape[0] // n_seq
    chan, hid = dq * n_tp, fq * n_tp
    place = s.reshape(1)
    order = net.order

    def quarter_t(w, q):
        return lax.dynamic_slice_in_dim(w, s * q, q, 1).T

    def by_owner(x):
        return x.reshape(slots, n_tp, pos_n, cols).transpose(1, 0, 2, 3).reshape(n_tp, rows, cols)

    def to_owner(x):
        return lax.all_to_all(x, "tp", 0, 0, tiled=True)

    def in_place(x):
        return x.reshape(n_tp, slots, pos_n, cols).transpose(1, 0, 2, 3).reshape(tokens.shape)

    where = s * group + t * pos_n + jnp.arange(pos_n, dtype=jnp.int32)
    live = (where[None, :] < lengths[:, None]).astype(F32).reshape(rows, 1)

    small = jnp.concatenate(
        [lax.dynamic_slice_in_dim(v, s * dq, dq) for v in (lower_bound, mix_gain)] + [mlp_gain], 0
    )
    terms, rest = [], small
    for _ in range(3):
        terms.append(hold(rest.astype(BF16))[0])
        rest = rest - terms[-1].astype(F32)
    terms = jnp.pad(jnp.concatenate(terms, 0), (0, 16 * cols - 3 * small.shape[0])).reshape(1, 16, cols)
    token_blocks = to_owner(jnp.concatenate([by_owner(tokens), jnp.broadcast_to(terms, (n_tp, 16, cols))], 1))
    small = token_blocks[:, rows:].reshape(n_tp, 16 * cols)[:, : 3 * small.shape[0]].astype(F32).reshape(n_tp, 3, -1)
    small = small[:, 0] + small[:, 1] + small[:, 2]
    bound = small[:, :dq].reshape(1, chan)
    gain = small[:, dq : 2 * dq].reshape(1, chan)
    mlp_full = small[:, 2 * dq :].reshape(1, width)
    mix_w = jnp.concatenate(
        [quarter_t(w, dq) for w in (w_input, w_forget, w_output_gate)]
        + [lax.dynamic_slice_in_dim(w_out, s * dq, dq, 0)],
        0,
    )
    tok, normed_own = norm_tokens(token_blocks, in_gain, rows)
    mix_ring = RingGather(net, after(mix_w, normed_own))
    mix_ring.launch(mix_ring.sends())
    normed = net.gather_rest(net.gather_first(normed_own))
    mix_ring.finish()
    w3, wo = Weights(), Weights()
    w3.add(mix_ring, [(i * dq, i * chan) for i in range(3)], dq, True)
    wo.add(mix_ring, [(3 * dq, 0)], dq, True)
    gate_ring = RingGather(net, after(quarter_t(w_gate, fq), *mix_ring.came))
    up_ring = RingGather(net, after(quarter_t(w_up, fq), *mix_ring.came))
    gate_ring.launch(gate_ring.sends())
    up_ring.launch(up_ring.sends())
    half = n_seq // 2

    pre, normed_all, decay, end = mixer_in(order, normed, w3, bound, slots, pos_n)

    def spread(pair, reverse):
        def joined(earlier, later):
            return earlier[0] * later[0], later[0] * earlier[1] + later[1]

        whole = pair
        before = (jnp.ones_like(pair[0]), jnp.zeros_like(pair[1]))
        for bit in net.tp_bits:
            moved = net.cross(jnp.stack(whole, 0), bit)
            moved = (moved[0], moved[1])
            upper = (jnp.bitwise_and(t, bit) != 0) != reverse
            ahead, behind = joined(moved, whole), joined(whole, moved)
            longer = joined(moved, before)
            before = tuple(jnp.where(upper, a, b) for a, b in zip(longer, before))
            whole = tuple(jnp.where(upper, a, b) for a, b in zip(ahead, behind))
        return before, whole

    (decay, end), gate_ring.came, up_ring.came = hold((decay, end), gate_ring.came, up_ring.came)
    head = scan_heads(place, *spread((decay, end), False), False)
    head, sends, up_sends = hold(head, gate_ring.sends(), up_ring.sends())
    gate_ring.launch(sends)
    some, far = mixer_out(order, pre, bound, gain, head, wo, pos_n, half, half)
    head_near, some = hold(head, some)
    (state, mix, squares), parts = mixer_out(order, pre, bound, gain, head_near, wo, pos_n, 0, half, some, False)
    near_far = net.quad_far_part(far)
    near_far, parts, squares, gate_ring.came = hold(near_far, parts, squares, gate_ring.came)
    moved_far = net.swap(near_far, net.bits[-1])
    up_ring.launch(up_sends)
    sum_all = net.total_far(net.total_near(jnp.sum(squares, -1).reshape(n_seq, rows)))
    near_own = net.quad_far_part(parts)
    near_own, up_ring.came, sends = hold(near_own, up_ring.came, gate_ring.sends())
    gate_ring.launch(sends)
    near_own, moved_far, sum_all, gate_ring.came, sends = hold(
        near_own, moved_far, sum_all, gate_ring.came, up_ring.sends()
    )
    up_ring.launch(sends)
    r_mix = lax.rsqrt(sum_all / width + EPS).reshape(n_seq * rows, 1)
    resid, mlp_own = residual(near_own, moved_far, tok, r_mix[:rows], mlp_full)
    mlp_in = net.gather_first(mlp_own)
    up_ring.came, mlp_own, sends = hold(up_ring.came, mlp_own, gate_ring.sends())
    gate_ring.launch(sends)
    up_ring.launch(up_ring.sends())
    gate_ring.finish()
    up_ring.finish()
    mlp_in = net.gather_rest(mlp_in, half)
    wgu = Weights()
    wgu.add(gate_ring, [(0, 0)], fq, False)
    wgu.add(up_ring, [(0, 0)], fq, False)
    down_w = lax.dynamic_slice_in_dim(w_down, s * fq, fq, 0)
    near_in, down_w, cot_sent, _ = hold(mlp_in[:half], down_w, by_owner(cotangent), (gate_ring.came, up_ring.came))

    down_ring = RingGather(net, down_w)
    down_ring.launch(down_ring.sends())
    cot_blocks = to_owner(cot_sent)
    some = feed_forward(order, near_in, wgu, 0, n_seq)
    some, far_first, down_ring.came = hold(some, mlp_in[half], down_ring.came)
    down_ring.launch(down_ring.sends())
    mlp_in = net.gather_rest(mlp_in[:half] + [far_first] + mlp_in[half + 1 :])
    hidden, slope_up, act, mlp_all = feed_forward(order, mlp_in[half:], wgu, half, n_seq, some, False)
    hidden, down_ring.came, cot_blocks = hold(hidden, down_ring.came, cot_blocks)
    down_ring.launch(down_ring.sends())
    cot = mask_rows(cot_blocks, live)
    grad_out = net.gather_first(cot)
    grad_out, down_ring.came = hold(grad_out, down_ring.came)
    down_ring.launch(down_ring.sends())
    down_ring.finish()
    grad_all = jnp.concatenate(net.gather_rest(grad_out), 0)

    def to_output(blocks, turned):
        q = blocks[0].shape[0]
        if q % 16 == 0:
            return turn_rows(blocks, place) if turned else order_rows(blocks, place)
        out = jnp.zeros((n_seq, q, width), F32)
        for j in range(n_seq):
            out = lax.dynamic_update_index_in_dim(out, blocks[j].astype(F32), lax.bitwise_xor(s, j), 0)
        out = out.reshape(n_seq * q, width)
        return out.T if turned else out

    dw_down = dot_tn(hidden, grad_all).astype(BF16)
    down_sum = RingScatter(net, [dw_down], False)
    wd = Weights()
    wd.add(down_ring, [(0, 0)], fq, False)
    sends, grad_all, _ = hold(down_sum.sends(), grad_all, down_ring.came)
    down_sum.launch(sends)
    grad_gate, grad_up = back_hidden(order, grad_all, wd, slope_up, act, rows)
    grad_gate, down_sum.came = hold(grad_gate, down_sum.came)
    sends, grad_gate = hold(down_sum.sends(), grad_gate)
    down_sum.launch(sends)
    far = back_pair(order, grad_gate, grad_up, wgu, rows, half, half)
    far, down_sum.came = hold(far, down_sum.came)
    sent, sends, grad_gate = hold(net.halved(net.quad_far_part(far)), down_sum.sends(), grad_gate)
    moved = [net.swap(x, net.bits[-1]) for x in sent]
    down_sum.launch(sends)
    parts = back_pair(order, grad_gate, grad_up, wgu, rows, 0, half)
    parts, moved[0], down_sum.came = hold(parts, moved[0], down_sum.came)
    sends, grad_gate = hold(down_sum.sends(), grad_gate)
    down_sum.launch(sends)
    near_own = net.quad_far_part(parts)
    dw_gate = dot_tn(grad_gate, mlp_all).astype(BF16)
    dw_gate, moved[1], near_own, down_sum.came = hold(dw_gate, moved[1], near_own, down_sum.came)
    grad_resid, branch_own, mlp_sum = back_residual(near_own, moved, resid, cot, mlp_full)
    gate_sum = RingScatter(net, [dw_gate], False)
    branch_own, sends, sent, hidden = hold(branch_own, gate_sum.sends(), net.halved(branch_own), hidden)
    grad_branch = [[x] for x in net.gather_near(branch_own)]
    moved = [net.swap(x, net.bits[-1]) for x in sent]
    gate_sum.launch(sends)
    ffn_parts = down_parts(order, hidden, wd, rows)
    ffn_parts, moved[0], grad_branch, gate_sum.came = hold(ffn_parts, moved[0], grad_branch, gate_sum.came)
    grad_branch_a = net.gather_near(moved[0])
    down_own = down_sum.result()
    sends, grad_up = hold(gate_sum.sends(), grad_up)
    gate_sum.launch(sends)
    ffn_near = net.quad_near(ffn_parts)
    dw_up = dot_tn(grad_up, mlp_all).astype(BF16)
    dw_up, moved[1], gate_sum.came, ffn_near = hold(dw_up, moved[1], gate_sum.came, ffn_near)
    grad_branch = grad_branch + [list(x) for x in zip(grad_branch_a, net.gather_near(moved[1]))]
    up_sum = RingScatter(net, [dw_up], False)

    sends, up_sends, grad_branch, down_own = hold(gate_sum.sends(), up_sum.sends(), grad_branch, down_own)
    gate_sum.launch(sends)
    up_sum.launch(up_sends)
    down_blocks = net.gather_first(down_own)
    g_norm, grad_og, mixed_out, branch_all, inner_lanes, gain_sums = back_mixer(
        order, grad_branch, rows, wo, pre, state, mix, r_mix, gain
    )
    inner_lanes, gate_sum.came, up_sum.came, down_blocks = hold(
        inner_lanes, gate_sum.came, up_sum.came, down_blocks
    )
    sends, up_sends, inner_lanes = hold(gate_sum.sends(), up_sum.sends(), inner_lanes)
    gate_sum.launch(sends)
    up_sum.launch(up_sends)
    inner = net.total_far(net.total_near(jnp.sum(inner_lanes, -1).reshape(n_seq, rows))).reshape(-1, 1)
    ffn = net.quad_far([after(p, inner) for p in ffn_near])
    coef = r_mix**3 * inner / width
    back_end = back_ends(pre, bound, g_norm, state, r_mix, coef, slots, pos_n)
    dw_out = dot_tn(after(mixed_out, back_end), branch_all).astype(BF16)
    dw_og = dot_tn(after(grad_og, dw_out), normed_all).astype(BF16)
    back_end, gate_sum.came, up_sum.came, dw_og = hold(back_end, gate_sum.came, up_sum.came, dw_og)
    tail = scan_heads(place, *spread((decay, back_end), True), True)
    gate_own = gate_sum.result()
    tail, up_sends, gate_own = hold(tail, up_sum.sends(), gate_own)
    up_sum.launch(up_sends)

    def back(start, tail, long):
        return back_states(
            order, pre, bound, g_norm, state, grad_og, r_mix, coef, head, tail, w3, pos_n, start, half, long
        )

    (far_in, far_fg, far_low), far = back(half, tail, True)
    far, far_in, up_sum.came, ffn = hold(far, far_in, up_sum.came, ffn)
    first_sum = RingScatter(net, [dw_out, dw_og], True)
    mixed_sent = block_output(*ffn, resid, live, n_tp)
    sent, tail, up_sends, sends, mixed_sent = hold(
        net.halved(net.quad_far_part(far)), tail, up_sum.sends(), first_sum.sends(), mixed_sent
    )
    moved = [net.swap(x, net.bits[-1]) for x in sent]
    up_sum.launch(up_sends)
    first_sum.launch(sends)
    mixed_got = to_owner(mixed_sent)
    (grad_in, grad_fg, low_sums), parts = back(0, tail, True)
    parts, moved[0], first_sum.came, up_sum.came = hold(parts, moved[0], first_sum.came, up_sum.came)
    up_own = up_sum.result()
    low_sums = low_sums + far_low
    grad_in, grad_fg = (jnp.concatenate([a, b], 0) for a, b in ((grad_in, far_in), (grad_fg, far_fg)))
    sends, up_own, grad_in = hold(first_sum.sends(), up_own, grad_in)
    first_sum.launch(sends)
    near_own = net.quad_far_part(parts)
    dw_in = dot_tn(grad_in, normed_all).astype(BF16)
    dw_fg = dot_tn(after(grad_fg, dw_in), normed_all).astype(BF16)
    last_sum = RingScatter(net, [dw_in, dw_fg], True)
    last_sends, near_own, first_sum.came = hold(last_sum.sends(), near_own, first_sum.came)
    last_sum.launch(last_sends)
    first_sum.launch(first_sum.sends())
    near_own, moved = hold(near_own, moved)
    sums = jnp.stack([jnp.sum(low_sums, axis=(0, 1)), jnp.sum(gain_sums, axis=(0, 1))], 0).reshape(2, n_tp, dq)
    high = hold(sums.astype(BF16))[0].astype(F32)
    chan_rows = jnp.concatenate([high, sums - high], 0).transpose(1, 0, 2).reshape(n_tp, 1, 4 * dq)
    chan_rows = jnp.pad(chan_rows, ((0, 0), (0, 0), (0, cols - 4 * dq)))
    sent = back_tokens(near_own, moved, tok, grad_resid, in_gain.reshape(1, width), mlp_sum, chan_rows)

    sent, up_own, last_sum.came, first_sum.came = hold(sent, up_own, last_sum.came, first_sum.came)
    got = to_owner(sent)
    up_blocks, gate_blocks = net.gather_first(up_own), net.gather_first(after(gate_own, up_own))
    down_blocks = net.gather_rest([after(down_blocks[0], up_own)] + down_blocks[1:])
    grad_w_down = to_output(down_blocks, False)
    sends, last_sends = hold(first_sum.sends(), last_sum.sends())
    last_sum.launch(last_sends)
    first_sum.launch(sends)
    last_sum.came, first_sum.came, grad_w_down = hold(last_sum.came, first_sum.came, grad_w_down)
    last_sum.launch(hold(last_sum.sends())[0])
    first_own = first_sum.result()
    first_blocks = net.gather_first(first_own)
    grad_w_up = to_output(net.gather_rest(up_blocks), False)
    grad_w_gate = to_output(net.gather_rest(gate_blocks), False)
    last_sum.came, grad_w_up, grad_w_gate, got, mixed_got = hold(
        last_sum.came, grad_w_up, grad_w_gate, got, mixed_got
    )
    last_sum.launch(hold(last_sum.sends())[0])
    grad_w_gate, grad_w_up = grad_w_gate.T, grad_w_up.T
    first_blocks = net.gather_rest(first_blocks)
    grad_w_out = to_output([b[:dq] for b in first_blocks], False)
    grad_w_og = to_output([b[dq:] for b in first_blocks], True)
    last_sum.came, grad_w_out, grad_w_og = hold(last_sum.came, grad_w_out, grad_w_og)
    last_own = last_sum.result()
    last_blocks = net.gather_rest(net.gather_first(last_own))
    grad_w_in = to_output([b[:dq] for b in last_blocks], True)
    grad_w_fg = to_output([b[dq:] for b in last_blocks], True)
    mixed = in_place(mixed_got)
    sums = jnp.sum(got[:, rows : rows + 5].astype(F32), 0)
    ends = jnp.concatenate([sums[:2] + sums[2:4], sums[4:5]], 0).reshape(1, 3, cols)
    for bit in net.bits:
        ends = jnp.concatenate([ends, net.swap(ends, bit)], 0)
    mine = jnp.sum(ends[:, :2], 0)
    chans = ends[lax.bitwise_xor(s, jnp.arange(n_seq, dtype=jnp.int32)), 2, : 4 * dq].reshape(n_seq, 2, 2, dq)
    chans = chans[:, 0] + chans[:, 1]
    return (
        mixed,
        in_place(got[:, :rows]).astype(F32),
        mine[0],
        grad_w_in,
        grad_w_fg,
        grad_w_og,
        chans[:, 0].reshape(-1),
        chans[:, 1].reshape(-1),
        grad_w_out,
        mine[1],
        grad_w_gate,
        grad_w_up,
        grad_w_down,
    )


def solution(mesh):
    return jax.shard_map(
        functools.partial(on_device, Net(mesh)),
        mesh=mesh,
        in_specs=(
            P(None, "seq", "tp"),
            P(None, "seq", "tp"),
            P(),
            P(),
            P(None, "tp"),
            P(None, "tp"),
            P(None, "tp"),
            P("tp"),
            P("tp"),
            P("tp", None),
            P("tp"),
            P(None, "tp"),
            P(None, "tp"),
            P("tp", None),
        ),
        out_specs=(
            P(None, "seq", "tp"),
            P(None, "seq", "tp"),
            P("tp"),
            P(None, "tp"),
            P(None, "tp"),
            P(None, "tp"),
            P("tp"),
            P("tp"),
            P("tp", None),
            P("tp"),
            P(None, "tp"),
            P(None, "tp"),
            P("tp", None),
        ),
        check_vma=False,
    )
```

```python
import functools

import jax
import jax.numpy as jnp
import numpy as np
from jax import lax
from jax.experimental import pallas as pl
from jax.experimental.pallas import tpu as pltpu
from jax.sharding import PartitionSpec as P

EPS = 1e-06
F32, BF16 = jnp.float32, jnp.bfloat16
VMEM_LIMIT = 56 * 1024 * 1024
NO_COST = pl.CostEstimate(flops=1, bytes_accessed=1, transcendentals=0)
LONG = pl.CostEstimate(flops=10**12, bytes_accessed=10**9, transcendentals=0)


def params(**more):
    return pltpu.CompilerParams(vmem_limit_bytes=VMEM_LIMIT, **more)


def sigmoid(v):
    return 1.0 / (1.0 + jnp.exp(-v))


def fast_sigmoid(v):
    d = 1.0 + jnp.exp(jnp.minimum(-v, 80.0))
    r = pl.reciprocal(d, approx=True)
    return r * (2.0 - d * r)


def ring_of(mesh):
    count = mesh.shape["tp"]
    try:
        coords = [tuple(d.coords) for d in mesh.devices[0]]
        ys = len({c[1] for c in coords})
    except (AttributeError, TypeError):
        ys = 2 if count % 2 == 0 else 1
    zs = count // ys
    if zs * ys != count or zs % 2 or ys < 2:
        return list(range(count))
    cycle = [(z, 0) for z in range(zs)]
    for turn, z in enumerate(reversed(range(zs))):
        across = range(1, ys) if turn % 2 == 0 else reversed(range(1, ys))
        cycle += [(z, y) for y in across]
    return [z * ys + y for z, y in cycle]


class Net:
    def __init__(self, mesh):
        self.seq, self.tp = mesh.shape["seq"], mesh.shape["tp"]
        self.cycle = ring_of(mesh)
        self.bits = [1 << b for b in range(self.seq.bit_length() - 1)]
        self.tp_bits = [1 << b for b in range(self.tp.bit_length() - 1)]

    def places(self):
        s, t = lax.axis_index("seq"), lax.axis_index("tp")
        where = np.zeros(self.tp, np.int32)
        for i, index in enumerate(self.cycle):
            where[index] = i
        pos = jnp.asarray(where)[t]
        steps = [[self.cycle[(i - d) % self.tp] for d in range(self.tp)] for i in where]
        self.order = lax.dynamic_index_in_dim(jnp.asarray(np.array(steps, np.int32)), t, 0, False)
        self.behind = [self.order[d] for d in range(self.tp)]
        self.inverse = (pos - jnp.asarray(where)) % self.tp
        return s, t

    def shift(self, x, k):
        n = self.tp
        return lax.ppermute(x, "tp", [(self.cycle[i], self.cycle[(i + k) % n]) for i in range(n)])

    def cross(self, x, bit):
        return lax.ppermute(x, "tp", [(i, i ^ bit) for i in range(self.tp)])

    def swap(self, x, bit):
        return lax.ppermute(x, "seq", [(i, i ^ bit) for i in range(self.seq)])

    def halves(self, size):
        half = size // 2
        return half // 16 * 16 if size >= 32 else half

    def gather_first(self, x):
        out = [x] + [None] * (self.seq - 1)
        for bit in reversed(self.bits):
            out[bit] = self.swap(x, bit)
        return out

    def gather_rest(self, out, end=None):
        out = list(out)
        for j in range(end or self.seq):
            if out[j] is None:
                out[j] = self.swap(out[j & (j - 1)], j & -j)
        return out

    def gather_near(self, x):
        out = [x]
        for bit in self.bits[:-1]:
            out = out + [self.swap(y, bit) for y in out]
        return out

    def halved(self, x):
        half = x.shape[0] // 2
        return [x[:half], x[half:]]

    def quad_far_part(self, parts):
        parts = list(parts)
        for bit in self.bits[:-1]:
            for j in reversed(range(0, len(parts), 2 * bit)):
                moved = self.swap(parts[j ^ bit], bit)
                parts[j] = (parts[j].astype(F32) + moved.astype(F32)).astype(BF16)
        return parts[0]

    def quad_near(self, parts):
        half = self.seq // 2
        far = self.quad_far_part(parts[half:])
        return [self.quad_far_part(parts[:half]), far]

    def quad_far(self, near):
        return [near[0], self.swap(near[1], self.bits[-1])]

    def total_step(self, x, bit):
        moved = self.swap(x, bit)
        return x + jnp.stack([moved[j ^ bit] for j in range(self.seq)], 0)

    def total_near(self, x):
        for bit in self.bits[:-1]:
            x = self.total_step(x, bit)
        return x

    def total_far(self, x):
        return self.total_step(x, self.bits[-1])


def after(x, *others):
    return lax.optimization_barrier((x,) + others)[0]


def hold(*trees):
    return lax.optimization_barrier(trees)


class RingGather:
    def __init__(self, net, x):
        self.net, self.size = net, x.shape[0]
        n = net.tp
        self.blocks = [[(x, 0)]] + [None] * (n - 1)
        self.full = (n - 1) // 2
        self.made = 0
        self.came = (x, x)

    def done(self):
        return self.made == self.net.tp // 2

    def sends(self):
        if self.done():
            return ()
        fore, back = self.came
        if self.made < self.full:
            return fore, back
        half = self.net.halves(self.size)
        return fore[:half], back[half:]

    def launch(self, sends):
        if self.done():
            return
        net, n = self.net, self.net.tp
        self.made += 1
        d = self.made
        self.came = net.shift(sends[0], 1), net.shift(sends[1], -1)
        if d <= self.full:
            self.blocks[d], self.blocks[n - d] = [(self.came[0], 0)], [(self.came[1], 0)]
        else:
            self.blocks[d] = [(self.came[0], 0), (self.came[1], net.halves(self.size))]

    def finish(self):
        while not self.done():
            self.launch(self.sends())

    def rows(self, start, q):
        out = []
        for block in self.blocks:
            whole = jnp.concatenate([a for a, _ in block], 0) if len(block) > 1 else block[0][0]
            out.append(whole[start : start + q])
        return out


class RingScatter:
    def __init__(self, net, wholes, canonical):
        self.net, self.wholes, self.canonical = net, wholes, canonical
        self.sizes = [w.shape[0] // net.tp for w in wholes]
        self.size = sum(self.sizes)
        self.d = net.tp // 2
        self.came = ()
        self.half = net.halves(self.size) if net.tp % 2 == 0 else 0

    def done(self):
        return self.d == 0

    def make(self, outs):
        net = self.net
        made = []
        for d, low, high, adds in outs:
            rows = []
            for w, q in zip(self.wholes, self.sizes):
                at = net.behind[d] * q if self.canonical else d * q
                rows.append(lax.dynamic_slice_in_dim(w, at, q, 0))
            whole = jnp.concatenate(rows, 0)[low:high]
            for part, start in adds:
                first = start - low
                part = jnp.pad(part.astype(F32), ((first, high - low - first - part.shape[0]), (0, 0)))
                whole = whole.astype(F32) + part
            made.append(whole.astype(BF16))
        return made

    def adds(self, which):
        if not self.came:
            return []
        after_half = which == 1 and 2 * (self.d + 1) == self.net.tp
        return [(self.came[which], self.half if after_half else 0)]

    def sends(self):
        if self.done():
            return ()
        n, d = self.net.tp, self.d
        if 2 * d == n:
            return self.make([(d, 0, self.half, []), (d, self.half, self.size, [])])
        return self.make([(n - d, 0, self.size, self.adds(0)), (d, 0, self.size, self.adds(1))])

    def launch(self, sends):
        if self.done():
            return
        self.d -= 1
        self.came = self.net.shift(sends[0], 1), self.net.shift(sends[1], -1)

    def result(self):
        while not self.done():
            self.launch(self.sends())
        return self.make([(0, 0, self.size, self.adds(0) + self.adds(1))])[0]


SMEM_SPEC = pl.BlockSpec(memory_space=pltpu.SMEM)
VMEM_SPEC = pl.BlockSpec(memory_space=pltpu.VMEM)


def norm_tokens(blocks, gain, rows):
    count, _, cols = blocks.shape
    width = count * cols

    def body(gain_ref, in_ref, x_ref, n_ref):
        total = jnp.zeros((rows, 1), F32)
        for k in range(count):
            c = in_ref[k, :rows].astype(F32)
            total += jnp.sum(c * c, axis=-1, keepdims=True)
        r = lax.rsqrt(total / width + EPS)
        for k in range(count):
            c = in_ref[k, :rows]
            at = slice(k * cols, (k + 1) * cols)
            x_ref[:, at] = c
            n_ref[:, at] = (c.astype(F32) * r * gain_ref[:, at]).astype(BF16)

    return pl.pallas_call(
        body,
        out_shape=[jax.ShapeDtypeStruct((rows, width), BF16)] * 2,
        in_specs=[VMEM_SPEC] * 2,
        out_specs=[VMEM_SPEC] * 2,
        compiler_params=params(),
        cost_estimate=NO_COST,
    )(gain.reshape(1, width), blocks)


def mask_rows(blocks, live):
    count, rows, cols = blocks.shape
    width = count * cols

    def body(live_ref, in_ref, x_ref):
        for k in range(count):
            at = slice(k * cols, (k + 1) * cols)
            x_ref[:, at] = (in_ref[k].astype(F32) * live_ref[...]).astype(BF16)

    return pl.pallas_call(
        body,
        out_shape=jax.ShapeDtypeStruct((rows, width), BF16),
        in_specs=[VMEM_SPEC] * 2,
        out_specs=VMEM_SPEC,
        compiler_params=params(),
        cost_estimate=NO_COST,
    )(live, blocks)


def tile_scan(decay, drive):
    place = lax.broadcasted_iota(jnp.int32, decay.shape, 0)
    for step in (1, 2, 4):
        inside = place >= step
        before_decay = jnp.where(inside, pltpu.roll(decay, step, 0), 1.0)
        before_drive = jnp.where(inside, pltpu.roll(drive, step, 0), 0.0)
        drive = drive + decay * before_drive
        decay = decay * before_decay
    return decay, drive


def tile_scan_up(decay, drive):
    place = lax.broadcasted_iota(jnp.int32, decay.shape, 0)
    for step in (1, 2, 4):
        inside = place < 8 - step
        before_decay = jnp.where(inside, pltpu.roll(decay, 8 - step, 0), 1.0)
        before_drive = jnp.where(inside, pltpu.roll(drive, 8 - step, 0), 0.0)
        drive = drive + decay * before_drive
        decay = decay * before_decay
    return decay, drive


def gates(pre_in, pre_fg, bound):
    sig_f = fast_sigmoid(pre_fg)
    forget = bound + (1.0 - bound) * sig_f
    sig_in = fast_sigmoid(pre_in)
    act_in = pre_in * sig_in
    slope_in = sig_in * (1.0 + pre_in * (1.0 - sig_in))
    keep = (1.0 - bound) * (1.0 - sig_f)
    return sig_f, forget, act_in, slope_in, keep


class Weights:
    def __init__(self):
        self.arrays, self.takes, self.shapes = [], [], []

    def add(self, ring, parts, stride, canonical):
        held, n = len(self.shapes), ring.net.tp
        width = ring.blocks[0][0][0].shape[1]
        self.shapes.append((len(parts) * n * stride, width))
        if stride % 16:
            for start, at in parts:
                rows = ring.rows(start, stride)
                whole = jnp.stack(rows, 0)
                if canonical:
                    whole = whole[ring.net.inverse]
                self.takes.append((len(self.arrays), 0, n * stride, held, None, at))
                self.arrays.append(whole.reshape(n * stride, width))
            return
        seen = {id(a): i for i, a in enumerate(self.arrays)}
        for d, block in enumerate(ring.blocks):
            for array, first in block:
                if id(array) not in seen:
                    seen[id(array)] = len(self.arrays)
                    self.arrays.append(array)
                for start, at in parts:
                    low, high = max(start, first), min(start + stride, first + array.shape[0])
                    if low < high:
                        place = (d, stride) if canonical else None
                        row = at + (low - start) + (0 if canonical else d * stride)
                        self.takes.append((seen[id(array)], low - first, high - low, held, place, row))

    def copies(self, order_ref, refs, held, sems):
        out = []
        for k, (source, first, size, to, place, row) in enumerate(self.takes):
            if place is not None:
                row = pl.multiple_of(order_ref[place[0]] * place[1] + row, 16)
            out.append(
                pltpu.make_async_copy(refs[source].at[pl.ds(first, size)], held[to].at[pl.ds(row, size)], sems.at[k])
            )
        return out


def step_kernel(body, order, count, rows, blocks, weights, ins, outs, width, onto=(), long=True):
    any_spec = pl.BlockSpec(memory_space=pl.ANY)
    pieces = [(j, i, sum(a.shape[0] for a in block[:i]), a) for j, block in enumerate(blocks) for i, a in enumerate(block)]
    n_x, n_w, n_in, n_out = len(pieces), len(weights.arrays), len(ins), len(outs)
    n_part = count if width else 0
    n_held, n_onto = len(weights.shapes), len(onto)

    def kernel(order_ref, *refs):
        refs = list(refs)

        def take(k):
            out = refs[:k]
            del refs[:k]
            return out

        x_refs, w_refs, in_refs, _ = take(n_x), take(n_w), take(n_in), take(n_onto)
        out_refs, part_refs = take(n_out), take(n_part)
        held, w_sems = take(n_held), take(1)[0]
        xs, x_sems = take(2) if n_x else (None, None)
        kept, part_sems = take(2) if n_part else (None, None)
        j = pl.program_id(0)
        loads = weights.copies(order_ref, w_refs, held, w_sems)
        x_loads = [
            pltpu.make_async_copy(x_refs[k], xs.at[at, pl.ds(start, a.shape[0])], x_sems.at[k])
            for k, (at, _, start, a) in enumerate(pieces)
        ]

        @pl.when(j == 0)
        def _():
            first = [x for x, (at, _, _, _) in zip(x_loads, pieces) if at == 0]
            for load in first + loads + x_loads[len(first) :]:
                load.start()

        left = list(zip(weights.takes, loads))

        def ready(which):
            now = [x for x in left if x[0][3] == which]
            for x in now:
                left.remove(x)
            if now:

                @pl.when(j == 0)
                def _():
                    for _, load in now:
                        load.wait()

        for k in range(n_x):

            @pl.when(j == pieces[k][0])
            def _(k=k):
                x_loads[k].wait()

        x = xs[j] if n_x else None
        part = body(x, held, in_refs, out_refs, ready)
        for which in range(n_held):
            ready(which)
        stores = [pltpu.make_async_copy(kept.at[k % 2], part_refs[k], part_sems.at[k]) for k in range(n_part)]
        for k in range(n_part):

            @pl.when(j == k)
            def _(k=k):
                if k >= 2:
                    stores[k - 2].wait()
                kept[k % 2] = part
                stores[k].start()
                if k == n_part - 1:
                    for store in stores[max(k - 1, 0) :]:
                        store.wait()

    scratch = [pltpu.VMEM(shape, BF16) for shape in weights.shapes]
    scratch.append(pltpu.SemaphoreType.DMA((max(len(weights.takes), 1),)))
    if n_x:
        scratch += [pltpu.VMEM((len(blocks), rows, pieces[0][3].shape[1]), BF16), pltpu.SemaphoreType.DMA((n_x,))]
    if n_part:
        scratch += [pltpu.VMEM((2, rows, width), BF16), pltpu.SemaphoreType.DMA((n_part,))]
    out = pl.pallas_call(
        kernel,
        grid=(count,),
        out_shape=[shape for shape, _ in outs] + [jax.ShapeDtypeStruct((rows, width), BF16)] * n_part,
        in_specs=[SMEM_SPEC] + [any_spec] * (n_x + n_w) + [spec for _, spec in ins] + [any_spec] * n_onto,
        out_specs=[spec for _, spec in outs] + [any_spec] * n_part,
        input_output_aliases={1 + n_x + n_w + n_in + i: i for i in range(n_onto)},
        scratch_shapes=scratch,
        compiler_params=params(),
        cost_estimate=LONG if long else NO_COST,
    )(order, *[a for _, _, _, a in pieces], *weights.arrays, *[a for a, _ in ins], *onto)
    return list(out[:n_out]), list(out[n_out:])


def shape_of(*shape, dtype=F32):
    return jax.ShapeDtypeStruct(shape, dtype)


def by_block(rows, wide, first=0, column=0):
    return pl.BlockSpec((rows, wide), lambda b: (b + first, column))


def whole_row(wide):
    return pl.BlockSpec((1, wide), lambda b: (0, 0))


def by_slot(slots, wide, first=0):
    return pl.BlockSpec((1, slots, wide), lambda b: (b + first, 0, 0))


def columns(wide):
    return [slice(c, min(c + 256, wide)) for c in range(0, wide, 256)]


def mixer_in(order, blocks, weights, bound, slots, pos_n):
    count, (rows, depth), wide = len(blocks), blocks[0].shape, bound.shape[1]

    def body(x, held, ins, outs, ready):
        pre_ref, all_ref, decay_ref, end_ref = outs
        low = ins[0][...]
        all_ref[...] = x
        ready(0)
        pre_ref[...] = dot_nt(x, held[0][...])

        def one(i, carry):
            out = []
            for k in range(slots):
                at = pl.ds(pl.multiple_of(k * pos_n + i * 8, 8), 8)
                _, forget, act, _, keep = gates(pre_ref[at, :wide], pre_ref[at, wide : 2 * wide], low)
                decay, local = tile_scan(forget, act * keep)
                a, h = carry[k]
                out.append((a * decay[7:8, :], decay[7:8, :] * h + local[7:8, :]))
            return tuple(out)

        start = (jnp.ones((1, wide), F32), jnp.zeros((1, wide), F32))
        ends = lax.fori_loop(0, pos_n // 8, one, (start,) * slots)
        for k in range(slots):
            decay_ref[0, k : k + 1] = ends[k][0]
            end_ref[0, k : k + 1] = ends[k][1]

    outs = [
        (shape_of(count * rows, 3 * wide), by_block(rows, 3 * wide)),
        (shape_of(count * rows, depth, dtype=BF16), by_block(rows, depth)),
        (shape_of(count, slots, wide), by_slot(slots, wide)),
        (shape_of(count, slots, wide), by_slot(slots, wide)),
    ]
    return step_kernel(
        body, order, count, rows, [[x] for x in blocks], weights, [(bound, whole_row(wide))], outs, 0
    )[0]


def scan_heads(place, before, whole, reverse):
    count, slots, wide = whole[0].shape

    def body(place_ref, pa_ref, pb_ref, wa_ref, wb_ref, head_ref):
        state = jnp.zeros((slots, wide), F32)
        for i in range(count):
            j = lax.bitwise_xor(place_ref[0], count - 1 - i if reverse else i)
            head_ref[j] = pa_ref[j] * state + pb_ref[j]
            state = wa_ref[j] * state + wb_ref[j]

    return pl.pallas_call(
        body,
        out_shape=shape_of(count, slots, wide),
        in_specs=[SMEM_SPEC] + [VMEM_SPEC] * 4,
        out_specs=VMEM_SPEC,
        compiler_params=params(),
        cost_estimate=NO_COST,
    )(place, *before, *whole)


def mixer_out(order, pre, bound, gain, head, weights, pos_n, first, steps, onto=(), long=True):
    wide = bound.shape[1]
    count, slots, _ = head.shape
    rows = slots * pos_n
    depth = weights.shapes[0][1]

    def body(x, held, ins, outs, ready):
        pre_ref, bound_ref, gain_ref, head_ref = ins
        state_ref, mix_ref, sum_ref = outs
        low = bound_ref[...]

        def one(i, carry):
            out = []
            for k in range(slots):
                at = pl.ds(pl.multiple_of(k * pos_n + i * 8, 8), 8)
                _, forget, act, _, keep = gates(pre_ref[at, :wide], pre_ref[at, wide : 2 * wide], low)
                decay, local = tile_scan(forget, act * keep)
                state = local + decay * carry[k]
                state_ref[at, :] = state
                square = state * state
                sum_ref[at, :] = sum(square[:, c : c + 128] for c in range(0, wide, 128))
                out.append(state[7:8, :])
            return tuple(out)

        lax.fori_loop(0, pos_n // 8, one, tuple(head_ref[0, k : k + 1] for k in range(slots)))
        og = pre_ref[:, 2 * wide :]
        mix = (state_ref[...] * gain_ref[...] * (og * fast_sigmoid(og))).astype(BF16)
        mix_ref[...] = mix
        ready(0)
        return dot_nn(mix, held[0][...]).astype(BF16)

    ins = [
        (pre, by_block(rows, 3 * wide, first)),
        (bound, whole_row(wide)),
        (gain, whole_row(wide)),
        (head, by_slot(slots, wide, first)),
    ]
    outs = [
        (shape_of(count * rows, wide), by_block(rows, wide, first)),
        (shape_of(count * rows, wide, dtype=BF16), by_block(rows, wide, first)),
        (shape_of(count * rows, 128), by_block(rows, 128, first)),
    ]
    return step_kernel(body, order, steps, rows, [], weights, ins, outs, depth, onto, long)


def feed_forward(order, blocks, weights, first, count, onto=(), long=True):
    (rows, depth), wide = blocks[0].shape, weights.shapes[0][0]

    def body(x, held, ins, outs, ready):
        hid_ref, slope_ref, act_ref, all_ref = outs
        all_ref[...] = x
        ready(0)
        ready(1)
        for at in columns(wide):
            gate = dot_nt(x, held[0][at, :])
            up = dot_nt(x, held[1][at, :])
            sig = fast_sigmoid(gate)
            act = gate * sig
            hid_ref[:, at] = (act * up).astype(BF16)
            slope_ref[:, at] = (up * (sig * (1.0 + gate * (1.0 - sig)))).astype(BF16)
            act_ref[:, at] = act.astype(BF16)

    outs = [(shape_of(count * rows, wide, dtype=BF16), by_block(rows, wide, first))] * 3
    outs = outs + [(shape_of(count * rows, depth, dtype=BF16), by_block(rows, depth, first))]
    return step_kernel(body, order, len(blocks), rows, [[x] for x in blocks], weights, [], outs, 0, onto, long)[0]


def down_parts(order, hidden, weights, rows):
    wide, depth = weights.shapes[0]
    count = hidden.shape[0] // rows

    def body(x, held, ins, outs, ready):
        ready(0)
        return dot_nn(ins[0][...], held[0][...]).astype(BF16)

    return step_kernel(
        body, order, count, rows, [], weights, [(hidden, by_block(rows, wide))], [], depth
    )[1]


def back_hidden(order, g, weights, slope, act, rows):
    wide, depth = weights.shapes[0]
    count = g.shape[0] // rows

    def body(x, held, ins, outs, ready):
        g_ref, slope_ref, act_ref = ins
        ready(0)
        for at in columns(wide):
            hid = dot_nt(g_ref[...], held[0][at, :])
            outs[0][:, at] = (hid * slope_ref[:, at].astype(F32)).astype(BF16)
            outs[1][:, at] = (hid * act_ref[:, at].astype(F32)).astype(BF16)

    block = by_block(rows, wide)
    ins = [(g, by_block(rows, depth)), (slope, block), (act, block)]
    outs = [(shape_of(count * rows, wide, dtype=BF16), block)] * 2
    return step_kernel(body, order, count, rows, [], weights, ins, outs, 0)[0]


def back_pair(order, a, b, weights, rows, first, count):
    wide, depth = weights.shapes[0]

    def body(x, held, ins, outs, ready):
        ready(0)
        ready(1)
        return (dot_nn(ins[0][...], held[0][...]) + dot_nn(ins[1][...], held[1][...])).astype(BF16)

    block = by_block(rows, wide, first)
    return step_kernel(
        body, order, count, rows, [], weights, [(a, block), (b, block)], [], depth
    )[1]


def back_mixer(order, blocks, rows, weights, pre, state, mix, r_mix, gain):
    count, depth, wide = len(blocks), blocks[0][0].shape[1], gain.shape[1]

    def body(x, held, ins, outs, ready):
        og_ref, state_ref, mix_ref, r_ref, gain_ref = ins
        norm_ref, og_out, mix_out, all_ref, inner_ref, sum_ref = outs
        all_ref[...] = x
        ready(0)
        mix_out[...] = (mix_ref[...].astype(F32) * r_ref[...]).astype(BF16)
        g = dot_nt(x, held[0][...])
        og, state = og_ref[...], state_ref[...]
        sig = fast_sigmoid(og)
        act = og * sig
        g_state = g * (state * r_ref[...])
        sum_ref[0] = jnp.sum((g_state * act).reshape(rows // 8, 8, wide), 0)
        og_out[...] = (g_state * gain_ref[...] * (sig * (1.0 + og * (1.0 - sig)))).astype(BF16)
        norm = g * gain_ref[...] * act
        norm_ref[...] = norm
        inner = state * norm
        inner_ref[...] = sum(inner[:, c : c + 128] for c in range(0, wide, 128))

    ins = [
        (pre, pl.BlockSpec((rows, wide), lambda b: (b, 2))),
        (state, by_block(rows, wide)),
        (mix, by_block(rows, wide)),
        (r_mix, by_block(rows, 1)),
        (gain, whole_row(wide)),
    ]
    outs = [
        (shape_of(count * rows, wide), by_block(rows, wide)),
        (shape_of(count * rows, wide, dtype=BF16), by_block(rows, wide)),
        (shape_of(count * rows, wide, dtype=BF16), by_block(rows, wide)),
        (shape_of(count * rows, depth, dtype=BF16), by_block(rows, depth)),
        (shape_of(count * rows, 128), by_block(rows, 128)),
        (shape_of(count, 8, wide), by_slot(8, wide)),
    ]
    return step_kernel(body, order, count, rows, blocks, weights, ins, outs, 0)[0]


def back_ends(pre, bound, norm, state, r_mix, coef, slots, pos_n):
    wide = norm.shape[1]
    rows = slots * pos_n
    count = norm.shape[0] // rows
    tiles = pos_n // 8

    def body(fg_ref, norm_ref, state_ref, r_ref, coef_ref, bound_ref, end_ref):
        low = bound_ref[...]

        def one(i, carry):
            out = []
            for k in range(slots):
                at = pl.ds(pl.multiple_of(k * pos_n + (tiles - 1 - i) * 8, 8), 8)
                local = r_ref[at, :] * norm_ref[at, :] - coef_ref[at, :] * state_ref[at, :]
                forget = low + (1.0 - low) * fast_sigmoid(fg_ref[at, :])
                decay, part = tile_scan_up(forget, forget * local)
                out.append(decay[0:1, :] * carry[k] + part[0:1, :])
            return tuple(out)

        ends = lax.fori_loop(0, tiles, one, (jnp.zeros((1, wide), F32),) * slots)
        for k in range(slots):
            end_ref[0, k : k + 1] = ends[k]

    block = by_block(rows, wide)
    return pl.pallas_call(
        body,
        grid=(count,),
        out_shape=shape_of(count, slots, wide),
        in_specs=[
            pl.BlockSpec((rows, wide), lambda b: (b, 1)),
            block,
            block,
            by_block(rows, 1),
            by_block(rows, 1),
            whole_row(wide),
        ],
        out_specs=by_slot(slots, wide),
        compiler_params=params(),
        cost_estimate=NO_COST,
    )(pre, norm, state, r_mix, coef, bound)


def back_states(order, pre, bound, norm, state, g_og, r_mix, coef, head, tail, weights, pos_n, first, count, long=True):
    wide = norm.shape[1]
    slots = head.shape[1]
    rows = slots * pos_n
    pairs = pos_n // 16
    depth = weights.shapes[0][1]

    def body(x, held, ins, outs, ready):
        in_ref, fg_ref, bound_ref, norm_ref, state_ref, og_ref, r_ref, coef_ref, head_ref, tail_ref = ins
        gin_ref, gfg_ref, low_ref = outs
        low = bound_ref[...]
        place = lax.broadcasted_iota(jnp.int32, (8, wide), 0)
        low_ref[0] = jnp.zeros((8, wide), F32)

        def half(k, tile, g):
            at = pl.ds(pl.multiple_of(k * pos_n + tile * 8, 8), 8)
            sig_f, forget, act, slope, keep = gates(in_ref[at, :], fg_ref[at, :], low)
            now = state_ref[at, :]
            local = r_ref[at, :] * norm_ref[at, :] - coef_ref[at, :] * now
            decay, part = tile_scan_up(forget, forget * local)
            whole = part + decay * g
            g_state = local + jnp.where(place == 7, g, pltpu.roll(whole, 7, 0))
            last = jnp.maximum(k * pos_n + tile * 8 - 1, 0)
            entry = jnp.where(tile == 0, head_ref[0, k : k + 1], state_ref[pl.ds(last, 1), :])
            before = jnp.where(place == 0, entry, pltpu.roll(now, 1, 0))
            g_forget = g_state * (before - act)
            return g_state * keep * slope, g_forget * keep * sig_f, whole[0:1, :], g_forget * (1.0 - sig_f)

        def one(i, carry):
            pair = pairs - 1 - i
            out, total = [], low_ref[0]
            for k in range(slots):
                in_2, fg_2, g, low_2 = half(k, 2 * pair + 1, carry[k])
                in_1, fg_1, g, low_1 = half(k, 2 * pair, g)
                at = pl.ds(pl.multiple_of(k * pos_n + pair * 16, 16), 16)
                gin_ref[at, :] = jnp.concatenate([in_1, in_2], 0).astype(BF16)
                gfg_ref[at, :] = jnp.concatenate([fg_1, fg_2], 0).astype(BF16)
                total = total + low_1 + low_2
                out.append(g)
            low_ref[0] = total
            return tuple(out)

        lax.fori_loop(0, pairs, one, tuple(tail_ref[0, k : k + 1] for k in range(slots)))
        ready(0)
        part = dot_nn(gin_ref[...], held[0][:wide]) + dot_nn(gfg_ref[...], held[0][wide : 2 * wide])
        return (part + dot_nn(og_ref[...], held[0][2 * wide :])).astype(BF16)

    block, edge, one_lane = by_block(rows, wide, first), by_slot(slots, wide, first), by_block(rows, 1, first)
    ins = [
        (pre, block),
        (pre, by_block(rows, wide, first, 1)),
        (bound, whole_row(wide)),
        (norm, block),
        (state, block),
        (g_og, block),
        (r_mix, one_lane),
        (coef, one_lane),
        (head, edge),
        (tail, edge),
    ]
    outs = [(shape_of(count * rows, wide, dtype=BF16), by_block(rows, wide))] * 2
    outs = outs + [(shape_of(count, 8, wide), by_slot(8, wide))]
    return step_kernel(body, order, count, rows, [], weights, ins, outs, depth, (), long)


STEPS = 4


def row_kernel(body, outs, ins, scratch=()):
    def spec(a, kind):
        if kind == "whole":
            return pl.BlockSpec(a.shape, lambda i: (0,) * len(a.shape))
        if kind == "rows":
            return pl.BlockSpec((a.shape[0] // STEPS,) + a.shape[1:], lambda i: (i, 0))
        size = a.shape[0] // (STEPS // 2)
        if kind == "first":
            return pl.BlockSpec((size,) + a.shape[1:], lambda i: (jnp.minimum(i, STEPS // 2 - 1), 0))
        return pl.BlockSpec((size,) + a.shape[1:], lambda i: (jnp.maximum(i - STEPS // 2, 0), 0))

    return pl.pallas_call(
        body,
        grid=(STEPS,),
        out_shape=[a for a, _ in outs],
        in_specs=[spec(*x) for x in ins],
        out_specs=[spec(*x) for x in outs],
        scratch_shapes=scratch,
        compiler_params=params(),
        cost_estimate=NO_COST,
    )(*[a for a, _ in ins])


def half_rows(first_ref, second_ref):
    early = pl.program_id(0) < STEPS // 2
    return jnp.where(early, first_ref[...].astype(F32), second_ref[...].astype(F32))


def add_to(ref, value):
    @pl.when(pl.program_id(0) == 0)
    def _():
        ref[...] = jnp.zeros_like(ref)

    ref[...] += value


def residual(near, moved, tok, r_mix, gain):
    rows, width = tok.shape

    def body(near_ref, moved_ref, tok_ref, r_ref, gain_ref, resid_ref, out_ref):
        branch = near_ref[...].astype(F32) + moved_ref[...].astype(F32)
        resid = tok_ref[...].astype(F32) + r_ref[...] * branch
        resid_ref[...] = resid
        r = lax.rsqrt(jnp.sum(resid * resid, axis=-1, keepdims=True) / width + EPS)
        out_ref[...] = (resid * r * gain_ref[...]).astype(BF16)

    outs = [(shape_of(rows, width), "rows"), (shape_of(rows, width, dtype=BF16), "rows")]
    ins = [(near, "rows"), (moved, "rows"), (tok, "rows"), (r_mix, "rows"), (gain, "whole")]
    return row_kernel(body, outs, ins)


def back_residual(near, moved, resid, cot, gain):
    rows, width = resid.shape

    def body(near_ref, first_ref, second_ref, resid_ref, cot_ref, gain_ref, grad_ref, out_ref, sum_ref):
        g = near_ref[...].astype(F32) + half_rows(first_ref, second_ref)
        resid = resid_ref[...]
        r = lax.rsqrt(jnp.sum(resid * resid, axis=-1, keepdims=True) / width + EPS)
        scaled = resid * r
        add_to(sum_ref, jnp.sum(g * scaled, axis=0, keepdims=True))
        g = g * gain_ref[...]
        inner = jnp.sum(resid * g, axis=-1, keepdims=True)
        grad = cot_ref[...].astype(F32) + r * g - resid * (r * r * r * inner / width)
        grad_ref[...] = grad
        out_ref[...] = grad.astype(BF16)

    outs = [
        (shape_of(rows, width), "rows"),
        (shape_of(rows, width, dtype=BF16), "rows"),
        (shape_of(1, width), "whole"),
    ]
    ins = [(near, "rows"), (moved[0], "first"), (moved[1], "second"), (resid, "rows"), (cot, "rows"), (gain, "whole")]
    return row_kernel(body, outs, ins)


def block_output(near, moved, resid, live, count):
    rows, width = resid.shape
    cols, size = width // count, rows // STEPS

    def body(near_ref, moved_ref, resid_ref, live_ref, out_ref):
        at_rows = pl.ds(pl.multiple_of(pl.program_id(0) * size, size), size)
        for k in range(count):
            at = slice(k * cols, (k + 1) * cols)
            ffn = near_ref[:, at].astype(F32) + moved_ref[:, at].astype(F32)
            out_ref[k, at_rows, :] = (live_ref[...] * (resid_ref[:, at] + ffn)).astype(BF16)

    outs = [(shape_of(count, rows, cols, dtype=BF16), "whole")]
    ins = [(near, "rows"), (moved, "rows"), (resid, "rows"), (live, "rows")]
    return row_kernel(body, outs, ins)[0]


def back_tokens(near, moved, tok, grad_resid, in_gain, mlp_sum, chan_rows):
    rows, width = tok.shape
    count, _, cols = chan_rows.shape
    size = rows // STEPS

    def body(near_ref, first_ref, second_ref, tok_ref, grad_ref, gain_ref, mlp_ref, chan_ref, out_ref, sum_ref):
        g = near_ref[...].astype(F32) + half_rows(first_ref, second_ref)
        x = tok_ref[...].astype(F32)
        r = lax.rsqrt(jnp.sum(x * x, axis=-1, keepdims=True) / width + EPS)
        add_to(sum_ref, jnp.sum(g * x * r, axis=0, keepdims=True))
        g = g * gain_ref[...]
        inner = jnp.sum(x * g, axis=-1, keepdims=True)
        grad = (grad_ref[...] + r * g - x * (r * r * r * inner / width)).astype(BF16)
        at_rows = pl.ds(pl.multiple_of(pl.program_id(0) * size, size), size)
        for k in range(count):
            out_ref[k, at_rows, :] = grad[:, k * cols : (k + 1) * cols]

        @pl.when(pl.program_id(0) == STEPS - 1)
        def _():
            place = lax.broadcasted_iota(jnp.int32, (16, cols), 0)
            for k in range(count):
                at = slice(k * cols, (k + 1) * cols)
                extra = jnp.zeros((16, cols), F32)
                for i, total in enumerate((sum_ref[:, at], mlp_ref[:, at])):
                    high = total.astype(BF16).astype(F32)
                    extra = jnp.where(place == i, high, jnp.where(place == 2 + i, total - high, extra))
                extra = jnp.where(place == 4, chan_ref[k], extra)
                out_ref[k, rows:, :] = extra.astype(BF16)

    outs = [(shape_of(count, rows + 16, cols, dtype=BF16), "whole")]
    ins = [(near, "rows"), (moved[0], "first"), (moved[1], "second"), (tok, "rows"), (grad_resid, "rows")]
    ins += [(in_gain, "whole"), (mlp_sum, "whole"), (chan_rows, "whole")]
    return row_kernel(body, outs, ins, [pltpu.VMEM((1, width), F32)])[0]


def order_rows(blocks, place):
    count = len(blocks)
    q, width = blocks[0].shape
    tile = 512

    def body(place_ref, *refs):
        out_ref = refs[count]
        for j in range(count):
            at = pl.multiple_of(lax.bitwise_xor(place_ref[0], j) * q, 16)
            out_ref[pl.ds(at, q), :] = refs[j][...].astype(F32)

    return pl.pallas_call(
        body,
        grid=(width // tile,),
        out_shape=shape_of(count * q, width),
        in_specs=[SMEM_SPEC] + [pl.BlockSpec((q, tile), lambda i: (0, i))] * count,
        out_specs=pl.BlockSpec((count * q, tile), lambda i: (0, i)),
        compiler_params=params(),
        cost_estimate=NO_COST,
    )(place, *blocks)


def turn_rows(blocks, place):
    count = len(blocks)
    q, width = blocks[0].shape
    tile = 256

    def body(place_ref, *refs):
        out_ref, held = refs[count], refs[count + 1]
        for j in range(count):
            held[lax.bitwise_xor(place_ref[0], j)] = refs[j][...].astype(F32)
        out_ref[...] = held[...].reshape(count * q, tile).T

    return pl.pallas_call(
        body,
        grid=(width // tile,),
        out_shape=shape_of(width, count * q),
        in_specs=[SMEM_SPEC] + [pl.BlockSpec((q, tile), lambda i: (0, i))] * count,
        out_specs=pl.BlockSpec((tile, count * q), lambda i: (i, 0)),
        scratch_shapes=[pltpu.VMEM((count, q, tile), F32)],
        compiler_params=params(),
        cost_estimate=NO_COST,
    )(place, *blocks)


def dot_nt(a, b):
    return lax.dot_general(a, b, (((1,), (1,)), ((), ())), preferred_element_type=F32)


def dot_nn(a, b):
    return lax.dot_general(a, b, (((1,), (0,)), ((), ())), preferred_element_type=F32)


def dot_tn(a, b):
    return lax.dot_general(a, b, (((0,), (0,)), ((), ())), preferred_element_type=F32)


def on_device(
    net,
    tokens,
    cotangent,
    lengths,
    in_gain,
    w_input,
    w_forget,
    w_output_gate,
    lower_bound,
    mix_gain,
    w_out,
    mlp_gain,
    w_gate,
    w_up,
    w_down,
):
    s, t = net.places()
    n_seq, n_tp = net.seq, net.tp
    slots, group, cols = tokens.shape
    width = cols * n_tp
    pos_n = group // n_tp
    rows = slots * pos_n
    dq = cols // n_seq
    fq = w_down.shape[0] // n_seq
    chan, hid = dq * n_tp, fq * n_tp
    place = s.reshape(1)
    order = net.order

    def quarter_t(w, q):
        return lax.dynamic_slice_in_dim(w, s * q, q, 1).T

    def by_owner(x):
        return x.reshape(slots, n_tp, pos_n, cols).transpose(1, 0, 2, 3).reshape(n_tp, rows, cols)

    def to_owner(x):
        return lax.all_to_all(x, "tp", 0, 0, tiled=True)

    def in_place(x):
        return x.reshape(n_tp, slots, pos_n, cols).transpose(1, 0, 2, 3).reshape(tokens.shape)

    where = s * group + t * pos_n + jnp.arange(pos_n, dtype=jnp.int32)
    live = (where[None, :] < lengths[:, None]).astype(F32).reshape(rows, 1)

    small = jnp.concatenate(
        [lax.dynamic_slice_in_dim(v, s * dq, dq) for v in (lower_bound, mix_gain)] + [mlp_gain], 0
    )
    terms, rest = [], small
    for _ in range(3):
        terms.append(hold(rest.astype(BF16))[0])
        rest = rest - terms[-1].astype(F32)
    terms = jnp.pad(jnp.concatenate(terms, 0), (0, 16 * cols - 3 * small.shape[0])).reshape(1, 16, cols)
    token_blocks = to_owner(jnp.concatenate([by_owner(tokens), jnp.broadcast_to(terms, (n_tp, 16, cols))], 1))
    small = token_blocks[:, rows:].reshape(n_tp, 16 * cols)[:, : 3 * small.shape[0]].astype(F32).reshape(n_tp, 3, -1)
    small = small[:, 0] + small[:, 1] + small[:, 2]
    bound = small[:, :dq].reshape(1, chan)
    gain = small[:, dq : 2 * dq].reshape(1, chan)
    mlp_full = small[:, 2 * dq :].reshape(1, width)
    mix_w = jnp.concatenate(
        [quarter_t(w, dq) for w in (w_input, w_forget, w_output_gate)]
        + [lax.dynamic_slice_in_dim(w_out, s * dq, dq, 0)],
        0,
    )
    tok, normed_own = norm_tokens(token_blocks, in_gain, rows)
    mix_ring = RingGather(net, after(mix_w, normed_own))
    mix_ring.launch(mix_ring.sends())
    normed = net.gather_rest(net.gather_first(normed_own))
    mix_ring.finish()
    w3, wo = Weights(), Weights()
    w3.add(mix_ring, [(i * dq, i * chan) for i in range(3)], dq, True)
    wo.add(mix_ring, [(3 * dq, 0)], dq, True)
    gate_ring = RingGather(net, after(quarter_t(w_gate, fq), *mix_ring.came))
    up_ring = RingGather(net, after(quarter_t(w_up, fq), *mix_ring.came))
    gate_ring.launch(gate_ring.sends())
    up_ring.launch(up_ring.sends())
    half = n_seq // 2

    pre, normed_all, decay, end = mixer_in(order, normed, w3, bound, slots, pos_n)

    def spread(pair, reverse):
        def joined(earlier, later):
            return earlier[0] * later[0], later[0] * earlier[1] + later[1]

        whole = pair
        before = (jnp.ones_like(pair[0]), jnp.zeros_like(pair[1]))
        for bit in net.tp_bits:
            moved = net.cross(jnp.stack(whole, 0), bit)
            moved = (moved[0], moved[1])
            upper = (jnp.bitwise_and(t, bit) != 0) != reverse
            ahead, behind = joined(moved, whole), joined(whole, moved)
            longer = joined(moved, before)
            before = tuple(jnp.where(upper, a, b) for a, b in zip(longer, before))
            whole = tuple(jnp.where(upper, a, b) for a, b in zip(ahead, behind))
        return before, whole

    (decay, end), gate_ring.came, up_ring.came = hold((decay, end), gate_ring.came, up_ring.came)
    head = scan_heads(place, *spread((decay, end), False), False)
    head, sends, up_sends = hold(head, gate_ring.sends(), up_ring.sends())
    gate_ring.launch(sends)
    some, far = mixer_out(order, pre, bound, gain, head, wo, pos_n, half, half)
    head_near, some = hold(head, some)
    (state, mix, squares), parts = mixer_out(order, pre, bound, gain, head_near, wo, pos_n, 0, half, some, False)
    near_far = net.quad_far_part(far)
    near_far, parts, squares, gate_ring.came = hold(near_far, parts, squares, gate_ring.came)
    moved_far = net.swap(near_far, net.bits[-1])
    up_ring.launch(up_sends)
    sum_all = net.total_far(net.total_near(jnp.sum(squares, -1).reshape(n_seq, rows)))
    near_own = net.quad_far_part(parts)
    near_own, up_ring.came, sends = hold(near_own, up_ring.came, gate_ring.sends())
    gate_ring.launch(sends)
    near_own, moved_far, sum_all, gate_ring.came, sends = hold(
        near_own, moved_far, sum_all, gate_ring.came, up_ring.sends()
    )
    up_ring.launch(sends)
    r_mix = lax.rsqrt(sum_all / width + EPS).reshape(n_seq * rows, 1)
    resid, mlp_own = residual(near_own, moved_far, tok, r_mix[:rows], mlp_full)
    mlp_in = net.gather_first(mlp_own)
    up_ring.came, mlp_own, sends = hold(up_ring.came, mlp_own, gate_ring.sends())
    gate_ring.launch(sends)
    up_ring.launch(up_ring.sends())
    gate_ring.finish()
    up_ring.finish()
    mlp_in = net.gather_rest(mlp_in, half)
    wgu = Weights()
    wgu.add(gate_ring, [(0, 0)], fq, False)
    wgu.add(up_ring, [(0, 0)], fq, False)
    down_w = lax.dynamic_slice_in_dim(w_down, s * fq, fq, 0)
    near_in, down_w, cot_sent, _ = hold(mlp_in[:half], down_w, by_owner(cotangent), (gate_ring.came, up_ring.came))

    down_ring = RingGather(net, down_w)
    down_ring.launch(down_ring.sends())
    cot_blocks = to_owner(cot_sent)
    some = feed_forward(order, near_in, wgu, 0, n_seq)
    some, far_first, down_ring.came = hold(some, mlp_in[half], down_ring.came)
    down_ring.launch(down_ring.sends())
    mlp_in = net.gather_rest(mlp_in[:half] + [far_first] + mlp_in[half + 1 :])
    hidden, slope_up, act, mlp_all = feed_forward(order, mlp_in[half:], wgu, half, n_seq, some, False)
    hidden, cot_blocks = hold(hidden, cot_blocks)
    cot = mask_rows(cot_blocks, live)
    grad_out = net.gather_first(cot)
    cot, down_ring.came = hold(cot, down_ring.came)
    down_ring.launch(down_ring.sends())
    grad_out, down_ring.came = hold(grad_out, down_ring.came)
    down_ring.launch(down_ring.sends())
    down_ring.finish()
    grad_all = jnp.concatenate(net.gather_rest(grad_out), 0)

    def to_output(blocks, turned):
        q = blocks[0].shape[0]
        if q % 16 == 0:
            return turn_rows(blocks, place) if turned else order_rows(blocks, place)
        out = jnp.zeros((n_seq, q, width), F32)
        for j in range(n_seq):
            out = lax.dynamic_update_index_in_dim(out, blocks[j].astype(F32), lax.bitwise_xor(s, j), 0)
        out = out.reshape(n_seq * q, width)
        return out.T if turned else out

    dw_down = dot_tn(hidden, grad_all).astype(BF16)
    down_sum = RingScatter(net, [dw_down], False)
    wd = Weights()
    wd.add(down_ring, [(0, 0)], fq, False)
    sends, grad_all, _ = hold(down_sum.sends(), grad_all, down_ring.came)
    down_sum.launch(sends)
    grad_gate, grad_up = back_hidden(order, grad_all, wd, slope_up, act, rows)
    grad_gate, down_sum.came = hold(grad_gate, down_sum.came)
    sends, grad_gate = hold(down_sum.sends(), grad_gate)
    down_sum.launch(sends)
    far = back_pair(order, grad_gate, grad_up, wgu, rows, half, half)
    far, down_sum.came = hold(far, down_sum.came)
    sent, sends, grad_gate = hold(net.halved(net.quad_far_part(far)), down_sum.sends(), grad_gate)
    moved = [net.swap(x, net.bits[-1]) for x in sent]
    down_sum.launch(sends)
    parts = back_pair(order, grad_gate, grad_up, wgu, rows, 0, half)
    parts, moved[0], down_sum.came = hold(parts, moved[0], down_sum.came)
    sends, grad_gate = hold(down_sum.sends(), grad_gate)
    down_sum.launch(sends)
    near_own = net.quad_far_part(parts)
    dw_gate = dot_tn(grad_gate, mlp_all).astype(BF16)
    dw_gate, moved[1], near_own, down_sum.came = hold(dw_gate, moved[1], near_own, down_sum.came)
    grad_resid, branch_own, mlp_sum = back_residual(near_own, moved, resid, cot, mlp_full)
    gate_sum = RingScatter(net, [dw_gate], False)
    branch_own, sends, sent, hidden = hold(branch_own, gate_sum.sends(), net.halved(branch_own), hidden)
    grad_branch = [[x] for x in net.gather_near(branch_own)]
    moved = [net.swap(x, net.bits[-1]) for x in sent]
    gate_sum.launch(sends)
    ffn_parts = down_parts(order, hidden, wd, rows)
    ffn_parts, moved[0], grad_branch, gate_sum.came = hold(ffn_parts, moved[0], grad_branch, gate_sum.came)
    grad_branch_a = net.gather_near(moved[0])
    down_own = down_sum.result()
    sends, grad_up = hold(gate_sum.sends(), grad_up)
    gate_sum.launch(sends)
    ffn_near = net.quad_near(ffn_parts)
    dw_up = dot_tn(grad_up, mlp_all).astype(BF16)
    dw_up, moved[1], gate_sum.came, ffn_near = hold(dw_up, moved[1], gate_sum.came, ffn_near)
    grad_branch = grad_branch + [list(x) for x in zip(grad_branch_a, net.gather_near(moved[1]))]
    up_sum = RingScatter(net, [dw_up], False)

    sends, up_sends, grad_branch, down_own = hold(gate_sum.sends(), up_sum.sends(), grad_branch, down_own)
    gate_sum.launch(sends)
    up_sum.launch(up_sends)
    down_blocks = net.gather_first(down_own)
    g_norm, grad_og, mixed_out, branch_all, inner_lanes, gain_sums = back_mixer(
        order, grad_branch, rows, wo, pre, state, mix, r_mix, gain
    )
    inner_lanes, gate_sum.came, up_sum.came, down_blocks = hold(
        inner_lanes, gate_sum.came, up_sum.came, down_blocks
    )
    sends, up_sends, inner_lanes = hold(gate_sum.sends(), up_sum.sends(), inner_lanes)
    gate_sum.launch(sends)
    up_sum.launch(up_sends)
    inner = net.total_far(net.total_near(jnp.sum(inner_lanes, -1).reshape(n_seq, rows))).reshape(-1, 1)
    ffn = net.quad_far([after(p, inner) for p in ffn_near])
    coef = r_mix**3 * inner / width
    back_end = back_ends(pre, bound, g_norm, state, r_mix, coef, slots, pos_n)
    dw_out = dot_tn(after(mixed_out, back_end), branch_all).astype(BF16)
    dw_og = dot_tn(after(grad_og, dw_out), normed_all).astype(BF16)
    back_end, gate_sum.came, up_sum.came, dw_og = hold(back_end, gate_sum.came, up_sum.came, dw_og)
    tail = scan_heads(place, *spread((decay, back_end), True), True)
    gate_own = gate_sum.result()
    tail, up_sends, gate_own = hold(tail, up_sum.sends(), gate_own)
    up_sum.launch(up_sends)

    def back(start, tail, long):
        return back_states(
            order, pre, bound, g_norm, state, grad_og, r_mix, coef, head, tail, w3, pos_n, start, half, long
        )

    (far_in, far_fg, far_low), far = back(half, tail, True)
    far, far_in, up_sum.came, ffn = hold(far, far_in, up_sum.came, ffn)
    first_sum = RingScatter(net, [dw_out, dw_og], True)
    mixed_sent = block_output(*ffn, resid, live, n_tp)
    sent, tail, up_sends, sends, mixed_sent = hold(
        net.halved(net.quad_far_part(far)), tail, up_sum.sends(), first_sum.sends(), mixed_sent
    )
    moved = [net.swap(x, net.bits[-1]) for x in sent]
    up_sum.launch(up_sends)
    first_sum.launch(sends)
    mixed_got = to_owner(mixed_sent)
    (grad_in, grad_fg, low_sums), parts = back(0, tail, True)
    parts, moved[0], first_sum.came, up_sum.came = hold(parts, moved[0], first_sum.came, up_sum.came)
    up_own = up_sum.result()
    low_sums = low_sums + far_low
    grad_in, grad_fg = (jnp.concatenate([a, b], 0) for a, b in ((grad_in, far_in), (grad_fg, far_fg)))
    sends, up_own, grad_in = hold(first_sum.sends(), up_own, grad_in)
    first_sum.launch(sends)
    near_own = net.quad_far_part(parts)
    dw_in = dot_tn(grad_in, normed_all).astype(BF16)
    dw_fg = dot_tn(after(grad_fg, dw_in), normed_all).astype(BF16)
    last_sum = RingScatter(net, [dw_in, dw_fg], True)
    last_sends, near_own, first_sum.came = hold(last_sum.sends(), near_own, first_sum.came)
    last_sum.launch(last_sends)
    first_sum.launch(first_sum.sends())
    near_own, moved = hold(near_own, moved)
    sums = jnp.stack([jnp.sum(low_sums, axis=(0, 1)), jnp.sum(gain_sums, axis=(0, 1))], 0).reshape(2, n_tp, dq)
    high = hold(sums.astype(BF16))[0].astype(F32)
    chan_rows = jnp.concatenate([high, sums - high], 0).transpose(1, 0, 2).reshape(n_tp, 1, 4 * dq)
    chan_rows = jnp.pad(chan_rows, ((0, 0), (0, 0), (0, cols - 4 * dq)))
    sent = back_tokens(near_own, moved, tok, grad_resid, in_gain.reshape(1, width), mlp_sum, chan_rows)

    sent, up_own, last_sum.came, first_sum.came = hold(sent, up_own, last_sum.came, first_sum.came)
    got = to_owner(sent)
    up_blocks, gate_blocks = net.gather_first(up_own), net.gather_first(after(gate_own, up_own))
    down_blocks = net.gather_rest([after(down_blocks[0], up_own)] + down_blocks[1:])
    grad_w_down = to_output(down_blocks, False)
    sends, last_sends = hold(first_sum.sends(), last_sum.sends())
    last_sum.launch(last_sends)
    first_sum.launch(sends)
    last_sum.came, first_sum.came, grad_w_down = hold(last_sum.came, first_sum.came, grad_w_down)
    last_sum.launch(hold(last_sum.sends())[0])
    first_own = first_sum.result()
    first_blocks = net.gather_first(first_own)
    grad_w_up = to_output(net.gather_rest(up_blocks), False)
    grad_w_gate = to_output(net.gather_rest(gate_blocks), False)
    last_sum.came, grad_w_up, grad_w_gate, got, mixed_got = hold(
        last_sum.came, grad_w_up, grad_w_gate, got, mixed_got
    )
    last_sum.launch(hold(last_sum.sends())[0])
    grad_w_gate, grad_w_up = grad_w_gate.T, grad_w_up.T
    first_blocks = net.gather_rest(first_blocks)
    grad_w_out = to_output([b[:dq] for b in first_blocks], False)
    grad_w_og = to_output([b[dq:] for b in first_blocks], True)
    last_sum.came, grad_w_out, grad_w_og = hold(last_sum.came, grad_w_out, grad_w_og)
    last_own = last_sum.result()
    last_blocks = net.gather_rest(net.gather_first(last_own))
    grad_w_in = to_output([b[:dq] for b in last_blocks], True)
    grad_w_fg = to_output([b[dq:] for b in last_blocks], True)
    mixed = in_place(mixed_got)
    sums = jnp.sum(got[:, rows : rows + 5].astype(F32), 0)
    ends = jnp.concatenate([sums[:2] + sums[2:4], sums[4:5]], 0).reshape(1, 3, cols)
    for bit in net.bits:
        ends = jnp.concatenate([ends, net.swap(ends, bit)], 0)
    mine = jnp.sum(ends[:, :2], 0)
    chans = ends[lax.bitwise_xor(s, jnp.arange(n_seq, dtype=jnp.int32)), 2, : 4 * dq].reshape(n_seq, 2, 2, dq)
    chans = chans[:, 0] + chans[:, 1]
    return (
        mixed,
        in_place(got[:, :rows]).astype(F32),
        mine[0],
        grad_w_in,
        grad_w_fg,
        grad_w_og,
        chans[:, 0].reshape(-1),
        chans[:, 1].reshape(-1),
        grad_w_out,
        mine[1],
        grad_w_gate,
        grad_w_up,
        grad_w_down,
    )


def solution(mesh):
    return jax.shard_map(
        functools.partial(on_device, Net(mesh)),
        mesh=mesh,
        in_specs=(
            P(None, "seq", "tp"),
            P(None, "seq", "tp"),
            P(),
            P(),
            P(None, "tp"),
            P(None, "tp"),
            P(None, "tp"),
            P("tp"),
            P("tp"),
            P("tp", None),
            P("tp"),
            P(None, "tp"),
            P(None, "tp"),
            P("tp", None),
        ),
        out_specs=(
            P(None, "seq", "tp"),
            P(None, "seq", "tp"),
            P("tp"),
            P(None, "tp"),
            P(None, "tp"),
            P(None, "tp"),
            P("tp"),
            P("tp"),
            P("tp", None),
            P("tp"),
            P(None, "tp"),
            P(None, "tp"),
            P("tp", None),
        ),
        check_vma=False,
    )
```

```python
import functools

import jax
import jax.numpy as jnp
import numpy as np
from jax import lax
from jax.experimental import pallas as pl
from jax.experimental.pallas import tpu as pltpu
from jax.sharding import PartitionSpec as P

EPS = 1e-06
F32, BF16 = jnp.float32, jnp.bfloat16
VMEM_LIMIT = 56 * 1024 * 1024
NO_COST = pl.CostEstimate(flops=1, bytes_accessed=1, transcendentals=0)
LONG = pl.CostEstimate(flops=10**12, bytes_accessed=10**9, transcendentals=0)


def params(**more):
    return pltpu.CompilerParams(vmem_limit_bytes=VMEM_LIMIT, **more)


def sigmoid(v):
    return 1.0 / (1.0 + jnp.exp(-v))


def fast_sigmoid(v):
    d = 1.0 + jnp.exp(jnp.minimum(-v, 80.0))
    r = pl.reciprocal(d, approx=True)
    return r * (2.0 - d * r)


def ring_of(mesh):
    count = mesh.shape["tp"]
    try:
        coords = [tuple(d.coords) for d in mesh.devices[0]]
        ys = len({c[1] for c in coords})
    except (AttributeError, TypeError):
        ys = 2 if count % 2 == 0 else 1
    zs = count // ys
    if zs * ys != count or zs % 2 or ys < 2:
        return list(range(count))
    cycle = [(z, 0) for z in range(zs)]
    for turn, z in enumerate(reversed(range(zs))):
        across = range(1, ys) if turn % 2 == 0 else reversed(range(1, ys))
        cycle += [(z, y) for y in across]
    return [z * ys + y for z, y in cycle]


class Net:
    def __init__(self, mesh):
        self.seq, self.tp = mesh.shape["seq"], mesh.shape["tp"]
        self.cycle = ring_of(mesh)
        self.bits = [1 << b for b in range(self.seq.bit_length() - 1)]
        self.tp_bits = [1 << b for b in range(self.tp.bit_length() - 1)]

    def places(self):
        s, t = lax.axis_index("seq"), lax.axis_index("tp")
        where = np.zeros(self.tp, np.int32)
        for i, index in enumerate(self.cycle):
            where[index] = i
        pos = jnp.asarray(where)[t]
        steps = [[self.cycle[(i - d) % self.tp] for d in range(self.tp)] for i in where]
        self.order = lax.dynamic_index_in_dim(jnp.asarray(np.array(steps, np.int32)), t, 0, False)
        self.behind = [self.order[d] for d in range(self.tp)]
        self.inverse = (pos - jnp.asarray(where)) % self.tp
        return s, t

    def shift(self, x, k):
        n = self.tp
        return lax.ppermute(x, "tp", [(self.cycle[i], self.cycle[(i + k) % n]) for i in range(n)])

    def cross(self, x, bit):
        return lax.ppermute(x, "tp", [(i, i ^ bit) for i in range(self.tp)])

    def swap(self, x, bit):
        return lax.ppermute(x, "seq", [(i, i ^ bit) for i in range(self.seq)])

    def halves(self, size):
        half = size // 2
        return half // 16 * 16 if size >= 32 else half

    def gather_first(self, x):
        out = [x] + [None] * (self.seq - 1)
        for bit in reversed(self.bits):
            out[bit] = self.swap(x, bit)
        return out

    def gather_rest(self, out, end=None):
        out = list(out)
        for j in range(end or self.seq):
            if out[j] is None:
                out[j] = self.swap(out[j & (j - 1)], j & -j)
        return out

    def gather_near(self, x):
        out = [x]
        for bit in self.bits[:-1]:
            out = out + [self.swap(y, bit) for y in out]
        return out

    def halved(self, x):
        half = x.shape[0] // 2
        return [x[:half], x[half:]]

    def quad_far_part(self, parts):
        parts = list(parts)
        for bit in self.bits[:-1]:
            for j in reversed(range(0, len(parts), 2 * bit)):
                moved = self.swap(parts[j ^ bit], bit)
                parts[j] = (parts[j].astype(F32) + moved.astype(F32)).astype(BF16)
        return parts[0]

    def quad_near(self, parts):
        half = self.seq // 2
        far = self.quad_far_part(parts[half:])
        return [self.quad_far_part(parts[:half]), far]

    def quad_far(self, near):
        return [near[0], self.swap(near[1], self.bits[-1])]

    def total_step(self, x, bit):
        moved = self.swap(x, bit)
        return x + jnp.stack([moved[j ^ bit] for j in range(self.seq)], 0)

    def total_near(self, x):
        for bit in self.bits[:-1]:
            x = self.total_step(x, bit)
        return x

    def total_far(self, x):
        return self.total_step(x, self.bits[-1])


def after(x, *others):
    return lax.optimization_barrier((x,) + others)[0]


def hold(*trees):
    return lax.optimization_barrier(trees)


class RingGather:
    def __init__(self, net, x):
        self.net, self.size = net, x.shape[0]
        n = net.tp
        self.blocks = [[(x, 0)]] + [None] * (n - 1)
        self.full = (n - 1) // 2
        self.made = 0
        self.came = (x, x)

    def done(self):
        return self.made == self.net.tp // 2

    def sends(self):
        if self.done():
            return ()
        fore, back = self.came
        if self.made < self.full:
            return fore, back
        half = self.net.halves(self.size)
        return fore[:half], back[half:]

    def launch(self, sends):
        if self.done():
            return
        net, n = self.net, self.net.tp
        self.made += 1
        d = self.made
        self.came = net.shift(sends[0], 1), net.shift(sends[1], -1)
        if d <= self.full:
            self.blocks[d], self.blocks[n - d] = [(self.came[0], 0)], [(self.came[1], 0)]
        else:
            self.blocks[d] = [(self.came[0], 0), (self.came[1], net.halves(self.size))]

    def finish(self):
        while not self.done():
            self.launch(self.sends())

    def rows(self, start, q):
        out = []
        for block in self.blocks:
            whole = jnp.concatenate([a for a, _ in block], 0) if len(block) > 1 else block[0][0]
            out.append(whole[start : start + q])
        return out


class RingScatter:
    def __init__(self, net, wholes, canonical):
        self.net, self.wholes, self.canonical = net, wholes, canonical
        self.sizes = [w.shape[0] // net.tp for w in wholes]
        self.size = sum(self.sizes)
        self.d = net.tp // 2
        self.came = ()
        self.half = net.halves(self.size) if net.tp % 2 == 0 else 0

    def done(self):
        return self.d == 0

    def make(self, outs):
        net = self.net
        made = []
        for d, low, high, adds in outs:
            rows = []
            for w, q in zip(self.wholes, self.sizes):
                at = net.behind[d] * q if self.canonical else d * q
                rows.append(lax.dynamic_slice_in_dim(w, at, q, 0))
            whole = jnp.concatenate(rows, 0)[low:high]
            for part, start in adds:
                first = start - low
                part = jnp.pad(part.astype(F32), ((first, high - low - first - part.shape[0]), (0, 0)))
                whole = whole.astype(F32) + part
            made.append(whole.astype(BF16))
        return made

    def adds(self, which):
        if not self.came:
            return []
        after_half = which == 1 and 2 * (self.d + 1) == self.net.tp
        return [(self.came[which], self.half if after_half else 0)]

    def sends(self):
        if self.done():
            return ()
        n, d = self.net.tp, self.d
        if 2 * d == n:
            return self.make([(d, 0, self.half, []), (d, self.half, self.size, [])])
        return self.make([(n - d, 0, self.size, self.adds(0)), (d, 0, self.size, self.adds(1))])

    def launch(self, sends):
        if self.done():
            return
        self.d -= 1
        self.came = self.net.shift(sends[0], 1), self.net.shift(sends[1], -1)

    def result(self):
        while not self.done():
            self.launch(self.sends())
        return self.make([(0, 0, self.size, self.adds(0) + self.adds(1))])[0]


SMEM_SPEC = pl.BlockSpec(memory_space=pltpu.SMEM)
VMEM_SPEC = pl.BlockSpec(memory_space=pltpu.VMEM)


def norm_tokens(blocks, gain, rows):
    count, _, cols = blocks.shape
    width = count * cols

    def body(gain_ref, in_ref, x_ref, n_ref):
        total = jnp.zeros((rows, 1), F32)
        for k in range(count):
            c = in_ref[k, :rows].astype(F32)
            total += jnp.sum(c * c, axis=-1, keepdims=True)
        r = lax.rsqrt(total / width + EPS)
        for k in range(count):
            c = in_ref[k, :rows]
            at = slice(k * cols, (k + 1) * cols)
            x_ref[:, at] = c
            n_ref[:, at] = (c.astype(F32) * r * gain_ref[:, at]).astype(BF16)

    return pl.pallas_call(
        body,
        out_shape=[jax.ShapeDtypeStruct((rows, width), BF16)] * 2,
        in_specs=[VMEM_SPEC] * 2,
        out_specs=[VMEM_SPEC] * 2,
        compiler_params=params(),
        cost_estimate=NO_COST,
    )(gain.reshape(1, width), blocks)


def mask_rows(blocks, live):
    count, rows, cols = blocks.shape
    width = count * cols

    def body(live_ref, in_ref, x_ref):
        for k in range(count):
            at = slice(k * cols, (k + 1) * cols)
            x_ref[:, at] = (in_ref[k].astype(F32) * live_ref[...]).astype(BF16)

    return pl.pallas_call(
        body,
        out_shape=jax.ShapeDtypeStruct((rows, width), BF16),
        in_specs=[VMEM_SPEC] * 2,
        out_specs=VMEM_SPEC,
        compiler_params=params(),
        cost_estimate=NO_COST,
    )(live, blocks)


def tile_scan(decay, drive):
    place = lax.broadcasted_iota(jnp.int32, decay.shape, 0)
    for step in (1, 2, 4):
        inside = place >= step
        before_decay = jnp.where(inside, pltpu.roll(decay, step, 0), 1.0)
        before_drive = jnp.where(inside, pltpu.roll(drive, step, 0), 0.0)
        drive = drive + decay * before_drive
        decay = decay * before_decay
    return decay, drive


def tile_scan_up(decay, drive):
    place = lax.broadcasted_iota(jnp.int32, decay.shape, 0)
    for step in (1, 2, 4):
        inside = place < 8 - step
        before_decay = jnp.where(inside, pltpu.roll(decay, 8 - step, 0), 1.0)
        before_drive = jnp.where(inside, pltpu.roll(drive, 8 - step, 0), 0.0)
        drive = drive + decay * before_drive
        decay = decay * before_decay
    return decay, drive


def gates(pre_in, pre_fg, bound):
    sig_f = fast_sigmoid(pre_fg)
    forget = bound + (1.0 - bound) * sig_f
    sig_in = fast_sigmoid(pre_in)
    act_in = pre_in * sig_in
    slope_in = sig_in * (1.0 + pre_in * (1.0 - sig_in))
    keep = (1.0 - bound) * (1.0 - sig_f)
    return sig_f, forget, act_in, slope_in, keep


class Weights:
    def __init__(self):
        self.arrays, self.takes, self.shapes = [], [], []

    def add(self, ring, parts, stride, canonical):
        held, n = len(self.shapes), ring.net.tp
        width = ring.blocks[0][0][0].shape[1]
        self.shapes.append((len(parts) * n * stride, width))
        if stride % 16:
            for start, at in parts:
                rows = ring.rows(start, stride)
                whole = jnp.stack(rows, 0)
                if canonical:
                    whole = whole[ring.net.inverse]
                self.takes.append((len(self.arrays), 0, n * stride, held, None, at))
                self.arrays.append(whole.reshape(n * stride, width))
            return
        seen = {id(a): i for i, a in enumerate(self.arrays)}
        for d, block in enumerate(ring.blocks):
            for array, first in block:
                if id(array) not in seen:
                    seen[id(array)] = len(self.arrays)
                    self.arrays.append(array)
                for start, at in parts:
                    low, high = max(start, first), min(start + stride, first + array.shape[0])
                    if low < high:
                        place = (d, stride) if canonical else None
                        row = at + (low - start) + (0 if canonical else d * stride)
                        self.takes.append((seen[id(array)], low - first, high - low, held, place, row))

    def copies(self, order_ref, refs, held, sems):
        out = []
        for k, (source, first, size, to, place, row) in enumerate(self.takes):
            if place is not None:
                row = pl.multiple_of(order_ref[place[0]] * place[1] + row, 16)
            out.append(
                pltpu.make_async_copy(refs[source].at[pl.ds(first, size)], held[to].at[pl.ds(row, size)], sems.at[k])
            )
        return out


def step_kernel(body, order, count, rows, blocks, weights, ins, outs, width, onto=(), long=True):
    any_spec = pl.BlockSpec(memory_space=pl.ANY)
    pieces = [(j, i, sum(a.shape[0] for a in block[:i]), a) for j, block in enumerate(blocks) for i, a in enumerate(block)]
    n_x, n_w, n_in, n_out = len(pieces), len(weights.arrays), len(ins), len(outs)
    n_part = count if width else 0
    n_held, n_onto = len(weights.shapes), len(onto)

    def kernel(order_ref, *refs):
        refs = list(refs)

        def take(k):
            out = refs[:k]
            del refs[:k]
            return out

        x_refs, w_refs, in_refs, _ = take(n_x), take(n_w), take(n_in), take(n_onto)
        out_refs, part_refs = take(n_out), take(n_part)
        held, w_sems = take(n_held), take(1)[0]
        xs, x_sems = take(2) if n_x else (None, None)
        kept, part_sems = take(2) if n_part else (None, None)
        j = pl.program_id(0)
        loads = weights.copies(order_ref, w_refs, held, w_sems)
        x_loads = [
            pltpu.make_async_copy(x_refs[k], xs.at[at, pl.ds(start, a.shape[0])], x_sems.at[k])
            for k, (at, _, start, a) in enumerate(pieces)
        ]

        @pl.when(j == 0)
        def _():
            first = [x for x, (at, _, _, _) in zip(x_loads, pieces) if at == 0]
            for load in first + loads + x_loads[len(first) :]:
                load.start()

        left = list(zip(weights.takes, loads))

        def ready(which):
            now = [x for x in left if x[0][3] == which]
            for x in now:
                left.remove(x)
            if now:

                @pl.when(j == 0)
                def _():
                    for _, load in now:
                        load.wait()

        for k in range(n_x):

            @pl.when(j == pieces[k][0])
            def _(k=k):
                x_loads[k].wait()

        x = xs[j] if n_x else None
        part = body(x, held, in_refs, out_refs, ready)
        for which in range(n_held):
            ready(which)
        stores = [pltpu.make_async_copy(kept.at[k % 2], part_refs[k], part_sems.at[k]) for k in range(n_part)]
        for k in range(n_part):

            @pl.when(j == k)
            def _(k=k):
                if k >= 2:
                    stores[k - 2].wait()
                kept[k % 2] = part
                stores[k].start()
                if k == n_part - 1:
                    for store in stores[max(k - 1, 0) :]:
                        store.wait()

    scratch = [pltpu.VMEM(shape, BF16) for shape in weights.shapes]
    scratch.append(pltpu.SemaphoreType.DMA((max(len(weights.takes), 1),)))
    if n_x:
        scratch += [pltpu.VMEM((len(blocks), rows, pieces[0][3].shape[1]), BF16), pltpu.SemaphoreType.DMA((n_x,))]
    if n_part:
        scratch += [pltpu.VMEM((2, rows, width), BF16), pltpu.SemaphoreType.DMA((n_part,))]
    out = pl.pallas_call(
        kernel,
        grid=(count,),
        out_shape=[shape for shape, _ in outs] + [jax.ShapeDtypeStruct((rows, width), BF16)] * n_part,
        in_specs=[SMEM_SPEC] + [any_spec] * (n_x + n_w) + [spec for _, spec in ins] + [any_spec] * n_onto,
        out_specs=[spec for _, spec in outs] + [any_spec] * n_part,
        input_output_aliases={1 + n_x + n_w + n_in + i: i for i in range(n_onto)},
        scratch_shapes=scratch,
        compiler_params=params(),
        cost_estimate=LONG if long else NO_COST,
    )(order, *[a for _, _, _, a in pieces], *weights.arrays, *[a for a, _ in ins], *onto)
    return list(out[:n_out]), list(out[n_out:])


def shape_of(*shape, dtype=F32):
    return jax.ShapeDtypeStruct(shape, dtype)


def by_block(rows, wide, first=0, column=0):
    return pl.BlockSpec((rows, wide), lambda b: (b + first, column))


def whole_row(wide):
    return pl.BlockSpec((1, wide), lambda b: (0, 0))


def by_slot(slots, wide, first=0):
    return pl.BlockSpec((1, slots, wide), lambda b: (b + first, 0, 0))


def columns(wide):
    return [slice(c, min(c + 256, wide)) for c in range(0, wide, 256)]


def mixer_in(order, blocks, weights, bound, slots, pos_n):
    count, (rows, depth), wide = len(blocks), blocks[0].shape, bound.shape[1]

    def body(x, held, ins, outs, ready):
        pre_ref, all_ref, decay_ref, end_ref = outs
        low = ins[0][...]
        all_ref[...] = x
        ready(0)
        pre_ref[...] = dot_nt(x, held[0][...])

        def one(i, carry):
            out = []
            for k in range(slots):
                at = pl.ds(pl.multiple_of(k * pos_n + i * 8, 8), 8)
                _, forget, act, _, keep = gates(pre_ref[at, :wide], pre_ref[at, wide : 2 * wide], low)
                decay, local = tile_scan(forget, act * keep)
                a, h = carry[k]
                out.append((a * decay[7:8, :], decay[7:8, :] * h + local[7:8, :]))
            return tuple(out)

        start = (jnp.ones((1, wide), F32), jnp.zeros((1, wide), F32))
        ends = lax.fori_loop(0, pos_n // 8, one, (start,) * slots)
        for k in range(slots):
            decay_ref[0, k : k + 1] = ends[k][0]
            end_ref[0, k : k + 1] = ends[k][1]

    outs = [
        (shape_of(count * rows, 3 * wide), by_block(rows, 3 * wide)),
        (shape_of(count * rows, depth, dtype=BF16), by_block(rows, depth)),
        (shape_of(count, slots, wide), by_slot(slots, wide)),
        (shape_of(count, slots, wide), by_slot(slots, wide)),
    ]
    return step_kernel(
        body, order, count, rows, [[x] for x in blocks], weights, [(bound, whole_row(wide))], outs, 0
    )[0]


def scan_heads(place, before, whole, reverse):
    count, slots, wide = whole[0].shape

    def body(place_ref, pa_ref, pb_ref, wa_ref, wb_ref, head_ref):
        state = jnp.zeros((slots, wide), F32)
        for i in range(count):
            j = lax.bitwise_xor(place_ref[0], count - 1 - i if reverse else i)
            head_ref[j] = pa_ref[j] * state + pb_ref[j]
            state = wa_ref[j] * state + wb_ref[j]

    return pl.pallas_call(
        body,
        out_shape=shape_of(count, slots, wide),
        in_specs=[SMEM_SPEC] + [VMEM_SPEC] * 4,
        out_specs=VMEM_SPEC,
        compiler_params=params(),
        cost_estimate=NO_COST,
    )(place, *before, *whole)


def mixer_out(order, pre, bound, gain, head, weights, pos_n, first, steps, onto=(), long=True):
    wide = bound.shape[1]
    count, slots, _ = head.shape
    rows = slots * pos_n
    depth = weights.shapes[0][1]

    def body(x, held, ins, outs, ready):
        pre_ref, bound_ref, gain_ref, head_ref = ins
        state_ref, mix_ref, sum_ref = outs
        low = bound_ref[...]

        def one(i, carry):
            out = []
            for k in range(slots):
                at = pl.ds(pl.multiple_of(k * pos_n + i * 8, 8), 8)
                _, forget, act, _, keep = gates(pre_ref[at, :wide], pre_ref[at, wide : 2 * wide], low)
                decay, local = tile_scan(forget, act * keep)
                state = local + decay * carry[k]
                state_ref[at, :] = state
                square = state * state
                sum_ref[at, :] = sum(square[:, c : c + 128] for c in range(0, wide, 128))
                out.append(state[7:8, :])
            return tuple(out)

        lax.fori_loop(0, pos_n // 8, one, tuple(head_ref[0, k : k + 1] for k in range(slots)))
        og = pre_ref[:, 2 * wide :]
        mix = (state_ref[...] * gain_ref[...] * (og * fast_sigmoid(og))).astype(BF16)
        mix_ref[...] = mix
        ready(0)
        return dot_nn(mix, held[0][...]).astype(BF16)

    ins = [
        (pre, by_block(rows, 3 * wide, first)),
        (bound, whole_row(wide)),
        (gain, whole_row(wide)),
        (head, by_slot(slots, wide, first)),
    ]
    outs = [
        (shape_of(count * rows, wide), by_block(rows, wide, first)),
        (shape_of(count * rows, wide, dtype=BF16), by_block(rows, wide, first)),
        (shape_of(count * rows, 128), by_block(rows, 128, first)),
    ]
    return step_kernel(body, order, steps, rows, [], weights, ins, outs, depth, onto, long)


def feed_forward(order, blocks, weights, first, count, onto=(), long=True):
    (rows, depth), wide = blocks[0].shape, weights.shapes[0][0]

    def body(x, held, ins, outs, ready):
        hid_ref, slope_ref, act_ref, all_ref = outs
        all_ref[...] = x
        ready(0)
        ready(1)
        for at in columns(wide):
            gate = dot_nt(x, held[0][at, :])
            up = dot_nt(x, held[1][at, :])
            sig = fast_sigmoid(gate)
            act = gate * sig
            hid_ref[:, at] = (act * up).astype(BF16)
            slope_ref[:, at] = (up * (sig * (1.0 + gate * (1.0 - sig)))).astype(BF16)
            act_ref[:, at] = act.astype(BF16)

    outs = [(shape_of(count * rows, wide, dtype=BF16), by_block(rows, wide, first))] * 3
    outs = outs + [(shape_of(count * rows, depth, dtype=BF16), by_block(rows, depth, first))]
    return step_kernel(body, order, len(blocks), rows, [[x] for x in blocks], weights, [], outs, 0, onto, long)[0]


def down_parts(order, hidden, weights, rows):
    wide, depth = weights.shapes[0]
    count = hidden.shape[0] // rows

    def body(x, held, ins, outs, ready):
        ready(0)
        return dot_nn(ins[0][...], held[0][...]).astype(BF16)

    return step_kernel(
        body, order, count, rows, [], weights, [(hidden, by_block(rows, wide))], [], depth
    )[1]


def back_hidden(order, g, weights, slope, act, rows):
    wide, depth = weights.shapes[0]
    count = g.shape[0] // rows

    def body(x, held, ins, outs, ready):
        g_ref, slope_ref, act_ref = ins
        ready(0)
        for at in columns(wide):
            hid = dot_nt(g_ref[...], held[0][at, :])
            outs[0][:, at] = (hid * slope_ref[:, at].astype(F32)).astype(BF16)
            outs[1][:, at] = (hid * act_ref[:, at].astype(F32)).astype(BF16)

    block = by_block(rows, wide)
    ins = [(g, by_block(rows, depth)), (slope, block), (act, block)]
    outs = [(shape_of(count * rows, wide, dtype=BF16), block)] * 2
    return step_kernel(body, order, count, rows, [], weights, ins, outs, 0)[0]


def back_pair(order, a, b, weights, rows, first, count):
    wide, depth = weights.shapes[0]

    def body(x, held, ins, outs, ready):
        ready(0)
        ready(1)
        return (dot_nn(ins[0][...], held[0][...]) + dot_nn(ins[1][...], held[1][...])).astype(BF16)

    block = by_block(rows, wide, first)
    return step_kernel(
        body, order, count, rows, [], weights, [(a, block), (b, block)], [], depth
    )[1]


def back_mixer(order, blocks, rows, weights, pre, state, mix, r_mix, gain):
    count, depth, wide = len(blocks), blocks[0][0].shape[1], gain.shape[1]

    def body(x, held, ins, outs, ready):
        og_ref, state_ref, mix_ref, r_ref, gain_ref = ins
        norm_ref, og_out, mix_out, all_ref, inner_ref, sum_ref = outs
        all_ref[...] = x
        ready(0)
        mix_out[...] = (mix_ref[...].astype(F32) * r_ref[...]).astype(BF16)
        g = dot_nt(x, held[0][...])
        og, state = og_ref[...], state_ref[...]
        sig = fast_sigmoid(og)
        act = og * sig
        g_state = g * (state * r_ref[...])
        sum_ref[0] = jnp.sum((g_state * act).reshape(rows // 8, 8, wide), 0)
        og_out[...] = (g_state * gain_ref[...] * (sig * (1.0 + og * (1.0 - sig)))).astype(BF16)
        norm = g * gain_ref[...] * act
        norm_ref[...] = norm
        inner = state * norm
        inner_ref[...] = sum(inner[:, c : c + 128] for c in range(0, wide, 128))

    ins = [
        (pre, pl.BlockSpec((rows, wide), lambda b: (b, 2))),
        (state, by_block(rows, wide)),
        (mix, by_block(rows, wide)),
        (r_mix, by_block(rows, 1)),
        (gain, whole_row(wide)),
    ]
    outs = [
        (shape_of(count * rows, wide), by_block(rows, wide)),
        (shape_of(count * rows, wide, dtype=BF16), by_block(rows, wide)),
        (shape_of(count * rows, wide, dtype=BF16), by_block(rows, wide)),
        (shape_of(count * rows, depth, dtype=BF16), by_block(rows, depth)),
        (shape_of(count * rows, 128), by_block(rows, 128)),
        (shape_of(count, 8, wide), by_slot(8, wide)),
    ]
    return step_kernel(body, order, count, rows, blocks, weights, ins, outs, 0)[0]


def back_ends(pre, bound, norm, state, r_mix, coef, slots, pos_n):
    wide = norm.shape[1]
    rows = slots * pos_n
    count = norm.shape[0] // rows
    tiles = pos_n // 8

    def body(fg_ref, norm_ref, state_ref, r_ref, coef_ref, bound_ref, end_ref):
        low = bound_ref[...]

        def one(i, carry):
            out = []
            for k in range(slots):
                at = pl.ds(pl.multiple_of(k * pos_n + (tiles - 1 - i) * 8, 8), 8)
                local = r_ref[at, :] * norm_ref[at, :] - coef_ref[at, :] * state_ref[at, :]
                forget = low + (1.0 - low) * fast_sigmoid(fg_ref[at, :])
                decay, part = tile_scan_up(forget, forget * local)
                out.append(decay[0:1, :] * carry[k] + part[0:1, :])
            return tuple(out)

        ends = lax.fori_loop(0, tiles, one, (jnp.zeros((1, wide), F32),) * slots)
        for k in range(slots):
            end_ref[0, k : k + 1] = ends[k]

    block = by_block(rows, wide)
    return pl.pallas_call(
        body,
        grid=(count,),
        out_shape=shape_of(count, slots, wide),
        in_specs=[
            pl.BlockSpec((rows, wide), lambda b: (b, 1)),
            block,
            block,
            by_block(rows, 1),
            by_block(rows, 1),
            whole_row(wide),
        ],
        out_specs=by_slot(slots, wide),
        compiler_params=params(),
        cost_estimate=NO_COST,
    )(pre, norm, state, r_mix, coef, bound)


def back_states(order, pre, bound, norm, state, g_og, r_mix, coef, head, tail, weights, pos_n, first, count, long=True):
    wide = norm.shape[1]
    slots = head.shape[1]
    rows = slots * pos_n
    pairs = pos_n // 16
    depth = weights.shapes[0][1]

    def body(x, held, ins, outs, ready):
        in_ref, fg_ref, bound_ref, norm_ref, state_ref, og_ref, r_ref, coef_ref, head_ref, tail_ref = ins
        gin_ref, gfg_ref, low_ref = outs
        low = bound_ref[...]
        place = lax.broadcasted_iota(jnp.int32, (8, wide), 0)
        low_ref[0] = jnp.zeros((8, wide), F32)

        def half(k, tile, g):
            at = pl.ds(pl.multiple_of(k * pos_n + tile * 8, 8), 8)
            sig_f, forget, act, slope, keep = gates(in_ref[at, :], fg_ref[at, :], low)
            now = state_ref[at, :]
            local = r_ref[at, :] * norm_ref[at, :] - coef_ref[at, :] * now
            decay, part = tile_scan_up(forget, forget * local)
            whole = part + decay * g
            g_state = local + jnp.where(place == 7, g, pltpu.roll(whole, 7, 0))
            last = jnp.maximum(k * pos_n + tile * 8 - 1, 0)
            entry = jnp.where(tile == 0, head_ref[0, k : k + 1], state_ref[pl.ds(last, 1), :])
            before = jnp.where(place == 0, entry, pltpu.roll(now, 1, 0))
            g_forget = g_state * (before - act)
            return g_state * keep * slope, g_forget * keep * sig_f, whole[0:1, :], g_forget * (1.0 - sig_f)

        def one(i, carry):
            pair = pairs - 1 - i
            out, total = [], low_ref[0]
            for k in range(slots):
                in_2, fg_2, g, low_2 = half(k, 2 * pair + 1, carry[k])
                in_1, fg_1, g, low_1 = half(k, 2 * pair, g)
                at = pl.ds(pl.multiple_of(k * pos_n + pair * 16, 16), 16)
                gin_ref[at, :] = jnp.concatenate([in_1, in_2], 0).astype(BF16)
                gfg_ref[at, :] = jnp.concatenate([fg_1, fg_2], 0).astype(BF16)
                total = total + low_1 + low_2
                out.append(g)
            low_ref[0] = total
            return tuple(out)

        lax.fori_loop(0, pairs, one, tuple(tail_ref[0, k : k + 1] for k in range(slots)))
        ready(0)
        part = dot_nn(gin_ref[...], held[0][:wide]) + dot_nn(gfg_ref[...], held[0][wide : 2 * wide])
        return (part + dot_nn(og_ref[...], held[0][2 * wide :])).astype(BF16)

    block, edge, one_lane = by_block(rows, wide, first), by_slot(slots, wide, first), by_block(rows, 1, first)
    ins = [
        (pre, block),
        (pre, by_block(rows, wide, first, 1)),
        (bound, whole_row(wide)),
        (norm, block),
        (state, block),
        (g_og, block),
        (r_mix, one_lane),
        (coef, one_lane),
        (head, edge),
        (tail, edge),
    ]
    outs = [(shape_of(count * rows, wide, dtype=BF16), by_block(rows, wide))] * 2
    outs = outs + [(shape_of(count, 8, wide), by_slot(8, wide))]
    return step_kernel(body, order, count, rows, [], weights, ins, outs, depth, (), long)


STEPS = 4


def row_kernel(body, outs, ins, scratch=()):
    def spec(a, kind):
        if kind == "whole":
            return pl.BlockSpec(a.shape, lambda i: (0,) * len(a.shape))
        if kind == "rows":
            return pl.BlockSpec((a.shape[0] // STEPS,) + a.shape[1:], lambda i: (i, 0))
        size = a.shape[0] // (STEPS // 2)
        if kind == "first":
            return pl.BlockSpec((size,) + a.shape[1:], lambda i: (jnp.minimum(i, STEPS // 2 - 1), 0))
        return pl.BlockSpec((size,) + a.shape[1:], lambda i: (jnp.maximum(i - STEPS // 2, 0), 0))

    return pl.pallas_call(
        body,
        grid=(STEPS,),
        out_shape=[a for a, _ in outs],
        in_specs=[spec(*x) for x in ins],
        out_specs=[spec(*x) for x in outs],
        scratch_shapes=scratch,
        compiler_params=params(),
        cost_estimate=NO_COST,
    )(*[a for a, _ in ins])


def half_rows(first_ref, second_ref):
    early = pl.program_id(0) < STEPS // 2
    return jnp.where(early, first_ref[...].astype(F32), second_ref[...].astype(F32))


def add_to(ref, value):
    @pl.when(pl.program_id(0) == 0)
    def _():
        ref[...] = jnp.zeros_like(ref)

    ref[...] += value


def residual(near, moved, tok, r_mix, gain):
    rows, width = tok.shape

    def body(near_ref, moved_ref, tok_ref, r_ref, gain_ref, resid_ref, out_ref):
        branch = near_ref[...].astype(F32) + moved_ref[...].astype(F32)
        resid = tok_ref[...].astype(F32) + r_ref[...] * branch
        resid_ref[...] = resid
        r = lax.rsqrt(jnp.sum(resid * resid, axis=-1, keepdims=True) / width + EPS)
        out_ref[...] = (resid * r * gain_ref[...]).astype(BF16)

    outs = [(shape_of(rows, width), "rows"), (shape_of(rows, width, dtype=BF16), "rows")]
    ins = [(near, "rows"), (moved, "rows"), (tok, "rows"), (r_mix, "rows"), (gain, "whole")]
    return row_kernel(body, outs, ins)


def back_residual(near, moved, resid, cot, gain):
    rows, width = resid.shape

    def body(near_ref, first_ref, second_ref, resid_ref, cot_ref, gain_ref, grad_ref, out_ref, sum_ref):
        g = near_ref[...].astype(F32) + half_rows(first_ref, second_ref)
        resid = resid_ref[...]
        r = lax.rsqrt(jnp.sum(resid * resid, axis=-1, keepdims=True) / width + EPS)
        scaled = resid * r
        add_to(sum_ref, jnp.sum(g * scaled, axis=0, keepdims=True))
        g = g * gain_ref[...]
        inner = jnp.sum(resid * g, axis=-1, keepdims=True)
        grad = cot_ref[...].astype(F32) + r * g - resid * (r * r * r * inner / width)
        grad_ref[...] = grad
        out_ref[...] = grad.astype(BF16)

    outs = [
        (shape_of(rows, width), "rows"),
        (shape_of(rows, width, dtype=BF16), "rows"),
        (shape_of(1, width), "whole"),
    ]
    ins = [(near, "rows"), (moved[0], "first"), (moved[1], "second"), (resid, "rows"), (cot, "rows"), (gain, "whole")]
    return row_kernel(body, outs, ins)


def block_output(near, moved, resid, live, count):
    rows, width = resid.shape
    cols, size = width // count, rows // STEPS

    def body(near_ref, moved_ref, resid_ref, live_ref, out_ref):
        at_rows = pl.ds(pl.multiple_of(pl.program_id(0) * size, size), size)
        for k in range(count):
            at = slice(k * cols, (k + 1) * cols)
            ffn = near_ref[:, at].astype(F32) + moved_ref[:, at].astype(F32)
            out_ref[k, at_rows, :] = (live_ref[...] * (resid_ref[:, at] + ffn)).astype(BF16)

    outs = [(shape_of(count, rows, cols, dtype=BF16), "whole")]
    ins = [(near, "rows"), (moved, "rows"), (resid, "rows"), (live, "rows")]
    return row_kernel(body, outs, ins)[0]


def back_tokens(near, moved, tok, grad_resid, in_gain, mlp_sum, chan_rows):
    rows, width = tok.shape
    count, _, cols = chan_rows.shape
    size = rows // STEPS

    def body(near_ref, first_ref, second_ref, tok_ref, grad_ref, gain_ref, mlp_ref, chan_ref, out_ref, sum_ref):
        g = near_ref[...].astype(F32) + half_rows(first_ref, second_ref)
        x = tok_ref[...].astype(F32)
        r = lax.rsqrt(jnp.sum(x * x, axis=-1, keepdims=True) / width + EPS)
        add_to(sum_ref, jnp.sum(g * x * r, axis=0, keepdims=True))
        g = g * gain_ref[...]
        inner = jnp.sum(x * g, axis=-1, keepdims=True)
        grad = (grad_ref[...] + r * g - x * (r * r * r * inner / width)).astype(BF16)
        at_rows = pl.ds(pl.multiple_of(pl.program_id(0) * size, size), size)
        for k in range(count):
            out_ref[k, at_rows, :] = grad[:, k * cols : (k + 1) * cols]

        @pl.when(pl.program_id(0) == STEPS - 1)
        def _():
            place = lax.broadcasted_iota(jnp.int32, (16, cols), 0)
            for k in range(count):
                at = slice(k * cols, (k + 1) * cols)
                extra = jnp.zeros((16, cols), F32)
                for i, total in enumerate((sum_ref[:, at], mlp_ref[:, at])):
                    high = total.astype(BF16).astype(F32)
                    extra = jnp.where(place == i, high, jnp.where(place == 2 + i, total - high, extra))
                extra = jnp.where(place == 4, chan_ref[k], extra)
                out_ref[k, rows:, :] = extra.astype(BF16)

    outs = [(shape_of(count, rows + 16, cols, dtype=BF16), "whole")]
    ins = [(near, "rows"), (moved[0], "first"), (moved[1], "second"), (tok, "rows"), (grad_resid, "rows")]
    ins += [(in_gain, "whole"), (mlp_sum, "whole"), (chan_rows, "whole")]
    return row_kernel(body, outs, ins, [pltpu.VMEM((1, width), F32)])[0]


def order_rows(blocks, place):
    count = len(blocks)
    q, width = blocks[0].shape
    tile = 512

    def body(place_ref, *refs):
        out_ref = refs[count]
        for j in range(count):
            at = pl.multiple_of(lax.bitwise_xor(place_ref[0], j) * q, 16)
            out_ref[pl.ds(at, q), :] = refs[j][...].astype(F32)

    return pl.pallas_call(
        body,
        grid=(width // tile,),
        out_shape=shape_of(count * q, width),
        in_specs=[SMEM_SPEC] + [pl.BlockSpec((q, tile), lambda i: (0, i))] * count,
        out_specs=pl.BlockSpec((count * q, tile), lambda i: (0, i)),
        compiler_params=params(),
        cost_estimate=NO_COST,
    )(place, *blocks)


def turn_rows(blocks, place):
    count = len(blocks)
    q, width = blocks[0].shape
    tile = 256

    def body(place_ref, *refs):
        out_ref, held = refs[count], refs[count + 1]
        for j in range(count):
            held[lax.bitwise_xor(place_ref[0], j)] = refs[j][...].astype(F32)
        out_ref[...] = held[...].reshape(count * q, tile).T

    return pl.pallas_call(
        body,
        grid=(width // tile,),
        out_shape=shape_of(width, count * q),
        in_specs=[SMEM_SPEC] + [pl.BlockSpec((q, tile), lambda i: (0, i))] * count,
        out_specs=pl.BlockSpec((tile, count * q), lambda i: (i, 0)),
        scratch_shapes=[pltpu.VMEM((count, q, tile), F32)],
        compiler_params=params(),
        cost_estimate=NO_COST,
    )(place, *blocks)


def dot_nt(a, b):
    return lax.dot_general(a, b, (((1,), (1,)), ((), ())), preferred_element_type=F32)


def dot_nn(a, b):
    return lax.dot_general(a, b, (((1,), (0,)), ((), ())), preferred_element_type=F32)


def dot_tn(a, b):
    return lax.dot_general(a, b, (((0,), (0,)), ((), ())), preferred_element_type=F32)


def on_device(
    net,
    tokens,
    cotangent,
    lengths,
    in_gain,
    w_input,
    w_forget,
    w_output_gate,
    lower_bound,
    mix_gain,
    w_out,
    mlp_gain,
    w_gate,
    w_up,
    w_down,
):
    s, t = net.places()
    n_seq, n_tp = net.seq, net.tp
    slots, group, cols = tokens.shape
    width = cols * n_tp
    pos_n = group // n_tp
    rows = slots * pos_n
    dq = cols // n_seq
    fq = w_down.shape[0] // n_seq
    chan, hid = dq * n_tp, fq * n_tp
    place = s.reshape(1)
    order = net.order

    def quarter_t(w, q):
        return lax.dynamic_slice_in_dim(w, s * q, q, 1).T

    def by_owner(x):
        return x.reshape(slots, n_tp, pos_n, cols).transpose(1, 0, 2, 3).reshape(n_tp, rows, cols)

    def to_owner(x):
        return lax.all_to_all(x, "tp", 0, 0, tiled=True)

    def in_place(x):
        return x.reshape(n_tp, slots, pos_n, cols).transpose(1, 0, 2, 3).reshape(tokens.shape)

    where = s * group + t * pos_n + jnp.arange(pos_n, dtype=jnp.int32)
    live = (where[None, :] < lengths[:, None]).astype(F32).reshape(rows, 1)

    small = jnp.concatenate(
        [lax.dynamic_slice_in_dim(v, s * dq, dq) for v in (lower_bound, mix_gain)] + [mlp_gain], 0
    )
    terms, rest = [], small
    for _ in range(3):
        terms.append(hold(rest.astype(BF16))[0])
        rest = rest - terms[-1].astype(F32)
    terms = jnp.pad(jnp.concatenate(terms, 0), (0, 16 * cols - 3 * small.shape[0])).reshape(1, 16, cols)
    token_blocks = to_owner(jnp.concatenate([by_owner(tokens), jnp.broadcast_to(terms, (n_tp, 16, cols))], 1))
    small = token_blocks[:, rows:].reshape(n_tp, 16 * cols)[:, : 3 * small.shape[0]].astype(F32).reshape(n_tp, 3, -1)
    small = small[:, 0] + small[:, 1] + small[:, 2]
    bound = small[:, :dq].reshape(1, chan)
    gain = small[:, dq : 2 * dq].reshape(1, chan)
    mlp_full = small[:, 2 * dq :].reshape(1, width)
    mix_w = jnp.concatenate(
        [quarter_t(w, dq) for w in (w_input, w_forget, w_output_gate)]
        + [lax.dynamic_slice_in_dim(w_out, s * dq, dq, 0)],
        0,
    )
    tok, normed_own = norm_tokens(token_blocks, in_gain, rows)
    mix_ring = RingGather(net, after(mix_w, normed_own))
    mix_ring.launch(mix_ring.sends())
    normed = net.gather_rest(net.gather_first(normed_own))
    mix_ring.finish()
    w3, wo = Weights(), Weights()
    w3.add(mix_ring, [(i * dq, i * chan) for i in range(3)], dq, True)
    wo.add(mix_ring, [(3 * dq, 0)], dq, True)
    gate_ring = RingGather(net, after(quarter_t(w_gate, fq), *mix_ring.came))
    up_ring = RingGather(net, after(quarter_t(w_up, fq), *mix_ring.came))
    gate_ring.launch(gate_ring.sends())
    up_ring.launch(up_ring.sends())
    half = n_seq // 2

    pre, normed_all, decay, end = mixer_in(order, normed, w3, bound, slots, pos_n)

    def spread(pair, reverse):
        def joined(earlier, later):
            return earlier[0] * later[0], later[0] * earlier[1] + later[1]

        whole = pair
        before = (jnp.ones_like(pair[0]), jnp.zeros_like(pair[1]))
        for bit in net.tp_bits:
            moved = net.cross(jnp.stack(whole, 0), bit)
            moved = (moved[0], moved[1])
            upper = (jnp.bitwise_and(t, bit) != 0) != reverse
            ahead, behind = joined(moved, whole), joined(whole, moved)
            longer = joined(moved, before)
            before = tuple(jnp.where(upper, a, b) for a, b in zip(longer, before))
            whole = tuple(jnp.where(upper, a, b) for a, b in zip(ahead, behind))
        return before, whole

    (decay, end), gate_ring.came, up_ring.came = hold((decay, end), gate_ring.came, up_ring.came)
    head = scan_heads(place, *spread((decay, end), False), False)
    head, sends, up_sends = hold(head, gate_ring.sends(), up_ring.sends())
    gate_ring.launch(sends)
    some, far = mixer_out(order, pre, bound, gain, head, wo, pos_n, half, half)
    head_near, some = hold(head, some)
    (state, mix, squares), parts = mixer_out(order, pre, bound, gain, head_near, wo, pos_n, 0, half, some, False)
    near_far = net.quad_far_part(far)
    near_far, parts, squares, gate_ring.came = hold(near_far, parts, squares, gate_ring.came)
    moved_far = net.swap(near_far, net.bits[-1])
    up_ring.launch(up_sends)
    sum_all = net.total_far(net.total_near(jnp.sum(squares, -1).reshape(n_seq, rows)))
    near_own = net.quad_far_part(parts)
    near_own, up_ring.came, sends = hold(near_own, up_ring.came, gate_ring.sends())
    gate_ring.launch(sends)
    near_own, moved_far, sum_all, gate_ring.came, sends = hold(
        near_own, moved_far, sum_all, gate_ring.came, up_ring.sends()
    )
    up_ring.launch(sends)
    r_mix = lax.rsqrt(sum_all / width + EPS).reshape(n_seq * rows, 1)
    resid, mlp_own = residual(near_own, moved_far, tok, r_mix[:rows], mlp_full)
    mlp_in = net.gather_first(mlp_own)
    up_ring.came, mlp_own, sends = hold(up_ring.came, mlp_own, gate_ring.sends())
    gate_ring.launch(sends)
    up_ring.launch(up_ring.sends())
    gate_ring.finish()
    up_ring.finish()
    mlp_in = net.gather_rest(mlp_in, half)
    wgu = Weights()
    wgu.add(gate_ring, [(0, 0)], fq, False)
    wgu.add(up_ring, [(0, 0)], fq, False)
    down_w = lax.dynamic_slice_in_dim(w_down, s * fq, fq, 0)
    near_in, down_w, cot_sent, _ = hold(mlp_in[:half], down_w, by_owner(cotangent), (gate_ring.came, up_ring.came))

    down_ring = RingGather(net, down_w)
    down_ring.launch(down_ring.sends())
    cot_blocks = to_owner(cot_sent)
    some = feed_forward(order, near_in, wgu, 0, n_seq)
    some, far_first, down_ring.came = hold(some, mlp_in[half], down_ring.came)
    down_ring.launch(down_ring.sends())
    mlp_in = net.gather_rest(mlp_in[:half] + [far_first] + mlp_in[half + 1 :])
    hidden, slope_up, act, mlp_all = feed_forward(order, mlp_in[half:], wgu, half, n_seq, some, False)
    hidden, cot_blocks = hold(hidden, cot_blocks)
    cot = mask_rows(cot_blocks, live)
    grad_out = net.gather_first(cot)
    cot, down_ring.came = hold(cot, down_ring.came)
    down_ring.launch(down_ring.sends())
    grad_out, down_ring.came = hold(grad_out, down_ring.came)
    down_ring.launch(down_ring.sends())
    down_ring.finish()
    grad_all = jnp.concatenate(net.gather_rest(grad_out), 0)

    def to_output(blocks, turned):
        q = blocks[0].shape[0]
        if q % 16 == 0:
            return turn_rows(blocks, place) if turned else order_rows(blocks, place)
        out = jnp.zeros((n_seq, q, width), F32)
        for j in range(n_seq):
            out = lax.dynamic_update_index_in_dim(out, blocks[j].astype(F32), lax.bitwise_xor(s, j), 0)
        out = out.reshape(n_seq * q, width)
        return out.T if turned else out

    dw_down = dot_tn(hidden, grad_all).astype(BF16)
    down_sum = RingScatter(net, [dw_down], False)
    wd = Weights()
    wd.add(down_ring, [(0, 0)], fq, False)
    sends, grad_all, _ = hold(down_sum.sends(), grad_all, down_ring.came)
    down_sum.launch(sends)
    grad_gate, grad_up = back_hidden(order, grad_all, wd, slope_up, act, rows)
    grad_gate, down_sum.came = hold(grad_gate, down_sum.came)
    sends, grad_gate = hold(down_sum.sends(), grad_gate)
    down_sum.launch(sends)
    far = back_pair(order, grad_gate, grad_up, wgu, rows, half, half)
    far, down_sum.came = hold(far, down_sum.came)
    sent, sends, grad_gate = hold(net.halved(net.quad_far_part(far)), down_sum.sends(), grad_gate)
    moved = [net.swap(x, net.bits[-1]) for x in sent]
    down_sum.launch(sends)
    parts = back_pair(order, grad_gate, grad_up, wgu, rows, 0, half)
    parts, moved[0], down_sum.came = hold(parts, moved[0], down_sum.came)
    sends, grad_gate = hold(down_sum.sends(), grad_gate)
    down_sum.launch(sends)
    near_own = net.quad_far_part(parts)
    dw_gate = dot_tn(grad_gate, mlp_all).astype(BF16)
    dw_gate, moved[1], near_own, down_sum.came = hold(dw_gate, moved[1], near_own, down_sum.came)
    grad_resid, branch_own, mlp_sum = back_residual(near_own, moved, resid, cot, mlp_full)
    gate_sum = RingScatter(net, [dw_gate], False)
    branch_own, sends, sent, hidden = hold(branch_own, gate_sum.sends(), net.halved(branch_own), hidden)
    grad_branch = [[x] for x in net.gather_near(branch_own)]
    moved = [net.swap(x, net.bits[-1]) for x in sent]
    gate_sum.launch(sends)
    ffn_parts = down_parts(order, hidden, wd, rows)
    ffn_parts, moved[0], grad_branch, gate_sum.came = hold(ffn_parts, moved[0], grad_branch, gate_sum.came)
    grad_branch_a = net.gather_near(moved[0])
    down_own = down_sum.result()
    sends, grad_up = hold(gate_sum.sends(), grad_up)
    gate_sum.launch(sends)
    ffn_near = net.quad_near(ffn_parts)
    dw_up = dot_tn(grad_up, mlp_all).astype(BF16)
    dw_up, moved[1], gate_sum.came, ffn_near = hold(dw_up, moved[1], gate_sum.came, ffn_near)
    grad_branch = grad_branch + [list(x) for x in zip(grad_branch_a, net.gather_near(moved[1]))]
    up_sum = RingScatter(net, [dw_up], False)

    sends, up_sends, grad_branch, down_own = hold(gate_sum.sends(), up_sum.sends(), grad_branch, down_own)
    gate_sum.launch(sends)
    up_sum.launch(up_sends)
    down_blocks = net.gather_first(down_own)
    g_norm, grad_og, mixed_out, branch_all, inner_lanes, gain_sums = back_mixer(
        order, grad_branch, rows, wo, pre, state, mix, r_mix, gain
    )
    inner_lanes, gate_sum.came, up_sum.came, down_blocks = hold(
        inner_lanes, gate_sum.came, up_sum.came, down_blocks
    )
    sends, up_sends, inner_lanes = hold(gate_sum.sends(), up_sum.sends(), inner_lanes)
    gate_sum.launch(sends)
    up_sum.launch(up_sends)
    inner = net.total_far(net.total_near(jnp.sum(inner_lanes, -1).reshape(n_seq, rows))).reshape(-1, 1)
    ffn = net.quad_far([after(p, inner) for p in ffn_near])
    coef = r_mix**3 * inner / width
    back_end = back_ends(pre, bound, g_norm, state, r_mix, coef, slots, pos_n)
    dw_out = dot_tn(after(mixed_out, back_end), branch_all).astype(BF16)
    dw_og = dot_tn(after(grad_og, dw_out), normed_all).astype(BF16)
    back_end, gate_sum.came, up_sum.came, dw_og = hold(back_end, gate_sum.came, up_sum.came, dw_og)
    tail = scan_heads(place, *spread((decay, back_end), True), True)
    gate_own = gate_sum.result()
    first_sum = RingScatter(net, [dw_out, dw_og], True)
    tail, up_sends, sends, gate_own = hold(tail, up_sum.sends(), first_sum.sends(), gate_own)
    up_sum.launch(up_sends)
    first_sum.launch(sends)

    def back(start, tail, long):
        return back_states(
            order, pre, bound, g_norm, state, grad_og, r_mix, coef, head, tail, w3, pos_n, start, half, long
        )

    (far_in, far_fg, far_low), far = back(half, tail, True)
    far, far_in, up_sum.came, first_sum.came, ffn = hold(far, far_in, up_sum.came, first_sum.came, ffn)
    mixed_sent = block_output(*ffn, resid, live, n_tp)
    sent, tail, up_sends, sends, mixed_sent = hold(
        net.halved(net.quad_far_part(far)), tail, up_sum.sends(), first_sum.sends(), mixed_sent
    )
    moved = [net.swap(x, net.bits[-1]) for x in sent]
    up_sum.launch(up_sends)
    first_sum.launch(sends)
    mixed_got = to_owner(mixed_sent)
    (grad_in, grad_fg, low_sums), parts = back(0, tail, True)
    parts, moved[0], first_sum.came, up_sum.came = hold(parts, moved[0], first_sum.came, up_sum.came)
    up_own = up_sum.result()
    low_sums = low_sums + far_low
    grad_in, grad_fg = (jnp.concatenate([a, b], 0) for a, b in ((grad_in, far_in), (grad_fg, far_fg)))
    sends, up_own, grad_in = hold(first_sum.sends(), up_own, grad_in)
    first_sum.launch(sends)
    near_own = net.quad_far_part(parts)
    dw_in = dot_tn(grad_in, normed_all).astype(BF16)
    dw_fg = dot_tn(after(grad_fg, dw_in), normed_all).astype(BF16)
    last_sum = RingScatter(net, [dw_in, dw_fg], True)
    last_sends, near_own, first_sum.came = hold(last_sum.sends(), near_own, first_sum.came)
    last_sum.launch(last_sends)
    first_sum.launch(first_sum.sends())
    near_own, moved = hold(near_own, moved)
    sums = jnp.stack([jnp.sum(low_sums, axis=(0, 1)), jnp.sum(gain_sums, axis=(0, 1))], 0).reshape(2, n_tp, dq)
    high = hold(sums.astype(BF16))[0].astype(F32)
    chan_rows = jnp.concatenate([high, sums - high], 0).transpose(1, 0, 2).reshape(n_tp, 1, 4 * dq)
    chan_rows = jnp.pad(chan_rows, ((0, 0), (0, 0), (0, cols - 4 * dq)))
    sent = back_tokens(near_own, moved, tok, grad_resid, in_gain.reshape(1, width), mlp_sum, chan_rows)

    sent, up_own, last_sum.came, first_sum.came = hold(sent, up_own, last_sum.came, first_sum.came)
    got = to_owner(sent)
    up_blocks, gate_blocks = net.gather_first(up_own), net.gather_first(after(gate_own, up_own))
    down_blocks = net.gather_rest([after(down_blocks[0], up_own)] + down_blocks[1:])
    grad_w_down = to_output(down_blocks, False)
    sends, last_sends = hold(first_sum.sends(), last_sum.sends())
    last_sum.launch(last_sends)
    first_sum.launch(sends)
    last_sum.came, first_sum.came, grad_w_down = hold(last_sum.came, first_sum.came, grad_w_down)
    last_sum.launch(hold(last_sum.sends())[0])
    first_own = first_sum.result()
    first_blocks = net.gather_first(first_own)
    grad_w_up = to_output(net.gather_rest(up_blocks), False)
    grad_w_gate = to_output(net.gather_rest(gate_blocks), False)
    last_sum.came, grad_w_up, grad_w_gate, got, mixed_got = hold(
        last_sum.came, grad_w_up, grad_w_gate, got, mixed_got
    )
    last_sum.launch(hold(last_sum.sends())[0])
    grad_w_gate, grad_w_up = grad_w_gate.T, grad_w_up.T
    first_blocks = net.gather_rest(first_blocks)
    grad_w_out = to_output([b[:dq] for b in first_blocks], False)
    grad_w_og = to_output([b[dq:] for b in first_blocks], True)
    last_sum.came, grad_w_out, grad_w_og = hold(last_sum.came, grad_w_out, grad_w_og)
    last_own = last_sum.result()
    last_blocks = net.gather_rest(net.gather_first(last_own))
    grad_w_in = to_output([b[:dq] for b in last_blocks], True)
    grad_w_fg = to_output([b[dq:] for b in last_blocks], True)
    mixed = in_place(mixed_got)
    sums = jnp.sum(got[:, rows : rows + 5].astype(F32), 0)
    ends = jnp.concatenate([sums[:2] + sums[2:4], sums[4:5]], 0).reshape(1, 3, cols)
    for bit in net.bits:
        ends = jnp.concatenate([ends, net.swap(ends, bit)], 0)
    mine = jnp.sum(ends[:, :2], 0)
    chans = ends[lax.bitwise_xor(s, jnp.arange(n_seq, dtype=jnp.int32)), 2, : 4 * dq].reshape(n_seq, 2, 2, dq)
    chans = chans[:, 0] + chans[:, 1]
    return (
        mixed,
        in_place(got[:, :rows]).astype(F32),
        mine[0],
        grad_w_in,
        grad_w_fg,
        grad_w_og,
        chans[:, 0].reshape(-1),
        chans[:, 1].reshape(-1),
        grad_w_out,
        mine[1],
        grad_w_gate,
        grad_w_up,
        grad_w_down,
    )


def solution(mesh):
    return jax.shard_map(
        functools.partial(on_device, Net(mesh)),
        mesh=mesh,
        in_specs=(
            P(None, "seq", "tp"),
            P(None, "seq", "tp"),
            P(),
            P(),
            P(None, "tp"),
            P(None, "tp"),
            P(None, "tp"),
            P("tp"),
            P("tp"),
            P("tp", None),
            P("tp"),
            P(None, "tp"),
            P(None, "tp"),
            P("tp", None),
        ),
        out_specs=(
            P(None, "seq", "tp"),
            P(None, "seq", "tp"),
            P("tp"),
            P(None, "tp"),
            P(None, "tp"),
            P(None, "tp"),
            P("tp"),
            P("tp"),
            P("tp", None),
            P("tp"),
            P(None, "tp"),
            P(None, "tp"),
            P("tp", None),
        ),
        check_vma=False,
    )
```

```python
import functools

import jax
import jax.numpy as jnp
import numpy as np
from jax import lax
from jax.experimental import pallas as pl
from jax.experimental.pallas import tpu as pltpu
from jax.sharding import PartitionSpec as P

EPS = 1e-06
F32, BF16 = jnp.float32, jnp.bfloat16
VMEM_LIMIT = 56 * 1024 * 1024
NO_COST = pl.CostEstimate(flops=1, bytes_accessed=1, transcendentals=0)
LONG = pl.CostEstimate(flops=10**12, bytes_accessed=10**9, transcendentals=0)


def params(**more):
    return pltpu.CompilerParams(vmem_limit_bytes=VMEM_LIMIT, **more)


def sigmoid(v):
    return 1.0 / (1.0 + jnp.exp(-v))


def fast_sigmoid(v):
    d = 1.0 + jnp.exp(jnp.minimum(-v, 80.0))
    r = pl.reciprocal(d, approx=True)
    return r * (2.0 - d * r)


def ring_of(mesh):
    count = mesh.shape["tp"]
    try:
        coords = [tuple(d.coords) for d in mesh.devices[0]]
        ys = len({c[1] for c in coords})
    except (AttributeError, TypeError):
        ys = 2 if count % 2 == 0 else 1
    zs = count // ys
    if zs * ys != count or zs % 2 or ys < 2:
        return list(range(count))
    cycle = [(z, 0) for z in range(zs)]
    for turn, z in enumerate(reversed(range(zs))):
        across = range(1, ys) if turn % 2 == 0 else reversed(range(1, ys))
        cycle += [(z, y) for y in across]
    return [z * ys + y for z, y in cycle]


class Net:
    def __init__(self, mesh):
        self.seq, self.tp = mesh.shape["seq"], mesh.shape["tp"]
        self.cycle = ring_of(mesh)
        self.bits = [1 << b for b in range(self.seq.bit_length() - 1)]
        self.tp_bits = [1 << b for b in range(self.tp.bit_length() - 1)]

    def places(self):
        s, t = lax.axis_index("seq"), lax.axis_index("tp")
        where = np.zeros(self.tp, np.int32)
        for i, index in enumerate(self.cycle):
            where[index] = i
        pos = jnp.asarray(where)[t]
        steps = [[self.cycle[(i - d) % self.tp] for d in range(self.tp)] for i in where]
        self.order = lax.dynamic_index_in_dim(jnp.asarray(np.array(steps, np.int32)), t, 0, False)
        self.behind = [self.order[d] for d in range(self.tp)]
        self.inverse = (pos - jnp.asarray(where)) % self.tp
        return s, t

    def shift(self, x, k):
        n = self.tp
        return lax.ppermute(x, "tp", [(self.cycle[i], self.cycle[(i + k) % n]) for i in range(n)])

    def cross(self, x, bit):
        return lax.ppermute(x, "tp", [(i, i ^ bit) for i in range(self.tp)])

    def swap(self, x, bit):
        return lax.ppermute(x, "seq", [(i, i ^ bit) for i in range(self.seq)])

    def halves(self, size):
        half = size // 2
        return half // 16 * 16 if size >= 32 else half

    def gather_first(self, x):
        out = [x] + [None] * (self.seq - 1)
        for bit in reversed(self.bits):
            out[bit] = self.swap(x, bit)
        return out

    def gather_rest(self, out, end=None):
        out = list(out)
        for j in range(end or self.seq):
            if out[j] is None:
                out[j] = self.swap(out[j & (j - 1)], j & -j)
        return out

    def gather_near(self, x):
        out = [x]
        for bit in self.bits[:-1]:
            out = out + [self.swap(y, bit) for y in out]
        return out

    def halved(self, x):
        half = x.shape[0] // 2
        return [x[:half], x[half:]]

    def quad_far_part(self, parts):
        parts = list(parts)
        for bit in self.bits[:-1]:
            for j in reversed(range(0, len(parts), 2 * bit)):
                moved = self.swap(parts[j ^ bit], bit)
                parts[j] = (parts[j].astype(F32) + moved.astype(F32)).astype(BF16)
        return parts[0]

    def quad_near(self, parts):
        half = self.seq // 2
        far = self.quad_far_part(parts[half:])
        return [self.quad_far_part(parts[:half]), far]

    def quad_far(self, near):
        return [near[0], self.swap(near[1], self.bits[-1])]

    def total_step(self, x, bit):
        moved = self.swap(x, bit)
        return x + jnp.stack([moved[j ^ bit] for j in range(self.seq)], 0)

    def total_near(self, x):
        for bit in self.bits[:-1]:
            x = self.total_step(x, bit)
        return x

    def total_far(self, x):
        return self.total_step(x, self.bits[-1])


def after(x, *others):
    return lax.optimization_barrier((x,) + others)[0]


def hold(*trees):
    return lax.optimization_barrier(trees)


class RingGather:
    def __init__(self, net, x):
        self.net, self.size = net, x.shape[0]
        n = net.tp
        self.blocks = [[(x, 0)]] + [None] * (n - 1)
        self.full = (n - 1) // 2
        self.made = 0
        self.came = (x, x)

    def done(self):
        return self.made == self.net.tp // 2

    def sends(self):
        if self.done():
            return ()
        fore, back = self.came
        if self.made < self.full:
            return fore, back
        half = self.net.halves(self.size)
        return fore[:half], back[half:]

    def launch(self, sends):
        if self.done():
            return
        net, n = self.net, self.net.tp
        self.made += 1
        d = self.made
        self.came = net.shift(sends[0], 1), net.shift(sends[1], -1)
        if d <= self.full:
            self.blocks[d], self.blocks[n - d] = [(self.came[0], 0)], [(self.came[1], 0)]
        else:
            self.blocks[d] = [(self.came[0], 0), (self.came[1], net.halves(self.size))]

    def finish(self):
        while not self.done():
            self.launch(self.sends())

    def rows(self, start, q):
        out = []
        for block in self.blocks:
            whole = jnp.concatenate([a for a, _ in block], 0) if len(block) > 1 else block[0][0]
            out.append(whole[start : start + q])
        return out


class RingScatter:
    def __init__(self, net, wholes, canonical):
        self.net, self.wholes, self.canonical = net, wholes, canonical
        self.sizes = [w.shape[0] // net.tp for w in wholes]
        self.size = sum(self.sizes)
        self.d = net.tp // 2
        self.came = ()
        self.half = net.halves(self.size) if net.tp % 2 == 0 else 0

    def done(self):
        return self.d == 0

    def make(self, outs):
        net = self.net
        made = []
        for d, low, high, adds in outs:
            rows = []
            for w, q in zip(self.wholes, self.sizes):
                at = net.behind[d] * q if self.canonical else d * q
                rows.append(lax.dynamic_slice_in_dim(w, at, q, 0))
            whole = jnp.concatenate(rows, 0)[low:high]
            for part, start in adds:
                first = start - low
                part = jnp.pad(part.astype(F32), ((first, high - low - first - part.shape[0]), (0, 0)))
                whole = whole.astype(F32) + part
            made.append(whole.astype(BF16))
        return made

    def adds(self, which):
        if not self.came:
            return []
        after_half = which == 1 and 2 * (self.d + 1) == self.net.tp
        return [(self.came[which], self.half if after_half else 0)]

    def sends(self):
        if self.done():
            return ()
        n, d = self.net.tp, self.d
        if 2 * d == n:
            return self.make([(d, 0, self.half, []), (d, self.half, self.size, [])])
        return self.make([(n - d, 0, self.size, self.adds(0)), (d, 0, self.size, self.adds(1))])

    def launch(self, sends):
        if self.done():
            return
        self.d -= 1
        self.came = self.net.shift(sends[0], 1), self.net.shift(sends[1], -1)

    def result(self):
        while not self.done():
            self.launch(self.sends())
        return self.make([(0, 0, self.size, self.adds(0) + self.adds(1))])[0]


SMEM_SPEC = pl.BlockSpec(memory_space=pltpu.SMEM)
VMEM_SPEC = pl.BlockSpec(memory_space=pltpu.VMEM)


def norm_tokens(blocks, gain, rows):
    count, _, cols = blocks.shape
    width = count * cols

    def body(gain_ref, in_ref, x_ref, n_ref):
        total = jnp.zeros((rows, 1), F32)
        for k in range(count):
            c = in_ref[k, :rows].astype(F32)
            total += jnp.sum(c * c, axis=-1, keepdims=True)
        r = lax.rsqrt(total / width + EPS)
        for k in range(count):
            c = in_ref[k, :rows]
            at = slice(k * cols, (k + 1) * cols)
            x_ref[:, at] = c
            n_ref[:, at] = (c.astype(F32) * r * gain_ref[:, at]).astype(BF16)

    return pl.pallas_call(
        body,
        out_shape=[jax.ShapeDtypeStruct((rows, width), BF16)] * 2,
        in_specs=[VMEM_SPEC] * 2,
        out_specs=[VMEM_SPEC] * 2,
        compiler_params=params(),
        cost_estimate=NO_COST,
    )(gain.reshape(1, width), blocks)


def mask_rows(blocks, live):
    count, rows, cols = blocks.shape
    width = count * cols

    def body(live_ref, in_ref, x_ref):
        for k in range(count):
            at = slice(k * cols, (k + 1) * cols)
            x_ref[:, at] = (in_ref[k].astype(F32) * live_ref[...]).astype(BF16)

    return pl.pallas_call(
        body,
        out_shape=jax.ShapeDtypeStruct((rows, width), BF16),
        in_specs=[VMEM_SPEC] * 2,
        out_specs=VMEM_SPEC,
        compiler_params=params(),
        cost_estimate=NO_COST,
    )(live, blocks)


def tile_scan(decay, drive):
    place = lax.broadcasted_iota(jnp.int32, decay.shape, 0)
    for step in (1, 2, 4):
        inside = place >= step
        before_decay = jnp.where(inside, pltpu.roll(decay, step, 0), 1.0)
        before_drive = jnp.where(inside, pltpu.roll(drive, step, 0), 0.0)
        drive = drive + decay * before_drive
        decay = decay * before_decay
    return decay, drive


def tile_scan_up(decay, drive):
    place = lax.broadcasted_iota(jnp.int32, decay.shape, 0)
    for step in (1, 2, 4):
        inside = place < 8 - step
        before_decay = jnp.where(inside, pltpu.roll(decay, 8 - step, 0), 1.0)
        before_drive = jnp.where(inside, pltpu.roll(drive, 8 - step, 0), 0.0)
        drive = drive + decay * before_drive
        decay = decay * before_decay
    return decay, drive


def gates(pre_in, pre_fg, bound):
    sig_f = fast_sigmoid(pre_fg)
    forget = bound + (1.0 - bound) * sig_f
    sig_in = fast_sigmoid(pre_in)
    act_in = pre_in * sig_in
    slope_in = sig_in * (1.0 + pre_in * (1.0 - sig_in))
    keep = (1.0 - bound) * (1.0 - sig_f)
    return sig_f, forget, act_in, slope_in, keep


class Weights:
    def __init__(self):
        self.arrays, self.takes, self.shapes = [], [], []

    def add(self, ring, parts, stride, canonical):
        held, n = len(self.shapes), ring.net.tp
        width = ring.blocks[0][0][0].shape[1]
        self.shapes.append((len(parts) * n * stride, width))
        if stride % 16:
            for start, at in parts:
                rows = ring.rows(start, stride)
                whole = jnp.stack(rows, 0)
                if canonical:
                    whole = whole[ring.net.inverse]
                self.takes.append((len(self.arrays), 0, n * stride, held, None, at))
                self.arrays.append(whole.reshape(n * stride, width))
            return
        seen = {id(a): i for i, a in enumerate(self.arrays)}
        for d, block in enumerate(ring.blocks):
            for array, first in block:
                if id(array) not in seen:
                    seen[id(array)] = len(self.arrays)
                    self.arrays.append(array)
                for start, at in parts:
                    low, high = max(start, first), min(start + stride, first + array.shape[0])
                    if low < high:
                        place = (d, stride) if canonical else None
                        row = at + (low - start) + (0 if canonical else d * stride)
                        self.takes.append((seen[id(array)], low - first, high - low, held, place, row))

    def copies(self, order_ref, refs, held, sems):
        out = []
        for k, (source, first, size, to, place, row) in enumerate(self.takes):
            if place is not None:
                row = pl.multiple_of(order_ref[place[0]] * place[1] + row, 16)
            out.append(
                pltpu.make_async_copy(refs[source].at[pl.ds(first, size)], held[to].at[pl.ds(row, size)], sems.at[k])
            )
        return out


def step_kernel(body, order, count, rows, blocks, weights, ins, outs, width, onto=(), long=True):
    any_spec = pl.BlockSpec(memory_space=pl.ANY)
    pieces = [(j, i, sum(a.shape[0] for a in block[:i]), a) for j, block in enumerate(blocks) for i, a in enumerate(block)]
    n_x, n_w, n_in, n_out = len(pieces), len(weights.arrays), len(ins), len(outs)
    n_part = count if width else 0
    n_held, n_onto = len(weights.shapes), len(onto)

    def kernel(order_ref, *refs):
        refs = list(refs)

        def take(k):
            out = refs[:k]
            del refs[:k]
            return out

        x_refs, w_refs, in_refs, _ = take(n_x), take(n_w), take(n_in), take(n_onto)
        out_refs, part_refs = take(n_out), take(n_part)
        held, w_sems = take(n_held), take(1)[0]
        xs, x_sems = take(2) if n_x else (None, None)
        kept, part_sems = take(2) if n_part else (None, None)
        j = pl.program_id(0)
        loads = weights.copies(order_ref, w_refs, held, w_sems)
        x_loads = [
            pltpu.make_async_copy(x_refs[k], xs.at[at, pl.ds(start, a.shape[0])], x_sems.at[k])
            for k, (at, _, start, a) in enumerate(pieces)
        ]

        @pl.when(j == 0)
        def _():
            first = [x for x, (at, _, _, _) in zip(x_loads, pieces) if at == 0]
            for load in first + loads + x_loads[len(first) :]:
                load.start()

        left = list(zip(weights.takes, loads))

        def ready(which):
            now = [x for x in left if x[0][3] == which]
            for x in now:
                left.remove(x)
            if now:

                @pl.when(j == 0)
                def _():
                    for _, load in now:
                        load.wait()

        for k in range(n_x):

            @pl.when(j == pieces[k][0])
            def _(k=k):
                x_loads[k].wait()

        x = xs[j] if n_x else None
        part = body(x, held, in_refs, out_refs, ready)
        for which in range(n_held):
            ready(which)
        stores = [pltpu.make_async_copy(kept.at[k % 2], part_refs[k], part_sems.at[k]) for k in range(n_part)]
        for k in range(n_part):

            @pl.when(j == k)
            def _(k=k):
                if k >= 2:
                    stores[k - 2].wait()
                kept[k % 2] = part
                stores[k].start()
                if k == n_part - 1:
                    for store in stores[max(k - 1, 0) :]:
                        store.wait()

    scratch = [pltpu.VMEM(shape, BF16) for shape in weights.shapes]
    scratch.append(pltpu.SemaphoreType.DMA((max(len(weights.takes), 1),)))
    if n_x:
        scratch += [pltpu.VMEM((len(blocks), rows, pieces[0][3].shape[1]), BF16), pltpu.SemaphoreType.DMA((n_x,))]
    if n_part:
        scratch += [pltpu.VMEM((2, rows, width), BF16), pltpu.SemaphoreType.DMA((n_part,))]
    out = pl.pallas_call(
        kernel,
        grid=(count,),
        out_shape=[shape for shape, _ in outs] + [jax.ShapeDtypeStruct((rows, width), BF16)] * n_part,
        in_specs=[SMEM_SPEC] + [any_spec] * (n_x + n_w) + [spec for _, spec in ins] + [any_spec] * n_onto,
        out_specs=[spec for _, spec in outs] + [any_spec] * n_part,
        input_output_aliases={1 + n_x + n_w + n_in + i: i for i in range(n_onto)},
        scratch_shapes=scratch,
        compiler_params=params(),
        cost_estimate=LONG if long else NO_COST,
    )(order, *[a for _, _, _, a in pieces], *weights.arrays, *[a for a, _ in ins], *onto)
    return list(out[:n_out]), list(out[n_out:])


def shape_of(*shape, dtype=F32):
    return jax.ShapeDtypeStruct(shape, dtype)


def by_block(rows, wide, first=0, column=0):
    return pl.BlockSpec((rows, wide), lambda b: (b + first, column))


def whole_row(wide):
    return pl.BlockSpec((1, wide), lambda b: (0, 0))


def by_slot(slots, wide, first=0):
    return pl.BlockSpec((1, slots, wide), lambda b: (b + first, 0, 0))


def columns(wide):
    return [slice(c, min(c + 256, wide)) for c in range(0, wide, 256)]


def mixer_in(order, blocks, weights, bound, slots, pos_n):
    count, (rows, depth), wide = len(blocks), blocks[0].shape, bound.shape[1]

    def body(x, held, ins, outs, ready):
        pre_ref, all_ref, decay_ref, end_ref = outs
        low = ins[0][...]
        all_ref[...] = x
        ready(0)
        pre_ref[...] = dot_nt(x, held[0][...])

        def one(i, carry):
            out = []
            for k in range(slots):
                at = pl.ds(pl.multiple_of(k * pos_n + i * 8, 8), 8)
                _, forget, act, _, keep = gates(pre_ref[at, :wide], pre_ref[at, wide : 2 * wide], low)
                decay, local = tile_scan(forget, act * keep)
                a, h = carry[k]
                out.append((a * decay[7:8, :], decay[7:8, :] * h + local[7:8, :]))
            return tuple(out)

        start = (jnp.ones((1, wide), F32), jnp.zeros((1, wide), F32))
        ends = lax.fori_loop(0, pos_n // 8, one, (start,) * slots)
        for k in range(slots):
            decay_ref[0, k : k + 1] = ends[k][0]
            end_ref[0, k : k + 1] = ends[k][1]

    outs = [
        (shape_of(count * rows, 3 * wide), by_block(rows, 3 * wide)),
        (shape_of(count * rows, depth, dtype=BF16), by_block(rows, depth)),
        (shape_of(count, slots, wide), by_slot(slots, wide)),
        (shape_of(count, slots, wide), by_slot(slots, wide)),
    ]
    return step_kernel(
        body, order, count, rows, [[x] for x in blocks], weights, [(bound, whole_row(wide))], outs, 0
    )[0]


def scan_heads(place, before, whole, reverse):
    count, slots, wide = whole[0].shape

    def body(place_ref, pa_ref, pb_ref, wa_ref, wb_ref, head_ref):
        state = jnp.zeros((slots, wide), F32)
        for i in range(count):
            j = lax.bitwise_xor(place_ref[0], count - 1 - i if reverse else i)
            head_ref[j] = pa_ref[j] * state + pb_ref[j]
            state = wa_ref[j] * state + wb_ref[j]

    return pl.pallas_call(
        body,
        out_shape=shape_of(count, slots, wide),
        in_specs=[SMEM_SPEC] + [VMEM_SPEC] * 4,
        out_specs=VMEM_SPEC,
        compiler_params=params(),
        cost_estimate=NO_COST,
    )(place, *before, *whole)


def mixer_out(order, pre, bound, gain, head, weights, pos_n, first, steps, onto=(), long=True):
    wide = bound.shape[1]
    count, slots, _ = head.shape
    rows = slots * pos_n
    depth = weights.shapes[0][1]

    def body(x, held, ins, outs, ready):
        pre_ref, bound_ref, gain_ref, head_ref = ins
        state_ref, mix_ref, sum_ref = outs
        low = bound_ref[...]

        def one(i, carry):
            out = []
            for k in range(slots):
                at = pl.ds(pl.multiple_of(k * pos_n + i * 8, 8), 8)
                _, forget, act, _, keep = gates(pre_ref[at, :wide], pre_ref[at, wide : 2 * wide], low)
                decay, local = tile_scan(forget, act * keep)
                state = local + decay * carry[k]
                state_ref[at, :] = state
                square = state * state
                sum_ref[at, :] = sum(square[:, c : c + 128] for c in range(0, wide, 128))
                out.append(state[7:8, :])
            return tuple(out)

        lax.fori_loop(0, pos_n // 8, one, tuple(head_ref[0, k : k + 1] for k in range(slots)))
        og = pre_ref[:, 2 * wide :]
        mix = (state_ref[...] * gain_ref[...] * (og * fast_sigmoid(og))).astype(BF16)
        mix_ref[...] = mix
        ready(0)
        return dot_nn(mix, held[0][...]).astype(BF16)

    ins = [
        (pre, by_block(rows, 3 * wide, first)),
        (bound, whole_row(wide)),
        (gain, whole_row(wide)),
        (head, by_slot(slots, wide, first)),
    ]
    outs = [
        (shape_of(count * rows, wide), by_block(rows, wide, first)),
        (shape_of(count * rows, wide, dtype=BF16), by_block(rows, wide, first)),
        (shape_of(count * rows, 128), by_block(rows, 128, first)),
    ]
    return step_kernel(body, order, steps, rows, [], weights, ins, outs, depth, onto, long)


def feed_forward(order, blocks, weights, first, count, onto=(), long=True):
    (rows, depth), wide = blocks[0].shape, weights.shapes[0][0]

    def body(x, held, ins, outs, ready):
        hid_ref, slope_ref, act_ref, all_ref = outs
        all_ref[...] = x
        ready(0)
        ready(1)
        for at in columns(wide):
            gate = dot_nt(x, held[0][at, :])
            up = dot_nt(x, held[1][at, :])
            sig = fast_sigmoid(gate)
            act = gate * sig
            hid_ref[:, at] = (act * up).astype(BF16)
            slope_ref[:, at] = (up * (sig * (1.0 + gate * (1.0 - sig)))).astype(BF16)
            act_ref[:, at] = act.astype(BF16)

    outs = [(shape_of(count * rows, wide, dtype=BF16), by_block(rows, wide, first))] * 3
    outs = outs + [(shape_of(count * rows, depth, dtype=BF16), by_block(rows, depth, first))]
    return step_kernel(body, order, len(blocks), rows, [[x] for x in blocks], weights, [], outs, 0, onto, long)[0]


def down_parts(order, hidden, weights, rows):
    wide, depth = weights.shapes[0]
    count = hidden.shape[0] // rows

    def body(x, held, ins, outs, ready):
        ready(0)
        return dot_nn(ins[0][...], held[0][...]).astype(BF16)

    return step_kernel(
        body, order, count, rows, [], weights, [(hidden, by_block(rows, wide))], [], depth
    )[1]


def back_hidden(order, g, weights, slope, act, rows):
    wide, depth = weights.shapes[0]
    count = g.shape[0] // rows

    def body(x, held, ins, outs, ready):
        g_ref, slope_ref, act_ref = ins
        ready(0)
        for at in columns(wide):
            hid = dot_nt(g_ref[...], held[0][at, :])
            outs[0][:, at] = (hid * slope_ref[:, at].astype(F32)).astype(BF16)
            outs[1][:, at] = (hid * act_ref[:, at].astype(F32)).astype(BF16)

    block = by_block(rows, wide)
    ins = [(g, by_block(rows, depth)), (slope, block), (act, block)]
    outs = [(shape_of(count * rows, wide, dtype=BF16), block)] * 2
    return step_kernel(body, order, count, rows, [], weights, ins, outs, 0)[0]


def back_pair(order, a, b, weights, rows, first, count):
    wide, depth = weights.shapes[0]

    def body(x, held, ins, outs, ready):
        ready(0)
        ready(1)
        return (dot_nn(ins[0][...], held[0][...]) + dot_nn(ins[1][...], held[1][...])).astype(BF16)

    block = by_block(rows, wide, first)
    return step_kernel(
        body, order, count, rows, [], weights, [(a, block), (b, block)], [], depth
    )[1]


def back_mixer(order, blocks, rows, weights, pre, state, mix, r_mix, gain):
    count, depth, wide = len(blocks), blocks[0][0].shape[1], gain.shape[1]

    def body(x, held, ins, outs, ready):
        og_ref, state_ref, mix_ref, r_ref, gain_ref = ins
        norm_ref, og_out, mix_out, all_ref, inner_ref, sum_ref = outs
        all_ref[...] = x
        ready(0)
        mix_out[...] = (mix_ref[...].astype(F32) * r_ref[...]).astype(BF16)
        g = dot_nt(x, held[0][...])
        og, state = og_ref[...], state_ref[...]
        sig = fast_sigmoid(og)
        act = og * sig
        g_state = g * (state * r_ref[...])
        sum_ref[0] = jnp.sum((g_state * act).reshape(rows // 8, 8, wide), 0)
        og_out[...] = (g_state * gain_ref[...] * (sig * (1.0 + og * (1.0 - sig)))).astype(BF16)
        norm = g * gain_ref[...] * act
        norm_ref[...] = norm
        inner = state * norm
        inner_ref[...] = sum(inner[:, c : c + 128] for c in range(0, wide, 128))

    ins = [
        (pre, pl.BlockSpec((rows, wide), lambda b: (b, 2))),
        (state, by_block(rows, wide)),
        (mix, by_block(rows, wide)),
        (r_mix, by_block(rows, 1)),
        (gain, whole_row(wide)),
    ]
    outs = [
        (shape_of(count * rows, wide), by_block(rows, wide)),
        (shape_of(count * rows, wide, dtype=BF16), by_block(rows, wide)),
        (shape_of(count * rows, wide, dtype=BF16), by_block(rows, wide)),
        (shape_of(count * rows, depth, dtype=BF16), by_block(rows, depth)),
        (shape_of(count * rows, 128), by_block(rows, 128)),
        (shape_of(count, 8, wide), by_slot(8, wide)),
    ]
    return step_kernel(body, order, count, rows, blocks, weights, ins, outs, 0)[0]


def back_ends(pre, bound, norm, state, r_mix, coef, slots, pos_n):
    wide = norm.shape[1]
    rows = slots * pos_n
    count = norm.shape[0] // rows
    tiles = pos_n // 8

    def body(fg_ref, norm_ref, state_ref, r_ref, coef_ref, bound_ref, end_ref):
        low = bound_ref[...]

        def one(i, carry):
            out = []
            for k in range(slots):
                at = pl.ds(pl.multiple_of(k * pos_n + (tiles - 1 - i) * 8, 8), 8)
                local = r_ref[at, :] * norm_ref[at, :] - coef_ref[at, :] * state_ref[at, :]
                forget = low + (1.0 - low) * fast_sigmoid(fg_ref[at, :])
                decay, part = tile_scan_up(forget, forget * local)
                out.append(decay[0:1, :] * carry[k] + part[0:1, :])
            return tuple(out)

        ends = lax.fori_loop(0, tiles, one, (jnp.zeros((1, wide), F32),) * slots)
        for k in range(slots):
            end_ref[0, k : k + 1] = ends[k]

    block = by_block(rows, wide)
    return pl.pallas_call(
        body,
        grid=(count,),
        out_shape=shape_of(count, slots, wide),
        in_specs=[
            pl.BlockSpec((rows, wide), lambda b: (b, 1)),
            block,
            block,
            by_block(rows, 1),
            by_block(rows, 1),
            whole_row(wide),
        ],
        out_specs=by_slot(slots, wide),
        compiler_params=params(),
        cost_estimate=NO_COST,
    )(pre, norm, state, r_mix, coef, bound)


def back_states(order, pre, bound, norm, state, g_og, r_mix, coef, head, tail, weights, pos_n, first, count, long=True):
    wide = norm.shape[1]
    slots = head.shape[1]
    rows = slots * pos_n
    pairs = pos_n // 16
    depth = weights.shapes[0][1]

    def body(x, held, ins, outs, ready):
        in_ref, fg_ref, bound_ref, norm_ref, state_ref, og_ref, r_ref, coef_ref, head_ref, tail_ref = ins
        gin_ref, gfg_ref, low_ref = outs
        low = bound_ref[...]
        place = lax.broadcasted_iota(jnp.int32, (8, wide), 0)
        low_ref[0] = jnp.zeros((8, wide), F32)

        def half(k, tile, g):
            at = pl.ds(pl.multiple_of(k * pos_n + tile * 8, 8), 8)
            sig_f, forget, act, slope, keep = gates(in_ref[at, :], fg_ref[at, :], low)
            now = state_ref[at, :]
            local = r_ref[at, :] * norm_ref[at, :] - coef_ref[at, :] * now
            decay, part = tile_scan_up(forget, forget * local)
            whole = part + decay * g
            g_state = local + jnp.where(place == 7, g, pltpu.roll(whole, 7, 0))
            last = jnp.maximum(k * pos_n + tile * 8 - 1, 0)
            entry = jnp.where(tile == 0, head_ref[0, k : k + 1], state_ref[pl.ds(last, 1), :])
            before = jnp.where(place == 0, entry, pltpu.roll(now, 1, 0))
            g_forget = g_state * (before - act)
            return g_state * keep * slope, g_forget * keep * sig_f, whole[0:1, :], g_forget * (1.0 - sig_f)

        def one(i, carry):
            pair = pairs - 1 - i
            out, total = [], low_ref[0]
            for k in range(slots):
                in_2, fg_2, g, low_2 = half(k, 2 * pair + 1, carry[k])
                in_1, fg_1, g, low_1 = half(k, 2 * pair, g)
                at = pl.ds(pl.multiple_of(k * pos_n + pair * 16, 16), 16)
                gin_ref[at, :] = jnp.concatenate([in_1, in_2], 0).astype(BF16)
                gfg_ref[at, :] = jnp.concatenate([fg_1, fg_2], 0).astype(BF16)
                total = total + low_1 + low_2
                out.append(g)
            low_ref[0] = total
            return tuple(out)

        lax.fori_loop(0, pairs, one, tuple(tail_ref[0, k : k + 1] for k in range(slots)))
        ready(0)
        part = dot_nn(gin_ref[...], held[0][:wide]) + dot_nn(gfg_ref[...], held[0][wide : 2 * wide])
        return (part + dot_nn(og_ref[...], held[0][2 * wide :])).astype(BF16)

    block, edge, one_lane = by_block(rows, wide, first), by_slot(slots, wide, first), by_block(rows, 1, first)
    ins = [
        (pre, block),
        (pre, by_block(rows, wide, first, 1)),
        (bound, whole_row(wide)),
        (norm, block),
        (state, block),
        (g_og, block),
        (r_mix, one_lane),
        (coef, one_lane),
        (head, edge),
        (tail, edge),
    ]
    outs = [(shape_of(count * rows, wide, dtype=BF16), by_block(rows, wide))] * 2
    outs = outs + [(shape_of(count, 8, wide), by_slot(8, wide))]
    return step_kernel(body, order, count, rows, [], weights, ins, outs, depth, (), long)


STEPS = 4


def row_kernel(body, outs, ins, scratch=()):
    def spec(a, kind):
        if kind == "whole":
            return pl.BlockSpec(a.shape, lambda i: (0,) * len(a.shape))
        if kind == "rows":
            return pl.BlockSpec((a.shape[0] // STEPS,) + a.shape[1:], lambda i: (i, 0))
        size = a.shape[0] // (STEPS // 2)
        if kind == "first":
            return pl.BlockSpec((size,) + a.shape[1:], lambda i: (jnp.minimum(i, STEPS // 2 - 1), 0))
        return pl.BlockSpec((size,) + a.shape[1:], lambda i: (jnp.maximum(i - STEPS // 2, 0), 0))

    return pl.pallas_call(
        body,
        grid=(STEPS,),
        out_shape=[a for a, _ in outs],
        in_specs=[spec(*x) for x in ins],
        out_specs=[spec(*x) for x in outs],
        scratch_shapes=scratch,
        compiler_params=params(),
        cost_estimate=NO_COST,
    )(*[a for a, _ in ins])


def half_rows(first_ref, second_ref):
    early = pl.program_id(0) < STEPS // 2
    return jnp.where(early, first_ref[...].astype(F32), second_ref[...].astype(F32))


def add_to(ref, value):
    @pl.when(pl.program_id(0) == 0)
    def _():
        ref[...] = jnp.zeros_like(ref)

    ref[...] += value


def residual(near, moved, tok, r_mix, gain):
    rows, width = tok.shape

    def body(near_ref, moved_ref, tok_ref, r_ref, gain_ref, resid_ref, out_ref):
        branch = near_ref[...].astype(F32) + moved_ref[...].astype(F32)
        resid = tok_ref[...].astype(F32) + r_ref[...] * branch
        resid_ref[...] = resid
        r = lax.rsqrt(jnp.sum(resid * resid, axis=-1, keepdims=True) / width + EPS)
        out_ref[...] = (resid * r * gain_ref[...]).astype(BF16)

    outs = [(shape_of(rows, width), "rows"), (shape_of(rows, width, dtype=BF16), "rows")]
    ins = [(near, "rows"), (moved, "rows"), (tok, "rows"), (r_mix, "rows"), (gain, "whole")]
    return row_kernel(body, outs, ins)


def back_residual(near, moved, resid, cot, gain):
    rows, width = resid.shape

    def body(near_ref, first_ref, second_ref, resid_ref, cot_ref, gain_ref, grad_ref, out_ref, sum_ref):
        g = near_ref[...].astype(F32) + half_rows(first_ref, second_ref)
        resid = resid_ref[...]
        r = lax.rsqrt(jnp.sum(resid * resid, axis=-1, keepdims=True) / width + EPS)
        scaled = resid * r
        add_to(sum_ref, jnp.sum(g * scaled, axis=0, keepdims=True))
        g = g * gain_ref[...]
        inner = jnp.sum(resid * g, axis=-1, keepdims=True)
        grad = cot_ref[...].astype(F32) + r * g - resid * (r * r * r * inner / width)
        grad_ref[...] = grad
        out_ref[...] = grad.astype(BF16)

    outs = [
        (shape_of(rows, width), "rows"),
        (shape_of(rows, width, dtype=BF16), "rows"),
        (shape_of(1, width), "whole"),
    ]
    ins = [(near, "rows"), (moved[0], "first"), (moved[1], "second"), (resid, "rows"), (cot, "rows"), (gain, "whole")]
    return row_kernel(body, outs, ins)


def block_output(near, moved, resid, live, count):
    rows, width = resid.shape
    cols, size = width // count, rows // STEPS

    def body(near_ref, moved_ref, resid_ref, live_ref, out_ref):
        at_rows = pl.ds(pl.multiple_of(pl.program_id(0) * size, size), size)
        for k in range(count):
            at = slice(k * cols, (k + 1) * cols)
            ffn = near_ref[:, at].astype(F32) + moved_ref[:, at].astype(F32)
            out_ref[k, at_rows, :] = (live_ref[...] * (resid_ref[:, at] + ffn)).astype(BF16)

    outs = [(shape_of(count, rows, cols, dtype=BF16), "whole")]
    ins = [(near, "rows"), (moved, "rows"), (resid, "rows"), (live, "rows")]
    return row_kernel(body, outs, ins)[0]


def back_tokens(near, moved, tok, grad_resid, in_gain, mlp_sum, chan_rows):
    rows, width = tok.shape
    count, _, cols = chan_rows.shape
    size = rows // STEPS

    def body(near_ref, first_ref, second_ref, tok_ref, grad_ref, gain_ref, mlp_ref, chan_ref, out_ref, sum_ref):
        g = near_ref[...].astype(F32) + half_rows(first_ref, second_ref)
        x = tok_ref[...].astype(F32)
        r = lax.rsqrt(jnp.sum(x * x, axis=-1, keepdims=True) / width + EPS)
        add_to(sum_ref, jnp.sum(g * x * r, axis=0, keepdims=True))
        g = g * gain_ref[...]
        inner = jnp.sum(x * g, axis=-1, keepdims=True)
        grad = (grad_ref[...] + r * g - x * (r * r * r * inner / width)).astype(BF16)
        at_rows = pl.ds(pl.multiple_of(pl.program_id(0) * size, size), size)
        for k in range(count):
            out_ref[k, at_rows, :] = grad[:, k * cols : (k + 1) * cols]

        @pl.when(pl.program_id(0) == STEPS - 1)
        def _():
            place = lax.broadcasted_iota(jnp.int32, (16, cols), 0)
            for k in range(count):
                at = slice(k * cols, (k + 1) * cols)
                extra = jnp.zeros((16, cols), F32)
                for i, total in enumerate((sum_ref[:, at], mlp_ref[:, at])):
                    high = total.astype(BF16).astype(F32)
                    extra = jnp.where(place == i, high, jnp.where(place == 2 + i, total - high, extra))
                extra = jnp.where(place == 4, chan_ref[k], extra)
                out_ref[k, rows:, :] = extra.astype(BF16)

    outs = [(shape_of(count, rows + 16, cols, dtype=BF16), "whole")]
    ins = [(near, "rows"), (moved[0], "first"), (moved[1], "second"), (tok, "rows"), (grad_resid, "rows")]
    ins += [(in_gain, "whole"), (mlp_sum, "whole"), (chan_rows, "whole")]
    return row_kernel(body, outs, ins, [pltpu.VMEM((1, width), F32)])[0]


def order_rows(blocks, place):
    count = len(blocks)
    q, width = blocks[0].shape
    tile = 512

    def body(place_ref, *refs):
        out_ref = refs[count]
        for j in range(count):
            at = pl.multiple_of(lax.bitwise_xor(place_ref[0], j) * q, 16)
            out_ref[pl.ds(at, q), :] = refs[j][...].astype(F32)

    return pl.pallas_call(
        body,
        grid=(width // tile,),
        out_shape=shape_of(count * q, width),
        in_specs=[SMEM_SPEC] + [pl.BlockSpec((q, tile), lambda i: (0, i))] * count,
        out_specs=pl.BlockSpec((count * q, tile), lambda i: (0, i)),
        compiler_params=params(),
        cost_estimate=NO_COST,
    )(place, *blocks)


def turn_rows(blocks, place):
    count = len(blocks)
    q, width = blocks[0].shape
    tile = 512

    def body(place_ref, *refs):
        out_ref, held = refs[count], refs[count + 1]
        for j in range(count):
            held[lax.bitwise_xor(place_ref[0], j)] = refs[j][...].astype(F32)
        out_ref[...] = held[...].reshape(count * q, tile).T

    return pl.pallas_call(
        body,
        grid=(width // tile,),
        out_shape=shape_of(width, count * q),
        in_specs=[SMEM_SPEC] + [pl.BlockSpec((q, tile), lambda i: (0, i))] * count,
        out_specs=pl.BlockSpec((tile, count * q), lambda i: (i, 0)),
        scratch_shapes=[pltpu.VMEM((count, q, tile), F32)],
        compiler_params=params(),
        cost_estimate=NO_COST,
    )(place, *blocks)


def dot_nt(a, b):
    return lax.dot_general(a, b, (((1,), (1,)), ((), ())), preferred_element_type=F32)


def dot_nn(a, b):
    return lax.dot_general(a, b, (((1,), (0,)), ((), ())), preferred_element_type=F32)


def dot_tn(a, b):
    return lax.dot_general(a, b, (((0,), (0,)), ((), ())), preferred_element_type=F32)


def on_device(
    net,
    tokens,
    cotangent,
    lengths,
    in_gain,
    w_input,
    w_forget,
    w_output_gate,
    lower_bound,
    mix_gain,
    w_out,
    mlp_gain,
    w_gate,
    w_up,
    w_down,
):
    s, t = net.places()
    n_seq, n_tp = net.seq, net.tp
    slots, group, cols = tokens.shape
    width = cols * n_tp
    pos_n = group // n_tp
    rows = slots * pos_n
    dq = cols // n_seq
    fq = w_down.shape[0] // n_seq
    chan, hid = dq * n_tp, fq * n_tp
    place = s.reshape(1)
    order = net.order

    def quarter_t(w, q):
        return lax.dynamic_slice_in_dim(w, s * q, q, 1).T

    def by_owner(x):
        return x.reshape(slots, n_tp, pos_n, cols).transpose(1, 0, 2, 3).reshape(n_tp, rows, cols)

    def to_owner(x):
        return lax.all_to_all(x, "tp", 0, 0, tiled=True)

    def in_place(x):
        return x.reshape(n_tp, slots, pos_n, cols).transpose(1, 0, 2, 3).reshape(tokens.shape)

    where = s * group + t * pos_n + jnp.arange(pos_n, dtype=jnp.int32)
    live = (where[None, :] < lengths[:, None]).astype(F32).reshape(rows, 1)

    small = jnp.concatenate(
        [lax.dynamic_slice_in_dim(v, s * dq, dq) for v in (lower_bound, mix_gain)] + [mlp_gain], 0
    )
    terms, rest = [], small
    for _ in range(3):
        terms.append(hold(rest.astype(BF16))[0])
        rest = rest - terms[-1].astype(F32)
    terms = jnp.pad(jnp.concatenate(terms, 0), (0, 16 * cols - 3 * small.shape[0])).reshape(1, 16, cols)
    token_blocks = to_owner(jnp.concatenate([by_owner(tokens), jnp.broadcast_to(terms, (n_tp, 16, cols))], 1))
    small = token_blocks[:, rows:].reshape(n_tp, 16 * cols)[:, : 3 * small.shape[0]].astype(F32).reshape(n_tp, 3, -1)
    small = small[:, 0] + small[:, 1] + small[:, 2]
    bound = small[:, :dq].reshape(1, chan)
    gain = small[:, dq : 2 * dq].reshape(1, chan)
    mlp_full = small[:, 2 * dq :].reshape(1, width)
    mix_w = jnp.concatenate(
        [quarter_t(w, dq) for w in (w_input, w_forget, w_output_gate)]
        + [lax.dynamic_slice_in_dim(w_out, s * dq, dq, 0)],
        0,
    )
    tok, normed_own = norm_tokens(token_blocks, in_gain, rows)
    mix_ring = RingGather(net, after(mix_w, normed_own))
    mix_ring.launch(mix_ring.sends())
    normed = net.gather_rest(net.gather_first(normed_own))
    mix_ring.finish()
    w3, wo = Weights(), Weights()
    w3.add(mix_ring, [(i * dq, i * chan) for i in range(3)], dq, True)
    wo.add(mix_ring, [(3 * dq, 0)], dq, True)
    gate_ring = RingGather(net, after(quarter_t(w_gate, fq), *mix_ring.came))
    up_ring = RingGather(net, after(quarter_t(w_up, fq), *mix_ring.came))
    gate_ring.launch(gate_ring.sends())
    up_ring.launch(up_ring.sends())
    half = n_seq // 2

    pre, normed_all, decay, end = mixer_in(order, normed, w3, bound, slots, pos_n)

    def spread(pair, reverse):
        def joined(earlier, later):
            return earlier[0] * later[0], later[0] * earlier[1] + later[1]

        whole = pair
        before = (jnp.ones_like(pair[0]), jnp.zeros_like(pair[1]))
        for bit in net.tp_bits:
            moved = net.cross(jnp.stack(whole, 0), bit)
            moved = (moved[0], moved[1])
            upper = (jnp.bitwise_and(t, bit) != 0) != reverse
            ahead, behind = joined(moved, whole), joined(whole, moved)
            longer = joined(moved, before)
            before = tuple(jnp.where(upper, a, b) for a, b in zip(longer, before))
            whole = tuple(jnp.where(upper, a, b) for a, b in zip(ahead, behind))
        return before, whole

    (decay, end), gate_ring.came, up_ring.came = hold((decay, end), gate_ring.came, up_ring.came)
    head = scan_heads(place, *spread((decay, end), False), False)
    head, sends, up_sends = hold(head, gate_ring.sends(), up_ring.sends())
    gate_ring.launch(sends)
    some, far = mixer_out(order, pre, bound, gain, head, wo, pos_n, half, half)
    head_near, some = hold(head, some)
    (state, mix, squares), parts = mixer_out(order, pre, bound, gain, head_near, wo, pos_n, 0, half, some, False)
    near_far = net.quad_far_part(far)
    near_far, parts, squares, gate_ring.came = hold(near_far, parts, squares, gate_ring.came)
    moved_far = net.swap(near_far, net.bits[-1])
    up_ring.launch(up_sends)
    sum_all = net.total_far(net.total_near(jnp.sum(squares, -1).reshape(n_seq, rows)))
    near_own = net.quad_far_part(parts)
    near_own, up_ring.came, sends = hold(near_own, up_ring.came, gate_ring.sends())
    gate_ring.launch(sends)
    near_own, moved_far, sum_all, gate_ring.came, sends = hold(
        near_own, moved_far, sum_all, gate_ring.came, up_ring.sends()
    )
    up_ring.launch(sends)
    r_mix = lax.rsqrt(sum_all / width + EPS).reshape(n_seq * rows, 1)
    resid, mlp_own = residual(near_own, moved_far, tok, r_mix[:rows], mlp_full)
    mlp_in = net.gather_first(mlp_own)
    up_ring.came, mlp_own, sends = hold(up_ring.came, mlp_own, gate_ring.sends())
    gate_ring.launch(sends)
    up_ring.launch(up_ring.sends())
    gate_ring.finish()
    up_ring.finish()
    mlp_in = net.gather_rest(mlp_in, half)
    wgu = Weights()
    wgu.add(gate_ring, [(0, 0)], fq, False)
    wgu.add(up_ring, [(0, 0)], fq, False)
    down_w = lax.dynamic_slice_in_dim(w_down, s * fq, fq, 0)
    near_in, down_w, cot_sent, _ = hold(mlp_in[:half], down_w, by_owner(cotangent), (gate_ring.came, up_ring.came))

    down_ring = RingGather(net, down_w)
    down_ring.launch(down_ring.sends())
    cot_blocks = to_owner(cot_sent)
    some = feed_forward(order, near_in, wgu, 0, n_seq)
    some, far_first, down_ring.came = hold(some, mlp_in[half], down_ring.came)
    down_ring.launch(down_ring.sends())
    mlp_in = net.gather_rest(mlp_in[:half] + [far_first] + mlp_in[half + 1 :])
    hidden, slope_up, act, mlp_all = feed_forward(order, mlp_in[half:], wgu, half, n_seq, some, False)
    hidden, cot_blocks = hold(hidden, cot_blocks)
    cot = mask_rows(cot_blocks, live)
    grad_out = net.gather_first(cot)
    cot, down_ring.came = hold(cot, down_ring.came)
    down_ring.launch(down_ring.sends())
    grad_out, down_ring.came = hold(grad_out, down_ring.came)
    down_ring.launch(down_ring.sends())
    down_ring.finish()
    grad_all = jnp.concatenate(net.gather_rest(grad_out), 0)

    def to_output(blocks, turned):
        q = blocks[0].shape[0]
        if q % 16 == 0:
            return turn_rows(blocks, place) if turned else order_rows(blocks, place)
        out = jnp.zeros((n_seq, q, width), F32)
        for j in range(n_seq):
            out = lax.dynamic_update_index_in_dim(out, blocks[j].astype(F32), lax.bitwise_xor(s, j), 0)
        out = out.reshape(n_seq * q, width)
        return out.T if turned else out

    dw_down = dot_tn(hidden, grad_all).astype(BF16)
    down_sum = RingScatter(net, [dw_down], False)
    wd = Weights()
    wd.add(down_ring, [(0, 0)], fq, False)
    sends, grad_all, _ = hold(down_sum.sends(), grad_all, down_ring.came)
    down_sum.launch(sends)
    grad_gate, grad_up = back_hidden(order, grad_all, wd, slope_up, act, rows)
    grad_gate, down_sum.came = hold(grad_gate, down_sum.came)
    sends, grad_gate = hold(down_sum.sends(), grad_gate)
    down_sum.launch(sends)
    far = back_pair(order, grad_gate, grad_up, wgu, rows, half, half)
    far, down_sum.came = hold(far, down_sum.came)
    sent, sends, grad_gate = hold(net.halved(net.quad_far_part(far)), down_sum.sends(), grad_gate)
    moved = [net.swap(x, net.bits[-1]) for x in sent]
    down_sum.launch(sends)
    parts = back_pair(order, grad_gate, grad_up, wgu, rows, 0, half)
    parts, moved[0], down_sum.came = hold(parts, moved[0], down_sum.came)
    sends, grad_gate = hold(down_sum.sends(), grad_gate)
    down_sum.launch(sends)
    near_own = net.quad_far_part(parts)
    dw_gate = dot_tn(grad_gate, mlp_all).astype(BF16)
    dw_gate, moved[1], near_own, down_sum.came = hold(dw_gate, moved[1], near_own, down_sum.came)
    grad_resid, branch_own, mlp_sum = back_residual(near_own, moved, resid, cot, mlp_full)
    gate_sum = RingScatter(net, [dw_gate], False)
    branch_own, sends, sent, hidden = hold(branch_own, gate_sum.sends(), net.halved(branch_own), hidden)
    grad_branch = [[x] for x in net.gather_near(branch_own)]
    moved = [net.swap(x, net.bits[-1]) for x in sent]
    gate_sum.launch(sends)
    ffn_parts = down_parts(order, hidden, wd, rows)
    ffn_parts, moved[0], grad_branch, gate_sum.came = hold(ffn_parts, moved[0], grad_branch, gate_sum.came)
    grad_branch_a = net.gather_near(moved[0])
    down_own = down_sum.result()
    sends, grad_up = hold(gate_sum.sends(), grad_up)
    gate_sum.launch(sends)
    ffn_near = net.quad_near(ffn_parts)
    dw_up = dot_tn(grad_up, mlp_all).astype(BF16)
    dw_up, moved[1], gate_sum.came, ffn_near = hold(dw_up, moved[1], gate_sum.came, ffn_near)
    grad_branch = grad_branch + [list(x) for x in zip(grad_branch_a, net.gather_near(moved[1]))]
    up_sum = RingScatter(net, [dw_up], False)

    sends, up_sends, grad_branch, down_own = hold(gate_sum.sends(), up_sum.sends(), grad_branch, down_own)
    gate_sum.launch(sends)
    up_sum.launch(up_sends)
    down_blocks = net.gather_first(down_own)
    g_norm, grad_og, mixed_out, branch_all, inner_lanes, gain_sums = back_mixer(
        order, grad_branch, rows, wo, pre, state, mix, r_mix, gain
    )
    inner_lanes, gate_sum.came, up_sum.came, down_blocks = hold(
        inner_lanes, gate_sum.came, up_sum.came, down_blocks
    )
    sends, up_sends, inner_lanes = hold(gate_sum.sends(), up_sum.sends(), inner_lanes)
    gate_sum.launch(sends)
    up_sum.launch(up_sends)
    inner = net.total_far(net.total_near(jnp.sum(inner_lanes, -1).reshape(n_seq, rows))).reshape(-1, 1)
    ffn = net.quad_far([after(p, inner) for p in ffn_near])
    coef = r_mix**3 * inner / width
    back_end = back_ends(pre, bound, g_norm, state, r_mix, coef, slots, pos_n)
    dw_out = dot_tn(after(mixed_out, back_end), branch_all).astype(BF16)
    dw_og = dot_tn(after(grad_og, dw_out), normed_all).astype(BF16)
    back_end, gate_sum.came, up_sum.came, dw_og = hold(back_end, gate_sum.came, up_sum.came, dw_og)
    tail = scan_heads(place, *spread((decay, back_end), True), True)
    gate_own = gate_sum.result()
    first_sum = RingScatter(net, [dw_out, dw_og], True)
    tail, up_sends, sends, gate_own = hold(tail, up_sum.sends(), first_sum.sends(), gate_own)
    up_sum.launch(up_sends)
    first_sum.launch(sends)

    def back(start, tail, long):
        return back_states(
            order, pre, bound, g_norm, state, grad_og, r_mix, coef, head, tail, w3, pos_n, start, half, long
        )

    (far_in, far_fg, far_low), far = back(half, tail, True)
    far, far_in, up_sum.came, first_sum.came, ffn = hold(far, far_in, up_sum.came, first_sum.came, ffn)
    mixed_sent = block_output(*ffn, resid, live, n_tp)
    sent, tail, up_sends, sends, mixed_sent = hold(
        net.halved(net.quad_far_part(far)), tail, up_sum.sends(), first_sum.sends(), mixed_sent
    )
    moved = [net.swap(x, net.bits[-1]) for x in sent]
    up_sum.launch(up_sends)
    first_sum.launch(sends)
    mixed_got = to_owner(mixed_sent)
    (grad_in, grad_fg, low_sums), parts = back(0, tail, True)
    parts, moved[0], first_sum.came, up_sum.came = hold(parts, moved[0], first_sum.came, up_sum.came)
    up_own = up_sum.result()
    low_sums = low_sums + far_low
    grad_in, grad_fg = (jnp.concatenate([a, b], 0) for a, b in ((grad_in, far_in), (grad_fg, far_fg)))
    sends, up_own, grad_in = hold(first_sum.sends(), up_own, grad_in)
    first_sum.launch(sends)
    near_own = net.quad_far_part(parts)
    dw_in = dot_tn(grad_in, normed_all).astype(BF16)
    dw_fg = dot_tn(after(grad_fg, dw_in), normed_all).astype(BF16)
    last_sum = RingScatter(net, [dw_in, dw_fg], True)
    last_sends, near_own, first_sum.came = hold(last_sum.sends(), near_own, first_sum.came)
    last_sum.launch(last_sends)
    first_sum.launch(first_sum.sends())
    near_own, moved = hold(near_own, moved)
    sums = jnp.stack([jnp.sum(low_sums, axis=(0, 1)), jnp.sum(gain_sums, axis=(0, 1))], 0).reshape(2, n_tp, dq)
    high = hold(sums.astype(BF16))[0].astype(F32)
    chan_rows = jnp.concatenate([high, sums - high], 0).transpose(1, 0, 2).reshape(n_tp, 1, 4 * dq)
    chan_rows = jnp.pad(chan_rows, ((0, 0), (0, 0), (0, cols - 4 * dq)))
    sent = back_tokens(near_own, moved, tok, grad_resid, in_gain.reshape(1, width), mlp_sum, chan_rows)

    sent, up_own, last_sum.came, first_sum.came = hold(sent, up_own, last_sum.came, first_sum.came)
    got = to_owner(sent)
    up_blocks, gate_blocks = net.gather_first(up_own), net.gather_first(after(gate_own, up_own))
    down_blocks = net.gather_rest([after(down_blocks[0], up_own)] + down_blocks[1:])
    grad_w_down = to_output(down_blocks, False)
    sends, last_sends = hold(first_sum.sends(), last_sum.sends())
    last_sum.launch(last_sends)
    first_sum.launch(sends)
    last_sum.came, first_sum.came, grad_w_down = hold(last_sum.came, first_sum.came, grad_w_down)
    last_sum.launch(hold(last_sum.sends())[0])
    first_own = first_sum.result()
    first_blocks = net.gather_first(first_own)
    grad_w_up = to_output(net.gather_rest(up_blocks), False)
    grad_w_gate = to_output(net.gather_rest(gate_blocks), False)
    last_sum.came, grad_w_up, grad_w_gate, got, mixed_got = hold(
        last_sum.came, grad_w_up, grad_w_gate, got, mixed_got
    )
    last_sum.launch(hold(last_sum.sends())[0])
    grad_w_gate, grad_w_up = grad_w_gate.T, grad_w_up.T
    first_blocks = net.gather_rest(first_blocks)
    grad_w_out = to_output([b[:dq] for b in first_blocks], False)
    grad_w_og = to_output([b[dq:] for b in first_blocks], True)
    last_sum.came, grad_w_out, grad_w_og = hold(last_sum.came, grad_w_out, grad_w_og)
    last_own = last_sum.result()
    last_blocks = net.gather_rest(net.gather_first(last_own))
    grad_w_in = to_output([b[:dq] for b in last_blocks], True)
    grad_w_fg = to_output([b[dq:] for b in last_blocks], True)
    mixed = in_place(mixed_got)
    sums = jnp.sum(got[:, rows : rows + 5].astype(F32), 0)
    ends = jnp.concatenate([sums[:2] + sums[2:4], sums[4:5]], 0).reshape(1, 3, cols)
    for bit in net.bits:
        ends = jnp.concatenate([ends, net.swap(ends, bit)], 0)
    mine = jnp.sum(ends[:, :2], 0)
    chans = ends[lax.bitwise_xor(s, jnp.arange(n_seq, dtype=jnp.int32)), 2, : 4 * dq].reshape(n_seq, 2, 2, dq)
    chans = chans[:, 0] + chans[:, 1]
    return (
        mixed,
        in_place(got[:, :rows]).astype(F32),
        mine[0],
        grad_w_in,
        grad_w_fg,
        grad_w_og,
        chans[:, 0].reshape(-1),
        chans[:, 1].reshape(-1),
        grad_w_out,
        mine[1],
        grad_w_gate,
        grad_w_up,
        grad_w_down,
    )


def solution(mesh):
    return jax.shard_map(
        functools.partial(on_device, Net(mesh)),
        mesh=mesh,
        in_specs=(
            P(None, "seq", "tp"),
            P(None, "seq", "tp"),
            P(),
            P(),
            P(None, "tp"),
            P(None, "tp"),
            P(None, "tp"),
            P("tp"),
            P("tp"),
            P("tp", None),
            P("tp"),
            P(None, "tp"),
            P(None, "tp"),
            P("tp", None),
        ),
        out_specs=(
            P(None, "seq", "tp"),
            P(None, "seq", "tp"),
            P("tp"),
            P(None, "tp"),
            P(None, "tp"),
            P(None, "tp"),
            P("tp"),
            P("tp"),
            P("tp", None),
            P("tp"),
            P(None, "tp"),
            P(None, "tp"),
            P("tp", None),
        ),
        check_vma=False,
    )
```
